128 devices in a mesh: wide: 64 (over y_hi, z, x, core), narrow: 2 (over y_lo).
Axes of the slice: x: 4, y: 4 (y_hi: 2, y_lo: 2; y = y_hi * 2 + y_lo), z: 4, core: 2. Of those that a mesh axis runs over, the one named last changes fastest.
Arguments:
- x_first: bfloat16 [8192, 1024], P('wide', 'narrow'), may hold values from -6 to 6
- x_second: bfloat16 [8192, 1024], P('wide', 'narrow'), may hold values from -6 to 6
- grad_first: bfloat16 [8192, 1024], P('wide', 'narrow'), may hold values from -6 to 6
- grad_second: bfloat16 [8192, 1024], P('wide', 'narrow'), may hold values from -6 to 6
- sort_target: int32 [2, 2, 8192], replicated, may hold values from 0 to 8191, as said below
- owner: int32 [176], replicated, may hold values from 0 to 319, as said below
- master: float32 [320, 128, 1024], P('wide', None, 'narrow')
- moment_first: float32 [320, 128, 1024], P('wide', None, 'narrow')
- moment_second: float32 [320, 128, 1024], P('wide', None, 'narrow')
- gains: float32 [2, 2, 1024], P(None, None, 'narrow'), may hold values from 0.5 to 1.5
- gain_first: float32 [2, 2, 1024], P(None, None, 'narrow')
- gain_second: float32 [2, 2, 1024], P(None, None, 'narrow')
Outputs:
- y_first: float32 [8192, 1024], P('wide', 'narrow')
- y_second: float32 [8192, 1024], P('wide', 'narrow')
- dx_first: float32 [8192, 1024], P('wide', 'narrow')
- dx_second: float32 [8192, 1024], P('wide', 'narrow')
- slot_grad: float32 [320, 128, 1024], P('wide', None, 'narrow')
- slot_first: float32 [320, 128, 1024], P('wide', None, 'narrow')
- slot_second: float32 [320, 128, 1024], P('wide', None, 'narrow')
- slot_new: float32 [320, 128, 1024], P('wide', None, 'narrow')
- gain_grad: float32 [2, 2, 1024], P(None, None, 'narrow')
- gain_first_new: float32 [2, 2, 1024], P(None, None, 'narrow')
- gain_second_new: float32 [2, 2, 1024], P(None, None, 'narrow')
- gain_new: float32 [2, 2, 1024], P(None, None, 'narrow')
The draws below stay inside these ranges and needn't reach their ends.
Inputs may be any that keep to these rules, and one draw needn't show every extreme that they name: For each layer and round, sort_target is a permutation of the 8192 positions in which the 128 positions of every aligned block of 128 go to exactly 128 // 64 places in every aligned block of 128 places. owner holds 176 different slots; slots k * 5 to k * 5 + 4 belong to index k of wide; the slots of some index are all used; in each aligned group of 3 tile numbers at most 1 tiles belong to one index of wide.
All inputs are finite; a program needn't handle non-finite values.
Results may differ from the reference program's by a relative error of at most 0.024.
Values may be sent and summed in bfloat16 or wider, within the bound.
No kernel may reach another device: no remote copies, remote signals or barrier semaphores. Data moves between devices by JAX's collectives and lax.ppermute only.
A program may use at most 320 MiB of HBM per device.

```python
import math
import jax
import jax.numpy as jnp
from jax import lax

D = 1024
HEADS = 8
DH = 128
FF = 4096
SPAN = 64
ROUNDS = 2
LAYERS = 2
STEP = 5
TR = 128
TOK_DEV = 128
SEQ = 8192
TILES = 176
CAP = 5
SLOTS = 320
PER = 3
N_WIDE = 64
N_NARROW = 2


def seat_order(seat_key):
    return jax.random.permutation(seat_key, CAP).astype(jnp.int32)


def make_owner(key):
    key = jax.random.fold_in(key, 101)
    pick_key, group_key, base_key, spread_key, slot_key = jax.random.split(key, 5)
    fullest = jax.random.randint(pick_key, (), 0, N_WIDE).astype(jnp.int32)
    groups = TILES // PER
    order = jax.random.permutation(group_key, groups).astype(jnp.int32)
    serial = jnp.arange(CAP, dtype=jnp.int32)
    chosen_group = order[serial % groups]
    offsets = jax.random.randint(base_key, (groups,), 0, PER).astype(jnp.int32)
    spots = chosen_group * PER + (offsets[chosen_group] + serial // groups) % PER
    crowded = jnp.zeros((TILES,), jnp.int32).at[spots].set(1)
    other_rank = jnp.cumsum(1 - crowded).astype(jnp.int32) - 1
    spread = jax.random.permutation(spread_key, N_WIDE - 1).astype(jnp.int32)
    other_dev = spread[jnp.maximum(other_rank, 0) % (N_WIDE - 1)]
    other_dev = other_dev + (other_dev >= fullest).astype(jnp.int32)
    device = jnp.where(crowded > 0, fullest, other_dev).astype(jnp.int32)
    hits = (device[:, None] == jnp.arange(N_WIDE, dtype=jnp.int32)[None, :]).astype(jnp.int32)
    arrival = jnp.sum((jnp.cumsum(hits, axis=0) - hits) * hits, axis=1).astype(jnp.int32)
    seats = jax.vmap(seat_order)(jax.random.split(slot_key, N_WIDE))
    return (device * CAP + seats[device, arrival]).astype(jnp.int32)


def slot_scales(owner, table):
    tile_ids = jnp.full((SLOTS,), -1, jnp.int32).at[owner].set(jnp.arange(TILES, dtype=jnp.int32))
    local = jnp.maximum(tile_ids, 0) % (TILES // LAYERS) * TR
    kind = (local >= D).astype(jnp.int32) + (local >= 2 * D).astype(jnp.int32) + (local >= 3 * D).astype(jnp.int32) + (local >= 3 * D + FF).astype(jnp.int32)
    values = jnp.asarray(table, jnp.float32)[kind]
    return jnp.where(tile_ids >= 0, values, table[0])


def grad_table():
    root = math.sqrt(SEQ)
    return [1.5 * root, 2.0 * root, 0.15 * root, 0.3 * root, 0.65 * root]


def draw_owner(key, part):
    return make_owner(key)


def draw_sort_target(key, part):
    key = jax.random.fold_in(key, 7)
    share = TOK_DEV // N_WIDE

    def shuffle(one_key):
        return jax.random.permutation(one_key, TOK_DEV).astype(jnp.int32)

    def one_round(round_key):
        rank_key, seat_key = jax.random.split(round_key)
        ranks = jax.vmap(shuffle)(jax.random.split(rank_key, N_WIDE))
        seats = jax.vmap(shuffle)(jax.random.split(seat_key, N_WIDE))
        target_dev = ranks // share
        arrival = jnp.arange(N_WIDE, dtype=jnp.int32)[:, None] * share + ranks % share
        place = seats[target_dev, arrival]
        return (target_dev * TOK_DEV + place).reshape(SEQ)
    keys = jax.random.split(key, LAYERS * ROUNDS)
    return jax.vmap(one_round)(keys).reshape(LAYERS, ROUNDS, SEQ).astype(jnp.int32)


def draw_master(key, part):
    owner = make_owner(key)
    key = jax.random.fold_in(key, 3)
    table = [D ** (-0.5), D ** (-0.5), (2.0 * SPAN / D) ** 0.5, D ** (-0.5), FF ** (-0.5)]
    scale = slot_scales(owner, table)
    return jax.random.normal(key, (SLOTS, TR, D), jnp.float32) * scale[:, None, None]


def draw_moment_first(key, part):
    owner = make_owner(key)
    key = jax.random.fold_in(key, 5)
    scale = slot_scales(owner, grad_table())
    return jax.random.normal(key, (SLOTS, TR, D), jnp.float32) * scale[:, None, None]


def draw_moment_second(key, part):
    owner = make_owner(key)
    key = jax.random.fold_in(key, 9)
    scale = slot_scales(owner, grad_table())
    factor = jnp.exp(jax.random.uniform(key, (SLOTS, TR, D), jnp.float32, 0.0, math.log(4.0)))
    return factor * (scale * scale)[:, None, None]


def draw_gain_first(key, part):
    key = jax.random.fold_in(key, 13)
    root = math.sqrt(SEQ)
    scale = jnp.asarray([2.5 * root, 0.3 * root], jnp.float32)
    return jax.random.normal(key, (LAYERS, 2, D), jnp.float32) * scale[None, :, None]


def draw_gain_second(key, part):
    key = jax.random.fold_in(key, 17)
    root = math.sqrt(SEQ)
    scale = jnp.asarray([2.5 * root, 0.3 * root], jnp.float32)
    factor = jnp.exp(jax.random.uniform(key, (LAYERS, 2, D), jnp.float32, 0.0, math.log(4.0)))
    return factor * (scale * scale)[None, :, None]


def block_levels(key, extent, pieces, low, high):
    def one(dim, blocks):
        steps = jax.random.uniform(jax.random.fold_in(jax.random.fold_in(key, 6), dim), (blocks,), jnp.float32, low / len(pieces), high / len(pieces))
        return jnp.repeat(jnp.exp(steps), extent[dim] // blocks).reshape((-1,) + (1,) * (len(extent) - dim - 1))

    loudness = one(*pieces[0])
    for cut in pieces[1:]:
        loudness = loudness * one(*cut)
    return loudness


def scatter_about(key, extent, scale, most, shards=(), held_as=jnp.bfloat16):
    values = jax.random.normal(key, extent, jnp.float32) * scale
    if len(shards) > 0:
        values = block_levels(key, extent, shards, -0.22, 0.18) * values
    return jnp.clip(values, min=-most, max=most).astype(held_as)


def setup_inputs(seed: int = 0) -> dict:
    splits = jax.random.split(jax.random.key(seed), 13)
    return {
        "x_first": scatter_about(splits[0], (SEQ, D), 1.0, 6.0, ((0, 64), (1, 2))),
        "x_second": scatter_about(splits[1], (SEQ, D), 1.0, 6.0, ((0, 64), (1, 2))),
        "grad_first": scatter_about(splits[2], (SEQ, D), 1.0, 6.0, ((0, 64), (1, 2))),
        "grad_second": scatter_about(splits[3], (SEQ, D), 1.0, 6.0, ((0, 64), (1, 2))),
        "sort_target": draw_sort_target(jax.random.fold_in(splits[12], 71), 0),
        "owner": draw_owner(jax.random.fold_in(splits[12], 71), 0),
        "master": draw_master(jax.random.fold_in(splits[12], 71), 0),
        "moment_first": draw_moment_first(jax.random.fold_in(splits[12], 71), 0),
        "moment_second": draw_moment_second(jax.random.fold_in(splits[12], 71), 0),
        "gains": jnp.clip(1.0 + 0.1 * jax.random.normal(splits[9], (LAYERS, 2, D), jnp.float32), 0.5, 1.5),
        "gain_first": draw_gain_first(jax.random.fold_in(splits[12], 71), 0),
        "gain_second": draw_gain_second(jax.random.fold_in(splits[12], 71), 0),
    }


HIGH = lax.Precision.HIGHEST
MASK_FILL = -1000000000.0
NORM_EPS = 1e-05
BETA_ONE = 0.5
BETA_TWO = 0.5
RATE_WEIGHT = 0.05
RATE_GAIN = 0.2
DECAY = 0.01
EPSILON = 1e-08

@jax.custom_vjp
def low(v):
    return lax.optimization_barrier(v.astype(jnp.bfloat16)).astype(jnp.float32)

@jax.custom_vjp
def low_back(v):
    return v

def low_keep(v):
    return (low(v), None)

def low_pass(kept, grad):
    return (grad,)

def back_keep(v):
    return (v, None)

def back_low(kept, grad):
    return (low(grad),)
low.defvjp(low_keep, low_pass)
low_back.defvjp(back_keep, back_low)

def layer_norm(values, gain):
    mean = lax.optimization_barrier(jnp.mean(values, axis=-1, keepdims=True))
    var = lax.optimization_barrier(jnp.mean(values * values, axis=-1, keepdims=True)) - mean * mean
    return (values - mean) * lax.rsqrt(var + NORM_EPS) * gain

def unpack(tiles):
    rows = tiles.reshape(LAYERS, -1, D)
    quad = FF // D
    layers = []
    for layer in range(LAYERS):
        block = rows[layer]
        up_rows = block[3 * D:3 * D + FF].reshape(D, quad, N_NARROW, D // N_NARROW)
        down_rows = block[3 * D + FF:].reshape(D, quad, N_NARROW, D // N_NARROW)
        layers.append({'qk': block[:D], 'value': block[D:2 * D], 'out': jnp.transpose(block[2 * D:3 * D]), 'up': jnp.transpose(up_rows, (0, 2, 1, 3)).reshape(D, FF), 'down': jnp.transpose(jnp.transpose(down_rows, (0, 2, 1, 3)).reshape(D, FF))})
    return layers

def attend(queries, values, prev_queries, prev_values):
    count = queries.shape[0] // SPAN
    heads = queries.shape[1]
    cur_q = queries.reshape(count, SPAN, heads, DH)
    cur_v = values.reshape(count, SPAN, heads, DH)
    keys = jnp.concatenate([jnp.concatenate([prev_queries[None], cur_q[:-1]], 0), cur_q], 1)
    vals = jnp.concatenate([jnp.concatenate([prev_values[None], cur_v[:-1]], 0), cur_v], 1)
    unit = low(keys * lax.rsqrt(lax.optimization_barrier(jnp.sum(keys * keys, axis=-1, keepdims=True)) + 1e-06))
    scores = low_back(jnp.einsum('cqhd,ckhd->chqk', cur_q, unit, precision=HIGH))
    own = jnp.arange(2 * SPAN)[None, :] == jnp.arange(SPAN)[:, None] + SPAN
    scores = jnp.where(own, MASK_FILL, scores)
    peak = lax.optimization_barrier(jnp.max(scores, axis=-1, keepdims=True))
    total = peak + jnp.log(lax.optimization_barrier(jnp.sum(jnp.exp(scores - peak), axis=-1, keepdims=True)))
    probs = low(jnp.exp(scores - total))
    out = low_back(jnp.einsum('chqk,ckhd->cqhd', probs, vals, precision=HIGH))
    lse = jnp.transpose(total[..., 0], (0, 2, 1)).reshape(count * SPAN, heads)
    return (out.reshape(count * SPAN, heads, DH), lse)

def combine(outs, totals):
    stacked = jnp.stack(outs)
    logits = jnp.stack(totals)
    top = lax.optimization_barrier(jnp.max(logits, axis=0, keepdims=True))
    expo = jnp.exp(logits - top)
    share = expo / lax.optimization_barrier(jnp.sum(expo, axis=0, keepdims=True))
    return lax.optimization_barrier(jnp.sum(share[..., None] * stacked, axis=0))

def adam(grad, first, second, weight, rate):
    first_new = BETA_ONE * first + (1.0 - BETA_ONE) * grad
    second_new = BETA_TWO * second + (1.0 - BETA_TWO) * grad * grad
    step = first_new / (1.0 - BETA_ONE ** STEP) / (jnp.sqrt(second_new / (1.0 - BETA_TWO ** STEP)) + EPSILON)
    return (first_new, second_new, weight - rate * (step + DECAY * weight))

def reference(x_first, x_second, grad_first, grad_second, sort_target, owner, master, moment_first, moment_second, gains, gain_first, gain_second):
    tiles = master[owner]

    def forward(x_one, x_two, tile_values, gain_values):
        layers = unpack(low(tile_values))
        for layer in range(LAYERS):
            weights = layers[layer]
            normed = low(layer_norm(x_two, gain_values[layer, 0]))
            mixed = low_back(low(jnp.dot(normed, weights['qk'], precision=HIGH))).reshape(SEQ, HEADS, DH)
            values = low_back(low(jnp.dot(normed, weights['value'], precision=HIGH))).reshape(SEQ, HEADS, DH)
            outs = []
            totals = []
            for rnd in range(ROUNDS):
                target = sort_target[layer, rnd]
                inverse = jnp.argsort(target, stable=True).astype(jnp.int32)
                sorted_q = mixed[inverse]
                sorted_v = values[inverse]
                attended, total = attend(sorted_q, sorted_v, sorted_q[-SPAN:], sorted_v[-SPAN:])
                outs.append(attended[target])
                totals.append(total[target])
            merged = low(combine(tuple(outs), tuple(totals)).reshape(SEQ, D))
            x_one = x_one + low_back(jnp.dot(merged, weights['out'], precision=HIGH))
            hidden = low(layer_norm(x_one, gain_values[layer, 1]))
            pre = low_back(jnp.dot(hidden, weights['up'], precision=HIGH))
            act = low(jax.nn.gelu(pre, approximate=False))
            x_two = x_two + low_back(jnp.dot(act, weights['down'], precision=HIGH))
        return (x_one, x_two)
    outputs, pull = jax.vjp(forward, x_first.astype(jnp.float32), x_second.astype(jnp.float32), tiles, gains)
    d_one, d_two, d_tiles, d_gains = pull((grad_first.astype(jnp.float32), grad_second.astype(jnp.float32)))
    slot_grad = jnp.zeros_like(master).at[owner].set(d_tiles)
    slot_first, slot_second, slot_new = adam(slot_grad, moment_first, moment_second, master, RATE_WEIGHT)
    gain_first_new, gain_second_new, gain_new = adam(d_gains, gain_first, gain_second, gains, RATE_GAIN)
    return (outputs[0], outputs[1], d_one, d_two, slot_grad, slot_first, slot_second, slot_new, d_gains, gain_first_new, gain_second_new, gain_new)
```

```python
import functools

import jax
import jax.numpy as jnp
import numpy as np
from jax import lax
from jax.experimental import pallas as pl
from jax.experimental.pallas import tpu as pltpu
from jax.sharding import PartitionSpec as P

D = 1024
PART = 512
DH = 128
HN = 4
SPAN = 64
TR = 128
CAP = 5
TOK = 128
NW = 64
LAYERS = 2
ROUNDS = 2
STEP = 5
GROUPS = 8
SEND_ROWS = 18
QV_LANES = SEND_ROWS * 2 * DH
O_LANES = 17 * DH
QUAD = 4
UP, DOWN = 0, 1
OUT, QK, VALUE = 8, 9, 10
LAYER_ROWS = 176
REST_ROWS = 144

MASK_FILL = -1000000000.0
NORM_EPS = 1e-05
BETA_ONE = 0.5
BETA_TWO = 0.5
RATE_WEIGHT = 0.05
RATE_GAIN = 0.2
DECAY = 0.01
EPSILON = 1e-08

F32 = jnp.float32
BF16 = jnp.bfloat16
I32 = jnp.int32
VMEM_BYTES = 56 * 1024 * 1024


def feature_of(p):
    c0 = p >> 9
    j3 = (p >> 6) & 7
    tau = (p >> 4) & 3
    t = (p >> 1) & 7
    e = p & 1
    return t * 128 + tau * 32 + c0 * 16 + j3 * 2 + e


def tile_rows():
    tiles, parity = [], []
    for base in (24, 56):
        for tau in range(4):
            for t in range(8):
                for e in range(2):
                    tiles.append(base + t * 4 + tau)
                    parity.append(e)
    for base in (16, 0, 8):
        for t in range(8):
            for e in range(2):
                tiles.append(base + t)
                parity.append(e)
    return np.array(tiles, np.int32), np.array(parity, np.int32)


def iota(shape, dim):
    return lax.broadcasted_iota(I32, shape, dim)


def hot(mask):
    return jnp.where(mask, 1.0, 0.0).astype(BF16)


def dot(a, b, ca, cb):
    return lax.dot_general(a, b, (((ca,), (cb,)), ((), ())), preferred_element_type=F32)


def call(kernel, args, outs, grid=(1,), specs=None, out_specs=None, scratch=(), prefetch=0, name=None):
    specs = specs or {}
    out_specs = out_specs or {}
    def whole(shape):
        zeros = (0,) * len(shape)
        return pl.BlockSpec(shape, lambda *_: zeros)
    in_list = [specs.get(i, whole(a.shape)) for i, a in enumerate(args[prefetch:])]
    out_list = [out_specs.get(i, whole(o.shape)) for i, o in enumerate(outs)]
    return pl.pallas_call(
        kernel,
        out_shape=outs,
        grid_spec=pltpu.PrefetchScalarGridSpec(
            num_scalar_prefetch=prefetch,
            grid=grid,
            in_specs=in_list,
            out_specs=out_list,
            scratch_shapes=list(scratch),
        ),
        compiler_params=pltpu.CompilerParams(vmem_limit_bytes=VMEM_BYTES),
        name=name,
    )(*args)


def sds(shape, dtype):
    return jax.ShapeDtypeStruct(shape, dtype)


def norm_parts(values):
    mean = jnp.mean(values, axis=-1, keepdims=True)
    var = jnp.mean(values * values, axis=-1, keepdims=True) - mean * mean
    rstd = lax.rsqrt(var + NORM_EPS)
    return (values - mean) * rstd, rstd


def norm_back(upstream, gain, xhat, rstd):
    gh = upstream * gain
    m1 = jnp.mean(gh, axis=-1, keepdims=True)
    m2 = jnp.mean(gh * xhat, axis=-1, keepdims=True)
    return rstd * (gh - m1 - xhat * m2), jnp.sum(upstream * xhat, axis=0, keepdims=True)


def weight(ref):
    return jnp.concatenate([ref[:, 0].reshape(PART, PART), ref[:, 1].reshape(PART, PART)], 0)


def send_select(rank_row, rows):
    r = iota((rows, 1), 0)
    i = r >> 3
    g = r & 7
    want = jnp.where(i < 16, 16 * g + i, (16 * g - 18 + i) & 127)
    return hot(want == rank_row)


def place_select(place_ref, b):
    col = jnp.concatenate([place_ref[:, 2 * b : 2 * b + 1], place_ref[:, 2 * b + 1 : 2 * b + 2]], 0)
    return hot(col == iota((TOK, TOK), 1))


def pieces(col):
    hi = col.astype(BF16).astype(F32)
    rest = col - hi
    mid = rest.astype(BF16).astype(F32)
    return hi, mid, rest - mid


def spread(col, lanes):
    hi, mid, lo = pieces(col)
    k = lanes & 7
    return jnp.where(k == 0, hi, jnp.where(k == 1, mid, jnp.where(k == 2, lo, 0.0)))


def slot_rows(kind):
    r = iota((TR, 1), 0)
    e = r >> 6
    j = r & 63
    c0 = j & 1
    tau = (j >> 1) & 3
    j3 = j >> 3
    low = c0 * 16 + j3 * 2 + e
    row = jnp.where(kind == 1, low * 4 + tau, tau * 32 + low)
    return hot(row == iota((TR, TR), 1))


def route_out_kernel(kind_ref, master_ref, out_ref):
    picked = slot_rows(kind_ref[pl.program_id(0)])
    rows = dot(picked, master_ref[0].astype(BF16), 1, 0).astype(BF16)
    out_ref[:, :PART] = rows[:NW]
    out_ref[:, PART:] = rows[NW:]


def route_out(kind, master):
    return call(
        route_out_kernel,
        (kind, master),
        [sds((NW, CAP * 2 * PART), BF16)],
        grid=(CAP,),
        specs={0: pl.BlockSpec((1, TR, PART), lambda s, k: (s, 0, 0))},
        out_specs={0: pl.BlockSpec((NW, 2 * PART), lambda s, k: (0, s))},
        prefetch=1,
        name="route_out",
    )[0]


def slot_code(rows, dim):
    shape = (rows, 1) if dim == 0 else (1, rows)
    m = iota(shape, dim)
    k = m & 63
    e = (m >> 6) & 1
    s = m >> 7
    return (k * CAP + s) * 2 + e


def pick_kernel(code_ref, moved_ref, first_ref, rest_ref, last_ref):
    all_rows = jnp.concatenate([moved_ref[:, m * PART : (m + 1) * PART] for m in range(2 * CAP)], 0)
    picked = hot(code_ref[...] == slot_code(2 * CAP * NW, 1))
    rows = dot(picked, all_rows, 1, 0).astype(BF16)
    rest_ref[...] = rows[:REST_ROWS]
    first_ref[...] = rows[REST_ROWS:LAYER_ROWS]
    last_ref[...] = rows[LAYER_ROWS:]


def pick(code_col, moved):
    return call(
        pick_kernel,
        (code_col, moved),
        [sds((32, PART), BF16), sds((REST_ROWS, PART), BF16), sds((LAYER_ROWS, PART), BF16)],
        name="pick",
    )


def route_back_kernel(code_ref, rows_ref, out_ref):
    placed = hot(slot_code(2 * CAP * NW, 0) == code_ref[...])
    rows = dot(placed, rows_ref[...].astype(BF16), 1, 0).astype(BF16)
    for m in range(2 * CAP):
        out_ref[:, m * PART : (m + 1) * PART] = rows[m * NW : (m + 1) * NW]


def route_back(code_row, rows):
    return call(
        route_back_kernel, (code_row, rows), [sds((NW, CAP * 2 * PART), BF16)], name="route_back"
    )[0]


def adam(grad, first, second, weights, rate):
    first_new = BETA_ONE * first + (1.0 - BETA_ONE) * grad
    second_new = BETA_TWO * second + (1.0 - BETA_TWO) * grad * grad
    step = (
        first_new
        / (1.0 - BETA_ONE**STEP)
        / (jnp.sqrt(second_new / (1.0 - BETA_TWO**STEP)) + EPSILON)
    )
    return first_new, second_new, weights - rate * (step + DECAY * weights)


def slots_kernel(kind_ref, moved_ref, m_ref, a_ref, b_ref, grad_ref, first_ref, second_ref, new_ref):
    placed = slot_rows(kind_ref[pl.program_id(0)])
    rows = jnp.concatenate([moved_ref[:, :PART], moved_ref[:, PART:]], 0)
    grad = dot(placed, rows, 0, 0)
    grad_ref[0] = grad
    first_ref[0], second_ref[0], new_ref[0] = adam(grad, a_ref[0], b_ref[0], m_ref[0], RATE_WEIGHT)


def slots_update(kind, moved, master, first, second):
    tile = pl.BlockSpec((1, TR, PART), lambda s, k: (s, 0, 0))
    return call(
        slots_kernel,
        (kind, moved, master, first, second),
        [sds((CAP, TR, PART), F32)] * 4,
        grid=(CAP,),
        specs={0: pl.BlockSpec((NW, 2 * PART), lambda s, k: (0, s)), 1: tile, 2: tile, 3: tile},
        out_specs={i: tile for i in range(4)},
        prefetch=1,
        name="slots_update",
    )


def inner_kernel(half_ref, *refs):
    count = len(refs) // 3
    n = half_ref[0]
    feature = feature_of(iota((1, D), 1))
    mine = hot(feature == iota((PART, 1), 0) + n * PART)
    theirs = hot(feature == iota((PART, 1), 0) + (1 - n) * PART)
    for i in range(count):
        own, other, out = refs[2 * i], refs[2 * i + 1], refs[2 * count + i]
        if own.dtype == BF16:
            out[...] = dot(own[...], mine, 1, 0) + dot(other[...], theirs, 1, 0)
        else:
            total = jnp.zeros(out.shape, F32)
            for a, b in zip(pieces(own[...]), pieces(other[...])):
                total = total + (dot(a.astype(BF16), mine, 1, 0) + dot(b.astype(BF16), theirs, 1, 0))
            out[...] = total


def inner(half, pairs, name):
    flat = [a for pair in pairs for a in pair]
    outs = [sds((own.shape[0], D), F32) for own, _ in pairs]
    return call(inner_kernel, (half, *flat), outs, prefetch=1, name=name)


def outer_kernel(count, half_ref, *refs):
    n = half_ref[0]
    feature = feature_of(iota((1, D), 1))
    back = hot(feature == iota((PART, 1), 0) + n * PART)
    for i in range(count):
        total = jnp.zeros(refs[count + i].shape, F32)
        for part in pieces(refs[i][...]):
            total = total + dot(part.astype(BF16), back, 1, 1)
        refs[count + i][...] = total


def outer(half, arrays, name):
    outs = [sds((a.shape[0], PART), F32) for a in arrays]
    return call(
        functools.partial(outer_kernel, len(arrays)), (half, *arrays), outs, prefetch=1, name=name
    )


def attn_spec(index):
    return pl.BlockSpec((32, 2, 16, PART), lambda *_: (0, 0, index, 0))


def project_kernel(pending, *refs):
    if pending:
        x_ref, own_ref, other_ref, gain_ref, wq_ref, wv_ref, rank_ref, x_out, hn_out, send_out = refs
        x = x_ref[...] + (own_ref[...] + other_ref[...].astype(F32))
    else:
        x_ref, gain_ref, wq_ref, wv_ref, rank_ref, x_out, hn_out, send_out = refs
        x = x_ref[...]
    x_out[...] = x
    xhat, _ = norm_parts(x)
    hn = (xhat * gain_ref[...]).astype(BF16)
    hn_out[0] = hn[:, :PART]
    hn_out[1] = hn[:, PART:]
    q = dot(hn, weight(wq_ref), 1, 0).astype(BF16)
    v = dot(hn, weight(wv_ref), 1, 0).astype(BF16)
    qv = jnp.concatenate(
        [m[:, h * DH : (h + 1) * DH] for h in range(HN) for m in (q, v)], 1
    )
    rows = []
    for r in range(ROUNDS):
        moved = dot(send_select(rank_ref[r : r + 1, :], SEND_ROWS * GROUPS), qv, 1, 0)
        for h in range(HN):
            cols = slice(h * 2 * DH, (h + 1) * 2 * DH)
            rows.append(
                jnp.concatenate([moved[i * 8 : i * 8 + 8, cols] for i in range(SEND_ROWS)], 1)
            )
    send_out[...] = jnp.concatenate(rows, 0).astype(BF16)


def project(x, pending, gain, wq, wv, rank_row):
    args = [x, *(pending or ()), gain, wq[0], wv[0], rank_row]
    at = len(args) - 3
    return call(
        functools.partial(project_kernel, pending is not None),
        args,
        [sds((TOK, D), F32), sds((2, TOK, PART), BF16), sds((NW, QV_LANES), BF16)],
        specs={at: attn_spec(wq[1]), at + 1: attn_spec(wv[1])},
        name="project",
    )


def sorted_rows(moved, place_ref, width):
    blocks = []
    for b in range(9):
        pair = jnp.concatenate(
            [
                moved[:, (2 * b) * width : (2 * b + 1) * width],
                moved[:, (2 * b + 1) * width : (2 * b + 2) * width],
            ],
            0,
        )
        blocks.append(dot(place_select(place_ref, b), pair, 0, 0).astype(BF16))
    return blocks


def scores_of(rows):
    keys = rows[:, :DH].astype(F32)
    inv = lax.rsqrt(jnp.sum(keys * keys, axis=-1, keepdims=True) + 1e-06)
    unit = (keys * inv).astype(BF16)
    scores = jnp.concatenate(
        [
            dot(
                rows[(c + 1) * SPAN : (c + 2) * SPAN, :DH],
                unit[c * SPAN : (c + 2) * SPAN],
                1,
                1,
            )
            for c in range(16)
        ],
        0,
    )
    own = iota((1024, TOK), 1) == (iota((1024, TOK), 0) & (SPAN - 1)) + SPAN
    scores = jnp.where(own, MASK_FILL, scores)
    peak = jnp.max(scores, axis=-1, keepdims=True)
    total = peak + jnp.log(jnp.sum(jnp.exp(scores - peak), axis=-1, keepdims=True))
    exact = jnp.exp(scores - total)
    return keys, inv, unit, own, total, exact


def attend_kernel(moved_ref, place_ref, sorted_out, send_out):
    blocks = sorted_rows(moved_ref[...], place_ref, 2 * DH)
    rows = jnp.concatenate([blocks[8][SPAN:]] + blocks[:8], 0)
    sorted_out[...] = rows
    _, _, _, _, total, exact = scores_of(rows)
    probs = exact.astype(BF16)
    lanes = iota((NW, TOK), 1)
    extra = jnp.zeros((NW, TOK), F32)
    for b in range(8):
        outs = jnp.concatenate(
            [
                dot(
                    probs[c * SPAN : (c + 1) * SPAN],
                    rows[c * SPAN : (c + 2) * SPAN, DH:],
                    1,
                    0,
                )
                for c in (2 * b, 2 * b + 1)
            ],
            0,
        )
        aux = spread(total[b * TOK : (b + 1) * TOK], iota((TOK, TOK), 1))
        back = dot(
            place_select(place_ref, b), jnp.concatenate([outs, aux], 1).astype(BF16), 1, 0
        )
        for j in range(2):
            i = 2 * b + j
            part = back[j * NW : (j + 1) * NW]
            send_out[:, i * DH : (i + 1) * DH] = part[:, :DH].astype(BF16)
            extra = extra + jnp.where(lanes >> 3 == i, part[:, DH:], 0.0)
    send_out[:, 16 * DH :] = extra.astype(BF16)


def attend(moved, place):
    return call(
        attend_kernel,
        (moved, place),
        [sds((1088, 2 * DH), BF16), sds((NW, O_LANES), BF16)],
        name="attend",
    )


def merge_kernel(moved_ref, rank_row_ref, rank_col_ref, wo_ref, part_out, send_out, o_out, share_out, merged_out):
    moved = moved_ref[...]
    wide = moved.astype(F32)
    lanes = iota((TOK, TOK), 1)
    outs, logs = [], []
    for r in range(ROUNDS):
        rows = jnp.concatenate(
            [
                jnp.concatenate(
                    [
                        wide[r * 32 + h * 8 : r * 32 + h * 8 + 8, i * DH : (i + 1) * DH]
                        for h in range(HN)
                    ],
                    1,
                )
                for i in range(16)
            ],
            0,
        ).astype(BF16)
        back = dot(send_select(rank_row_ref[r : r + 1, :], TOK), rows, 0, 0)
        o_out[r] = back.astype(BF16)
        outs.append(back)
        rank = rank_col_ref[:, r : r + 1]
        logs_r = []
        for h in range(HN):
            at = hot(iota((TOK, NW), 1) == r * 32 + h * 8 + (rank >> 4))
            aux = dot(at, moved[:, 16 * DH :], 1, 0)
            logs_r.append(
                jnp.sum(jnp.where(lanes >> 3 == (rank & 15), aux, 0.0), axis=-1, keepdims=True)
            )
        logs.append(logs_r)
    merged = []
    share_all = jnp.zeros((TOK, TOK), F32)
    for h in range(HN):
        top = jnp.maximum(logs[0][h], logs[1][h])
        e0 = jnp.exp(logs[0][h] - top)
        e1 = jnp.exp(logs[1][h] - top)
        total = e0 + e1
        cols = slice(h * DH, (h + 1) * DH)
        s0, s1 = e0 / total, e1 / total
        merged.append(s0 * outs[0][:, cols] + s1 * outs[1][:, cols])
        share_all = jnp.where(lanes == h, s0, jnp.where(lanes == HN + h, s1, share_all))
    share_out[...] = share_all
    merged = jnp.concatenate(merged, 1).astype(BF16)
    merged_out[...] = merged
    partial = dot(merged, weight(wo_ref), 1, 1)
    part_out[...] = partial
    send_out[...] = partial.astype(BF16)


def merge(moved, rank_row, rank_col, wo):
    return call(
        merge_kernel,
        (moved, rank_row, rank_col, wo[0]),
        [
            sds((TOK, D), F32),
            sds((TOK, D), BF16),
            sds((ROUNDS, TOK, PART), BF16),
            sds((TOK, TOK), F32),
            sds((TOK, PART), BF16),
        ],
        specs={3: attn_spec(wo[1])},
        name="merge",
    )


def ffn_specs(rows):
    def block(index):
        return pl.BlockSpec((8, 1, 2, 64, PART), lambda c: (0, c, 0, index, 0))

    return block


def ffn_weight(ref):
    return jnp.concatenate([ref[:, 0, 0].reshape(PART, PART), ref[:, 0, 1].reshape(PART, PART)], 0)


def ffn_kernel(
    x_ref, own_ref, other_ref, gain_ref, up_ref, down_ref, y_out, hf_out, pre_out, act_out, part_out, send_out, hf_ref, acc_ref
):
    c = pl.program_id(0)

    @pl.when(c == 0)
    def _():
        y = x_ref[...] + (own_ref[...] + other_ref[...].astype(F32))
        y_out[...] = y
        xhat, _ = norm_parts(y)
        hf = (xhat * gain_ref[...]).astype(BF16)
        hf_ref[...] = hf
        hf_out[0] = hf[:, :PART]
        hf_out[1] = hf[:, PART:]
        acc_ref[...] = jnp.zeros_like(acc_ref)

    pre = dot(hf_ref[...], ffn_weight(up_ref), 1, 0)
    pre_out[...] = pre
    act = (0.5 * pre * (1.0 + lax.erf(pre * (0.5**0.5)))).astype(BF16)
    act_out[...] = act
    acc_ref[...] += dot(act, ffn_weight(down_ref), 1, 1)

    @pl.when(c == QUAD - 1)
    def _():
        part_out[...] = acc_ref[...]
        send_out[...] = acc_ref[...].astype(BF16)


def ffn(x, own, other, gain, w):
    block = ffn_specs(0)
    cols = pl.BlockSpec((TOK, PART), lambda c: (0, c))
    return call(
        ffn_kernel,
        (x, own, other, gain, w, w),
        [
            sds((TOK, D), F32),
            sds((2, TOK, PART), BF16),
            sds((TOK, QUAD * PART), F32),
            sds((TOK, QUAD * PART), BF16),
            sds((TOK, D), F32),
            sds((TOK, D), BF16),
        ],
        grid=(QUAD,),
        specs={4: block(UP), 5: block(DOWN)},
        out_specs={2: cols, 3: cols},
        scratch=[pltpu.VMEM((TOK, D), BF16), pltpu.VMEM((TOK, D), F32)],
        name="ffn",
    )


def ffn_back_kernel(pending, *refs):
    if pending:
        g_ref, own_ref, other_ref, x_ref, gain_ref = refs[:5]
        rest = refs[5:]
    else:
        g_ref = refs[0]
        rest = refs[1:]
    pre_ref, up_ref, down_ref, g_out, back_out, da_out, part_out, send_out, dgain_out, back_ref, acc_ref = rest
    c = pl.program_id(0)

    @pl.when(c == 0)
    def _():
        g = g_ref[...]
        if pending:
            xhat, rstd = norm_parts(x_ref[...])
            add, dgain = norm_back(
                own_ref[...] + other_ref[...].astype(F32), gain_ref[...], xhat, rstd
            )
            g = g + add
            dgain_out[...] = dgain
        else:
            dgain_out[...] = jnp.zeros_like(dgain_out)
        g_out[...] = g
        back = g.astype(BF16)
        back_ref[...] = back
        back_out[0] = back[:, :PART]
        back_out[1] = back[:, PART:]
        acc_ref[...] = jnp.zeros_like(acc_ref)

    d_act = dot(back_ref[...], ffn_weight(down_ref), 1, 0)
    pre = pre_ref[...]
    slope = 0.5 * (1.0 + lax.erf(pre * (0.5**0.5))) + pre * (
        jnp.exp(-0.5 * pre * pre) * np.float32(1.0 / np.sqrt(2.0 * np.pi))
    )
    d_pre = (d_act * slope).astype(BF16)
    da_out[...] = d_pre
    acc_ref[...] += dot(d_pre, ffn_weight(up_ref), 1, 1)

    @pl.when(c == QUAD - 1)
    def _():
        part_out[...] = acc_ref[...]
        send_out[...] = acc_ref[...].astype(BF16)


def ffn_back(g, pending, pre, w):
    block = ffn_specs(0)
    cols = pl.BlockSpec((TOK, PART), lambda c: (0, c))
    args = [g, *(pending or ()), pre, w, w]
    at = len(args) - 3
    return call(
        functools.partial(ffn_back_kernel, pending is not None),
        args,
        [
            sds((TOK, D), F32),
            sds((2, TOK, PART), BF16),
            sds((TOK, QUAD * PART), BF16),
            sds((TOK, D), F32),
            sds((TOK, D), BF16),
            sds((1, D), F32),
        ],
        grid=(QUAD,),
        specs={at: cols, at + 1: block(UP), at + 2: block(DOWN)},
        out_specs={2: cols},
        scratch=[pltpu.VMEM((TOK, D), BF16), pltpu.VMEM((TOK, D), F32)],
        name="ffn_back",
    )


def merge_back_kernel(
    g_ref, own_ref, other_ref, y_ref, gain_ref, wo_ref, o_ref, share_ref, rank_row_ref, rank_col_ref, g_out, back_out, send_out, dgain_out
):
    xhat, rstd = norm_parts(y_ref[...])
    add, dgain = norm_back(own_ref[...] + other_ref[...].astype(F32), gain_ref[...], xhat, rstd)
    dgain_out[...] = dgain
    g = g_ref[...] + add
    g_out[...] = g
    back = g.astype(BF16)
    back_out[0] = back[:, :PART]
    back_out[1] = back[:, PART:]
    dout = dot(back, weight(wo_ref), 1, 0)
    share = share_ref[...]
    o0 = o_ref[0].astype(F32)
    o1 = o_ref[1].astype(F32)
    lanes = iota((TOK, TOK), 1)
    parts = [[], []]
    logs = [[], []]
    for h in range(HN):
        cols = slice(h * DH, (h + 1) * DH)
        s0 = share[:, h : h + 1]
        s1 = share[:, HN + h : HN + h + 1]
        dh = dout[:, cols]
        t0 = jnp.sum(dh * o0[:, cols], axis=-1, keepdims=True)
        t1 = jnp.sum(dh * o1[:, cols], axis=-1, keepdims=True)
        mean = s0 * t0 + s1 * t1
        parts[0].append(s0 * dh)
        parts[1].append(s1 * dh)
        logs[0].append(s0 * (t0 - mean))
        logs[1].append(s1 * (t1 - mean))
    rows = []
    for r in range(ROUNDS):
        rank = rank_col_ref[:, r : r + 1]
        moved = dot(
            send_select(rank_row_ref[r : r + 1, :], TOK),
            jnp.concatenate(parts[r], 1).astype(BF16),
            1,
            0,
        )
        group = hot(iota((TOK, 8), 1) == (rank >> 4))
        for h in range(HN):
            aux = jnp.where(lanes >> 3 == (rank & 15), spread(logs[r][h], lanes), 0.0).astype(BF16)
            extra = dot(group, aux, 0, 0)
            rows.append(
                jnp.concatenate(
                    [moved[i * 8 : i * 8 + 8, h * DH : (h + 1) * DH] for i in range(16)] + [extra],
                    1,
                )
            )
    send_out[...] = jnp.concatenate(rows, 0).astype(BF16)


def merge_back(g, own, other, y, gain, wo, o, share, rank_row, rank_col):
    return call(
        merge_back_kernel,
        (g, own, other, y, gain, wo[0], o, share, rank_row, rank_col),
        [
            sds((TOK, D), F32),
            sds((2, TOK, PART), BF16),
            sds((NW, O_LANES), BF16),
            sds((1, D), F32),
        ],
        specs={5: attn_spec(wo[1])},
        name="merge_back",
    )


def attend_back_kernel(moved_ref, sorted_ref, place_ref, send_out):
    moved = moved_ref[...]
    extra = moved[:, 16 * DH :]
    lanes = iota((NW, TOK), 1)
    d_outs, d_logs = [], []
    for b in range(8):
        pair = jnp.concatenate(
            [
                jnp.concatenate(
                    [
                        moved[:, i * DH : (i + 1) * DH],
                        jnp.where(lanes >> 3 == i, extra.astype(F32), 0.0).astype(BF16),
                    ],
                    1,
                )
                for i in (2 * b, 2 * b + 1)
            ],
            0,
        )
        got = dot(place_select(place_ref, b), pair, 0, 0)
        d_outs.append(got[:, :DH].astype(BF16))
        d_logs.append(jnp.sum(got[:, DH:], axis=-1, keepdims=True))
    d_out = jnp.concatenate(d_outs, 0)
    d_log = jnp.concatenate(d_logs, 0)
    rows = sorted_ref[...]
    keys, inv, unit, own, total, exact = scores_of(rows)
    probs = exact.astype(BF16)
    g_probs = jnp.concatenate(
        [
            dot(
                d_out[c * SPAN : (c + 1) * SPAN],
                rows[c * SPAN : (c + 2) * SPAN, DH:],
                1,
                1,
            )
            for c in range(16)
        ],
        0,
    )
    inner_sum = jnp.sum(g_probs * exact, axis=-1, keepdims=True)
    g_scores = exact * (g_probs - inner_sum + d_log)
    g_scores = jnp.where(own, 0.0, g_scores).astype(BF16)
    d_query, d_unit, d_value = [], [], []
    for c in range(16):
        here = slice(c * SPAN, (c + 1) * SPAN)
        both = slice(c * SPAN, (c + 2) * SPAN)
        after = slice((c + 1) * SPAN, (c + 2) * SPAN)
        d_query.append(dot(g_scores[here], unit[both], 1, 0))
        d_unit.append(dot(g_scores[here], rows[after, :DH], 0, 0))
        d_value.append(dot(probs[here], d_out[here], 0, 0))

    def overlap(parts):
        out = [parts[0][:SPAN]]
        for c in range(15):
            out.append(parts[c][SPAN:] + parts[c + 1][:SPAN])
        out.append(parts[15][SPAN:])
        return jnp.concatenate(out, 0)

    g_unit = overlap(d_unit)
    along = jnp.sum(g_unit * keys, axis=-1, keepdims=True)
    g_keys = inv * g_unit - keys * (inv * inv * inv) * along
    g_query = jnp.concatenate([jnp.zeros((SPAN, DH), F32)] + d_query, 0) + g_keys
    grads = jnp.concatenate([g_query, overlap(d_value)], 1).astype(BF16)
    for b in range(9):
        picked = place_select(place_ref, b)
        if b < 8:
            back = dot(picked, grads[SPAN + b * TOK : SPAN + (b + 1) * TOK], 1, 0)
        else:
            lent = jnp.concatenate([jnp.zeros((SPAN, 2 * DH), BF16), grads[:SPAN]], 0)
            back = dot(picked, lent, 1, 0)
        for j in range(2):
            i = 2 * b + j
            send_out[:, i * 2 * DH : (i + 1) * 2 * DH] = back[j * NW : (j + 1) * NW].astype(BF16)


def attend_back(moved, rows, place):
    return call(
        attend_back_kernel, (moved, rows, place), [sds((NW, QV_LANES), BF16)], name="attend_back"
    )[0]


def project_back_kernel(moved_ref, rank_ref, wq_ref, wv_ref, part_out, send_out, dq_out, dv_out):
    wide = moved_ref[...].astype(F32)
    total = jnp.zeros((TOK, HN * 2 * DH), F32)
    for r in range(ROUNDS):
        rows = jnp.concatenate(
            [
                jnp.concatenate(
                    [
                        wide[r * 32 + h * 8 : r * 32 + h * 8 + 8, i * 2 * DH : (i + 1) * 2 * DH]
                        for h in range(HN)
                    ],
                    1,
                )
                for i in range(SEND_ROWS)
            ],
            0,
        ).astype(BF16)
        total = total + dot(send_select(rank_ref[r : r + 1, :], SEND_ROWS * GROUPS), rows, 0, 0)
    total = total.astype(BF16)
    d_q = jnp.concatenate([total[:, h * 2 * DH : h * 2 * DH + DH] for h in range(HN)], 1)
    d_v = jnp.concatenate([total[:, h * 2 * DH + DH : (h + 1) * 2 * DH] for h in range(HN)], 1)
    dq_out[...] = d_q
    dv_out[...] = d_v
    partial = dot(d_q, weight(wq_ref), 1, 1) + dot(d_v, weight(wv_ref), 1, 1)
    part_out[...] = partial
    send_out[...] = partial.astype(BF16)


def project_back(moved, rank_row, wq, wv):
    return call(
        project_back_kernel,
        (moved, rank_row, wq[0], wv[0]),
        [
            sds((TOK, D), F32),
            sds((TOK, D), BF16),
            sds((TOK, PART), BF16),
            sds((TOK, PART), BF16),
        ],
        specs={2: attn_spec(wq[1]), 3: attn_spec(wv[1])},
        name="project_back",
    )


def last_kernel(g_ref, own_ref, other_ref, x_ref, gain_ref, g_out, dgain_out):
    xhat, rstd = norm_parts(x_ref[...])
    add, dgain = norm_back(own_ref[...] + other_ref[...].astype(F32), gain_ref[...], xhat, rstd)
    g_out[...] = g_ref[...] + add
    dgain_out[...] = dgain


def last(g, own, other, x, gain):
    return call(
        last_kernel, (g, own, other, x, gain), [sds((TOK, D), F32), sds((1, D), F32)], name="last"
    )


def pair_dot(left_a, left_b, right_a, right_b):
    left = jnp.concatenate([left_a, left_b], 0)
    right = jnp.concatenate([right_a, right_b], 0)
    return dot(left, right, 0, 0).astype(BF16)


def ffn_grad_kernel(core_ref, hf_a, hf_b, back_a, back_b, da_a, da_b, u_a, u_b, out_ref):
    up = pair_dot(hf_a[0], hf_b[0], da_a[...], da_b[...])
    down = pair_dot(back_a[0], back_b[0], u_a[...], u_b[...])
    out_ref[:, 0, :64] = up.reshape(8, 64, PART)
    out_ref[:, 0, 64:] = down.reshape(8, 64, PART)


def ffn_grad(core, hf, back, da, act):
    half = pl.BlockSpec((1, TOK, PART), lambda c, core: (core[0], 0, 0))
    cols = pl.BlockSpec((TOK, PART), lambda c, core: (0, c))
    return call(
        ffn_grad_kernel,
        (core, *hf, *back, *da, *act),
        [sds((8, QUAD, 128, PART), BF16)],
        grid=(QUAD,),
        specs={0: half, 1: half, 2: half, 3: half, 4: cols, 5: cols, 6: cols, 7: cols},
        out_specs={0: pl.BlockSpec((8, 1, 128, PART), lambda c, core: (0, c, 0, 0))},
        prefetch=1,
        name="ffn_grad",
    )[0].reshape(32, 128, PART)


def attn_grad_kernel(count, core_ref, *refs):
    out_ref = refs[-1]
    for i in range(count):
        la, lb, ra, rb = refs[4 * i : 4 * i + 4]
        got = pair_dot(la[0], lb[0], ra[...], rb[...])
        out_ref[:, i * 16 : (i + 1) * 16] = got.reshape(32, 16, PART)


def attn_grad(core, pairs):
    half = pl.BlockSpec((1, TOK, PART), lambda i, core: (core[0], 0, 0))
    args = [a for left, right in pairs for a in (*left, *right)]
    specs = {4 * i + j: half for i in range(len(pairs)) for j in range(2)}
    return call(
        functools.partial(attn_grad_kernel, len(pairs)),
        (core, *args),
        [sds((32, 16 * len(pairs), PART), BF16)],
        specs=specs,
        prefetch=1,
        name="attn_grad",
    )[0]


def swap_narrow(values):
    return lax.ppermute(values, "narrow", [(0, 1), (1, 0)])


def with_core(values):
    other = lax.ppermute(values, "wide", [(i, i ^ 1) for i in range(NW)])
    return values, other


def to_all(values):
    return lax.all_to_all(values, "wide", split_axis=0, concat_axis=0, tiled=True)


SAME_CORE = [[2 * k + c for k in range(NW // 2)] for c in range(2)]


def summed(values):
    moved = lax.all_to_all(
        values, "wide", split_axis=0, concat_axis=0, tiled=True, axis_index_groups=SAME_CORE
    )
    return jnp.sum(moved.astype(F32), axis=0)


def gathered(rows):
    got = lax.all_gather(rows, "wide", axis=0, tiled=True)
    return got.reshape(32, 2, rows.shape[0], PART)


def on_device(
    x_first,
    x_second,
    grad_first,
    grad_second,
    sort_target,
    owner,
    master,
    moment_first,
    moment_second,
    gains,
    gain_first,
    gain_second,
):
    me = lax.axis_index("wide").astype(I32)
    half = lax.axis_index("narrow").astype(I32).reshape(1)
    core = (me & 1).reshape(1)

    tiles, parity = tile_rows()
    tile_of_row = np.concatenate([tiles, tiles + 88])
    code = owner[tile_of_row] * 2 + np.concatenate([parity, parity])
    code_col = code.reshape(-1, 1)
    code_row = code.reshape(1, -1)
    is_ffn = (np.arange(176) % 88 >= 24)[None, :]
    slots = me * CAP + jnp.arange(CAP, dtype=I32)
    kind = jnp.any((owner[None, :] == slots[:, None]) & is_ffn, axis=1).astype(I32)
    mine = lax.dynamic_slice_in_dim(sort_target, me * TOK, TOK, axis=2)
    ranks = jnp.sum((mine[:, :, None, :] < mine[:, :, :, None]).astype(I32), axis=3)
    rank_rows = [ranks[l] for l in range(LAYERS)]
    rank_cols = [ranks[l].T for l in range(LAYERS)]
    rnd, group = me >> 5, me & 7
    by_source = lax.dynamic_slice_in_dim(sort_target, rnd, 1, axis=1).reshape(LAYERS, NW, 1, TOK)
    wanted = jnp.concatenate([group * 8 + jnp.arange(8, dtype=I32), ((group * 8 - 1) & 63).reshape(1)])
    inside = (by_source >> 7) == wanted[None, None, :, None]
    low = jnp.min(jnp.where(inside, by_source & 127, TOK), axis=3)
    high = jnp.max(jnp.where(inside, by_source & 127, -1), axis=3)
    places = jnp.stack([low, high], axis=3).reshape(LAYERS, NW, SEND_ROWS)

    moved = to_all(route_out(kind, master))
    first_rows, rest_rows, last_rows = pick(code_col, moved)
    first_w = to_all(jnp.broadcast_to(first_rows[None], (NW, 32, PART))).reshape(32, 2, 32, PART)
    rest_w = gathered(rest_rows)
    last_w = gathered(last_rows)
    attn_w = [
        {"qk": (first_w, 0), "value": (first_w, 1), "out": (rest_w, OUT)},
        {"qk": (last_w, QK), "value": (last_w, VALUE), "out": (last_w, OUT)},
    ]
    ffn_w = [
        rest_w.reshape(8, QUAD, 2, REST_ROWS, PART),
        last_w.reshape(8, QUAD, 2, LAYER_ROWS, PART),
    ]

    flat_gains = gains.reshape(LAYERS * 2, PART)
    x_two, gain_rows = inner(
        half, [(x_second, swap_narrow(x_second)), (flat_gains, swap_narrow(flat_gains))], "inner_a"
    )
    x_one, g_one, g_two = inner(
        half, [(a, swap_narrow(a)) for a in (x_first, grad_first, grad_second)], "inner_b"
    )
    gain = [[gain_rows[2 * l + i].reshape(1, D) for i in range(2)] for l in range(LAYERS)]

    saved = []
    pending = None
    for l in range(LAYERS):
        w = attn_w[l]
        x_two, hn, send = project(x_two, pending, gain[l][0], w["qk"], w["value"], rank_rows[l])
        rows, send = attend(to_all(send), places[l])
        own, send, o, share, merged = merge(to_all(send), rank_rows[l], rank_cols[l], w["out"])
        x_one, hf, pre, act, own_f, send_f = ffn(x_one, own, swap_narrow(send), gain[l][1], ffn_w[l])
        pending = (own_f, swap_narrow(send_f))
        saved.append((x_two, x_one, hn, rows, o, share, merged, hf, pre, act))
    y_two = x_two + (pending[0] + pending[1].astype(F32))
    y_first, y_second = outer(half, (x_one, y_two), "outer_y")

    pending = None
    reduced = [None] * LAYERS
    dgains = [[None, None], [None, None]]
    for l in reversed(range(LAYERS)):
        w = attn_w[l]
        x_in, y_mid, hn, rows, o, share, merged, hf, pre, act = saved[l]
        g_two, back, da, own, send, dgain = ffn_back(g_two, pending, pre, ffn_w[l])
        if pending is not None:
            dgains[l + 1][0] = dgain
        other = swap_narrow(send)
        ffn_rows = summed(
            ffn_grad(core, with_core(hf), with_core(back), with_core(da), with_core(act))
        )
        g_one, back, send, dgains[l][1] = merge_back(
            g_one, own, other, y_mid, gain[l][1], w["out"], o, share, rank_rows[l], rank_cols[l]
        )
        send = attend_back(to_all(send), rows, places[l])
        own, send, dq, dv = project_back(to_all(send), rank_rows[l], w["qk"], w["value"])
        pending = (own, swap_narrow(send), x_in, gain[l][0])
        hn2 = with_core(hn)
        out_pair = (with_core(back), with_core(merged))
        in_pairs = [(hn2, with_core(dq)), (hn2, with_core(dv))]
        if l > 0:
            attn_rows = summed(attn_grad(core, [out_pair] + in_pairs))
        else:
            attn_rows = jnp.concatenate(
                [summed(attn_grad(core, [out_pair])), summed(attn_grad(core, in_pairs))], 0
            )
        reduced[l] = jnp.concatenate([ffn_rows, attn_rows], 0)
    g_two, dgains[0][0] = last(g_two, *pending)
    dx_first, dx_second = outer(half, (g_one, g_two), "outer_dx")

    back_rows = to_all(route_back(code_row, jnp.concatenate(reduced, 0).astype(BF16)))
    slot_grad, slot_first, slot_second, slot_new = slots_update(
        kind, back_rows, master, moment_first, moment_second
    )
    gain_sum = lax.psum(jnp.concatenate([d for pair in dgains for d in pair], 0), "wide")
    gain_grad = outer(half, (gain_sum,), "outer_gain")[0].reshape(LAYERS, 2, PART)
    gain_first_new, gain_second_new, gain_new = adam(
        gain_grad, gain_first, gain_second, gains, RATE_GAIN
    )
    return (
        y_first,
        y_second,
        dx_first,
        dx_second,
        slot_grad,
        slot_first,
        slot_second,
        slot_new,
        gain_grad,
        gain_first_new,
        gain_second_new,
        gain_new,
    )


def solution(mesh):
    rows = P("wide", "narrow")
    tiles = P("wide", None, "narrow")
    gains = P(None, None, "narrow")
    return jax.shard_map(
        on_device,
        mesh=mesh,
        in_specs=(rows,) * 4 + (P(), P()) + (tiles,) * 3 + (gains,) * 3,
        out_specs=(rows,) * 4 + (tiles,) * 4 + (gains,) * 4,
        check_vma=False,
    )
```

```python
import functools

import jax
import jax.numpy as jnp
import numpy as np
from jax import lax
from jax.experimental import pallas as pl
from jax.experimental.pallas import tpu as pltpu
from jax.sharding import PartitionSpec as P

D = 1024
PART = 512
DH = 128
HN = 4
SPAN = 64
TR = 128
CAP = 5
TOK = 128
NW = 64
LAYERS = 2
ROUNDS = 2
STEP = 5
GROUPS = 8
QV_LANES = 5 * DH
O_LANES = 3 * DH
ROWS = NW * 8
QUAD = 4
UP, DOWN = 0, 1
LAYER_ROWS = 176
REST_ROWS = 144
EARLY_ROWS = 192
FFN_ROWS = 128

MASK_FILL = -1000000000.0
NORM_EPS = 1e-05
BETA_ONE = 0.5
BETA_TWO = 0.5
RATE_WEIGHT = 0.05
RATE_GAIN = 0.2
DECAY = 0.01
EPSILON = 1e-08

F32 = jnp.float32
BF16 = jnp.bfloat16
I32 = jnp.int32
VMEM_BYTES = 56 * 1024 * 1024


def feature_of(p):
    c0 = p >> 9
    j3 = (p >> 6) & 7
    tau = (p >> 4) & 3
    t = (p >> 1) & 7
    e = p & 1
    return t * 128 + tau * 32 + c0 * 16 + j3 * 2 + e


def tile_rows():
    tiles, parity = [], []
    for base in (24, 56):
        for tau in range(4):
            for t in range(8):
                for e in range(2):
                    tiles.append(base + t * 4 + tau)
                    parity.append(e)
    for base in (16, 0, 8):
        for t in range(8):
            for e in range(2):
                tiles.append(base + t)
                parity.append(e)
    return np.array(tiles, np.int32), np.array(parity, np.int32)


def iota(shape, dim):
    return lax.broadcasted_iota(I32, shape, dim)


def hot(mask):
    return jnp.where(mask, 1.0, 0.0).astype(BF16)


def dot(a, b, ca, cb):
    return lax.dot_general(a, b, (((ca,), (cb,)), ((), ())), preferred_element_type=F32)


def call(kernel, args, outs, grid=(1,), specs=None, out_specs=None, scratch=(), prefetch=0, name=None):
    specs = specs or {}
    out_specs = out_specs or {}
    def whole(shape):
        zeros = (0,) * len(shape)
        return pl.BlockSpec(shape, lambda *_: zeros)
    in_list = [specs.get(i, whole(a.shape)) for i, a in enumerate(args[prefetch:])]
    out_list = [out_specs.get(i, whole(o.shape)) for i, o in enumerate(outs)]
    return pl.pallas_call(
        kernel,
        out_shape=outs,
        grid_spec=pltpu.PrefetchScalarGridSpec(
            num_scalar_prefetch=prefetch,
            grid=grid,
            in_specs=in_list,
            out_specs=out_list,
            scratch_shapes=list(scratch),
        ),
        compiler_params=pltpu.CompilerParams(vmem_limit_bytes=VMEM_BYTES),
        name=name,
    )(*args)


def sds(shape, dtype):
    return jax.ShapeDtypeStruct(shape, dtype)


def norm_parts(values):
    mean = jnp.mean(values, axis=-1, keepdims=True)
    var = jnp.mean(values * values, axis=-1, keepdims=True) - mean * mean
    rstd = lax.rsqrt(var + NORM_EPS)
    return (values - mean) * rstd, rstd


def norm_back(upstream, gain, xhat, rstd):
    gh = upstream * gain
    m1 = jnp.mean(gh, axis=-1, keepdims=True)
    m2 = jnp.mean(gh * xhat, axis=-1, keepdims=True)
    return rstd * (gh - m1 - xhat * m2), jnp.sum(upstream * xhat, axis=0, keepdims=True)


def flat(ref):
    return ref[...].reshape(PART, PART)


def halves(core, first, second):
    mine = core == 0
    return jnp.where(mine, first, second), jnp.where(mine, second, first)


def into(core, full, weights):
    own, other = halves(core, full[:, :PART], full[:, PART:])
    return dot(own.astype(BF16), weights[0], 1, 0) + dot(other.astype(BF16), weights[1], 1, 0)


def out_of(core, part, weights):
    return halves(core, dot(part, weights[0], 1, 1), dot(part, weights[1], 1, 1))


def wanted(shape, dim):
    m = iota(shape, dim)
    g16 = (m >> 3) * 16
    b = m & 7
    before = (g16 - 2) & 127
    lent = before + (b >> 1)
    return (
        g16 + 2 * b,
        g16 + 2 * b + 1,
        jnp.where((b == 0) | (b == 2), lent, -1),
        jnp.where((b == 1) | (b == 3), lent, -1),
    )


def send_hots(rank_row, count=4):
    return hot(jnp.concatenate(wanted((NW, 1), 0)[:count], 0) == rank_row)


def return_hots(rank_col, count=4):
    return hot(rank_col == jnp.concatenate(wanted((1, NW), 1)[:count], 1))


def spread(col, lanes):
    hi, mid, lo = pieces(col)
    k = lanes & 7
    return jnp.where(k == 0, hi, jnp.where(k == 1, mid, jnp.where(k == 2, lo, 0.0)))


def pieces(col):
    hi = col.astype(BF16).astype(F32)
    rest = col - hi
    mid = rest.astype(BF16).astype(F32)
    return hi, mid, rest - mid


def either(lanes, even, odd):
    return jnp.where(lanes < 8, even, jnp.where(lanes < 16, odd, 0.0))


def slot_rows(kind):
    r = iota((TR, 1), 0)
    e = r >> 6
    j = r & 63
    c0 = j & 1
    tau = (j >> 1) & 3
    j3 = j >> 3
    low = c0 * 16 + j3 * 2 + e
    row = jnp.where(kind == 1, low * 4 + tau, tau * 32 + low)
    return hot(row == iota((TR, TR), 1))


def route_out_kernel(kind_ref, master_ref, out_ref):
    picked = slot_rows(kind_ref[pl.program_id(0)])
    rows = dot(picked, master_ref[0].astype(BF16), 1, 0).astype(BF16)
    out_ref[:, :PART] = rows[:NW]
    out_ref[:, PART:] = rows[NW:]


def route_out(kind, master):
    return call(
        route_out_kernel,
        (kind, master),
        [sds((NW, CAP * 2 * PART), BF16)],
        grid=(CAP,),
        specs={0: pl.BlockSpec((1, TR, PART), lambda s, k: (s, 0, 0))},
        out_specs={0: pl.BlockSpec((NW, 2 * PART), lambda s, k: (0, s))},
        prefetch=1,
        name="route_out",
    )[0]


def slot_code(rows, dim):
    shape = (rows, 1) if dim == 0 else (1, rows)
    m = iota(shape, dim)
    k = m & 63
    e = (m >> 6) & 1
    s = m >> 7
    return (k * CAP + s) * 2 + e


def pick_kernel(code_ref, moved_ref, first_ref, early_ref, late_ref):
    all_rows = jnp.concatenate([moved_ref[:, m * PART : (m + 1) * PART] for m in range(2 * CAP)], 0)
    picked = hot(code_ref[...] == slot_code(2 * CAP * NW, 1))
    rows = dot(picked, all_rows, 1, 0).astype(BF16)
    first_ref[...] = jnp.broadcast_to(rows[REST_ROWS:LAYER_ROWS][None], first_ref.shape)
    early_ref[:REST_ROWS] = rows[:REST_ROWS]
    early_ref[REST_ROWS:] = rows[LAYER_ROWS + FFN_ROWS :]
    late_ref[...] = rows[LAYER_ROWS : LAYER_ROWS + FFN_ROWS]


def pick(code_col, moved):
    return call(
        pick_kernel,
        (code_col, moved),
        [sds((32, 32, PART), BF16), sds((EARLY_ROWS, PART), BF16), sds((FFN_ROWS, PART), BF16)],
        name="pick",
    )


def route_back_kernel(code_ref, rows_ref, gains_ref, out_ref):
    placed = hot(slot_code(2 * CAP * NW, 0) == code_ref[...])
    rows = dot(placed, rows_ref[...].astype(BF16), 1, 0).astype(BF16)
    for m in range(2 * CAP):
        out_ref[:, m * PART : (m + 1) * PART] = rows[m * NW : (m + 1) * NW]
    base = 2 * CAP * PART
    for i in range(2 * LAYERS):
        row = jnp.broadcast_to(gains_ref[i : i + 1, :], (NW, D)).astype(BF16)
        out_ref[:, base + i * D : base + (i + 1) * D] = row


def route_back(code_row, rows, gains):
    return call(
        route_back_kernel,
        (code_row, rows, gains),
        [sds((NW, CAP * 2 * PART + 2 * LAYERS * D), BF16)],
        name="route_back",
    )[0]


def adam(grad, first, second, weights, rate):
    first_new = BETA_ONE * first + (1.0 - BETA_ONE) * grad
    second_new = BETA_TWO * second + (1.0 - BETA_TWO) * grad * grad
    step = (
        first_new
        / (1.0 - BETA_ONE**STEP)
        / (jnp.sqrt(second_new / (1.0 - BETA_TWO**STEP)) + EPSILON)
    )
    return first_new, second_new, weights - rate * (step + DECAY * weights)


def slots_kernel(kind_ref, moved_ref, m_ref, a_ref, b_ref, grad_ref, first_ref, second_ref, new_ref):
    placed = slot_rows(kind_ref[pl.program_id(0)])
    rows = jnp.concatenate([moved_ref[:, :PART], moved_ref[:, PART:]], 0)
    grad = dot(placed, rows, 0, 0)
    grad_ref[0] = grad
    first_ref[0], second_ref[0], new_ref[0] = adam(grad, a_ref[0], b_ref[0], m_ref[0], RATE_WEIGHT)


def slots_update(kind, moved, master, first, second):
    tile = pl.BlockSpec((1, TR, PART), lambda s, k: (s, 0, 0))
    return call(
        slots_kernel,
        (kind, moved, master, first, second),
        [sds((CAP, TR, PART), F32)] * 4,
        grid=(CAP,),
        specs={0: pl.BlockSpec((NW, 2 * PART), lambda s, k: (0, s)), 1: tile, 2: tile, 3: tile},
        out_specs={i: tile for i in range(4)},
        prefetch=1,
        name="slots_update",
    )


def inner_kernel(half_ref, *refs):
    count = len(refs) // 3
    n = half_ref[0]
    feature = feature_of(iota((1, D), 1))
    mine = hot(feature == iota((PART, 1), 0) + n * PART)
    theirs = hot(feature == iota((PART, 1), 0) + (1 - n) * PART)
    for i in range(count):
        own, other, out = refs[2 * i], refs[2 * i + 1], refs[2 * count + i]
        if own.dtype == BF16:
            out[...] = dot(own[...], mine, 1, 0) + dot(other[...], theirs, 1, 0)
        else:
            total = jnp.zeros(out.shape, F32)
            for a, b in zip(pieces(own[...]), pieces(other[...])):
                total = total + (dot(a.astype(BF16), mine, 1, 0) + dot(b.astype(BF16), theirs, 1, 0))
            out[...] = total


def inner(half, pairs, name):
    flat = [a for pair in pairs for a in pair]
    outs = [sds((own.shape[0], D), F32) for own, _ in pairs]
    return call(inner_kernel, (half, *flat), outs, prefetch=1, name=name)


def outer_kernel(count, half_ref, *refs):
    n = half_ref[0]
    feature = feature_of(iota((1, D), 1))
    back = hot(feature == iota((PART, 1), 0) + n * PART)
    for i in range(count):
        total = jnp.zeros(refs[count + i].shape, F32)
        for part in pieces(refs[i][...]):
            total = total + dot(part.astype(BF16), back, 1, 1)
        refs[count + i][...] = total


def outer(half, arrays, name):
    outs = [sds((a.shape[0], PART), F32) for a in arrays]
    return call(
        functools.partial(outer_kernel, len(arrays)), (half, *arrays), outs, prefetch=1, name=name
    )


def attn_spec(index):
    return pl.BlockSpec((32, 16, PART), lambda *_: (0, index, 0))


def attn_specs(args, places):
    specs = {}
    for at in places:
        specs[at - 1] = attn_spec(args[at][1])
        args[at] = args[at][0]
    return specs


def project_kernel(pending, core_ref, *refs):
    if pending:
        x_ref, own_ref, other_ref, *rest = refs
        x = x_ref[...] + (own_ref[...] + other_ref[...].astype(F32))
    else:
        x_ref, *rest = refs
        x = x_ref[...]
    gain_ref, q_own, q_other, v_own, v_other, rank_ref, x_out, hn_out, send_out = rest
    core = core_ref[0]
    x_out[...] = x
    xhat, _ = norm_parts(x)
    hn = xhat * gain_ref[...]
    hn_out[0] = hn[:, :PART].astype(BF16)
    hn_out[1] = hn[:, PART:].astype(BF16)
    q = into(core, hn, (flat(q_own), flat(q_other))).astype(BF16)
    v = into(core, hn, (flat(v_own), flat(v_other))).astype(BF16)
    qv = jnp.concatenate([m[:, h * DH : (h + 1) * DH] for h in range(HN) for m in (q, v)], 1)
    for r in range(ROUNDS):
        moved = dot(send_hots(rank_ref[r : r + 1, :]), qv, 1, 0)
        even, odd = moved[:NW].astype(BF16), moved[NW : 2 * NW].astype(BF16)
        lent_q, lent_v = moved[2 * NW : 3 * NW], moved[3 * NW :]
        for h in range(HN):
            rows = slice((r * HN + h) * NW, (r * HN + h + 1) * NW)
            at = h * 2 * DH
            send_out[rows, : 2 * DH] = even[:, at : at + 2 * DH]
            send_out[rows, 2 * DH : 4 * DH] = odd[:, at : at + 2 * DH]
            send_out[rows, 4 * DH :] = (
                lent_q[:, at : at + DH] + lent_v[:, at + DH : at + 2 * DH]
            ).astype(BF16)


def project(core, x, pending, gain, wq, wv, rank_row):
    args = [core, x, *(pending or ()), gain, *wq, *wv, rank_row]
    at = len(args) - 5
    specs = attn_specs(args, range(at, at + 4))
    return call(
        functools.partial(project_kernel, pending is not None),
        args,
        [sds((TOK, D), F32), sds((2, TOK, PART), BF16), sds((ROWS, QV_LANES), BF16)],
        specs=specs,
        prefetch=1,
        name="project",
    )


def scores_of(rows):
    keys = rows[:, :DH].astype(F32)
    inv = lax.rsqrt(jnp.sum(keys * keys, axis=-1, keepdims=True) + 1e-06)
    unit = (keys * inv).astype(BF16)
    scores = jnp.concatenate(
        [
            dot(
                rows[(c + 1) * SPAN : (c + 2) * SPAN, :DH],
                unit[c * SPAN : (c + 2) * SPAN],
                1,
                1,
            )
            for c in range(16)
        ],
        0,
    )
    own = iota((1024, TOK), 1) == (iota((1024, TOK), 0) & (SPAN - 1)) + SPAN
    scores = jnp.where(own, MASK_FILL, scores)
    peak = jnp.max(scores, axis=-1, keepdims=True)
    total = peak + jnp.log(jnp.sum(jnp.exp(scores - peak), axis=-1, keepdims=True))
    exact = jnp.exp(scores - total)
    return keys, inv, unit, own, total, exact


def arrive(place_row_ref, j, rows):
    count = 1024 if j < 2 else SPAN
    return dot(hot(iota((count, 1), 0) == place_row_ref[j : j + 1, :]), rows, 1, 0)


def leave(place_col_ref, j, rows):
    return dot(hot(place_col_ref[:, j : j + 1] == iota((1, rows.shape[0]), 1)), rows, 1, 0)


def attend_kernel(moved_ref, place_row_ref, place_col_ref, sorted_out, send_out):
    q_lent = arrive(place_row_ref, 2, moved_ref[:, 4 * DH :])
    v_lent = arrive(place_row_ref, 3, moved_ref[:, 4 * DH :])
    main = arrive(place_row_ref, 0, moved_ref[:, : 2 * DH]) + arrive(
        place_row_ref, 1, moved_ref[:, 2 * DH : 4 * DH]
    )
    rows = jnp.concatenate([jnp.concatenate([q_lent, v_lent], 1), main], 0).astype(BF16)
    sorted_out[...] = rows
    _, _, _, _, total, exact = scores_of(rows)
    probs = exact.astype(BF16)
    outs = jnp.concatenate(
        [
            dot(probs[c * SPAN : (c + 1) * SPAN], rows[c * SPAN : (c + 2) * SPAN, DH:], 1, 0)
            for c in range(16)
        ],
        0,
    )
    aux = spread(total, iota((1024, TOK), 1))
    both = jnp.concatenate([outs, aux], 1).astype(BF16)
    even = leave(place_col_ref, 0, both)
    odd = leave(place_col_ref, 1, both)
    send_out[:, :DH] = even[:, :DH].astype(BF16)
    send_out[:, DH : 2 * DH] = odd[:, :DH].astype(BF16)
    lanes = iota((ROWS, TOK), 1)
    send_out[:, 2 * DH :] = either(lanes, even[:, DH:], odd[:, DH:]).astype(BF16)


def attend(moved, place_row, place_col):
    return call(
        attend_kernel,
        (moved, place_row, place_col),
        [sds((1088, 2 * DH), BF16), sds((ROWS, O_LANES), BF16)],
        name="attend",
    )


def by_head(ref, r, cols):
    return jnp.concatenate(
        [ref[(r * HN + h) * NW : (r * HN + h + 1) * NW, cols] for h in range(HN)], 1
    )


def merge_kernel(
    core_ref, moved_ref, rank_col_ref, w_own, w_other, part_out, send_out, o_out, share_out, merged_out
):
    lanes = iota((TOK, TOK), 1)
    outs, logs = [], []
    for r in range(ROUNDS):
        hots = return_hots(rank_col_ref[:, r : r + 1], 2)
        aux = by_head(moved_ref, r, slice(2 * DH, 3 * DH))
        even = dot(
            hots[:, :NW], jnp.concatenate([by_head(moved_ref, r, slice(0, DH)), aux], 1), 1, 0
        )
        odd = dot(
            hots[:, NW:], jnp.concatenate([by_head(moved_ref, r, slice(DH, 2 * DH)), aux], 1), 1, 0
        )
        outs.append(even[:, :PART] + odd[:, :PART])
        o_out[r] = outs[r].astype(BF16)
        logs.append(
            [
                jnp.sum(
                    either(
                        lanes,
                        even[:, PART + h * DH : PART + (h + 1) * DH],
                        odd[:, PART + h * DH : PART + (h + 1) * DH],
                    ),
                    axis=-1,
                    keepdims=True,
                )
                for h in range(HN)
            ]
        )
    merged = []
    share_all = jnp.zeros((TOK, TOK), F32)
    for h in range(HN):
        top = jnp.maximum(logs[0][h], logs[1][h])
        e0 = jnp.exp(logs[0][h] - top)
        e1 = jnp.exp(logs[1][h] - top)
        total = e0 + e1
        cols = slice(h * DH, (h + 1) * DH)
        s0, s1 = e0 / total, e1 / total
        merged.append(s0 * outs[0][:, cols] + s1 * outs[1][:, cols])
        share_all = jnp.where(lanes == h, s0, jnp.where(lanes == HN + h, s1, share_all))
    share_out[...] = share_all
    merged = jnp.concatenate(merged, 1).astype(BF16)
    merged_out[...] = merged
    put_halves(out_of(core_ref[0], merged, (flat(w_own), flat(w_other))), part_out, send_out)


def put_halves(pair, part_out, send_out):
    for i in range(2):
        cols = slice(i * PART, (i + 1) * PART)
        part_out[:, cols] = pair[i]
        send_out[:, cols] = pair[i].astype(BF16)


def merge(core, moved, rank_col, wo):
    args = [core, moved, rank_col, *wo]
    specs = attn_specs(args, (3, 4))
    return call(
        merge_kernel,
        args,
        [
            sds((TOK, D), F32),
            sds((TOK, D), BF16),
            sds((ROUNDS, TOK, PART), BF16),
            sds((TOK, TOK), F32),
            sds((TOK, PART), BF16),
        ],
        specs=specs,
        prefetch=1,
        name="merge",
    )


def ffn_spec(index):
    return pl.BlockSpec((8, 1, 64, PART), lambda c, _: (0, c, index, 0))


def ffn_kernel(
    core_ref, x_ref, own_ref, other_ref, gain_ref, up_own, up_other, down_own, down_other,
    y_out, hf_out, pre_out, act_out, part_out, send_out, hf_ref, acc_ref
):
    c = pl.program_id(0)
    core = core_ref[0]

    @pl.when(c == 0)
    def _():
        y = x_ref[...] + (own_ref[...] + other_ref[...].astype(F32))
        y_out[...] = y
        xhat, _ = norm_parts(y)
        hf = xhat * gain_ref[...]
        first, second = hf[:, :PART], hf[:, PART:]
        hf_out[0] = first.astype(BF16)
        hf_out[1] = second.astype(BF16)
        own, other = halves(core, first, second)
        hf_ref[0] = own.astype(BF16)
        hf_ref[1] = other.astype(BF16)
        acc_ref[...] = jnp.zeros_like(acc_ref)

    pre = dot(hf_ref[0], flat(up_own), 1, 0) + dot(hf_ref[1], flat(up_other), 1, 0)
    pre_out[...] = pre
    act = (0.5 * pre * (1.0 + lax.erf(pre * (0.5**0.5)))).astype(BF16)
    act_out[...] = act
    acc_ref[0] += dot(act, flat(down_own), 1, 1)
    acc_ref[1] += dot(act, flat(down_other), 1, 1)

    @pl.when(c == QUAD - 1)
    def _():
        put_halves(halves(core, acc_ref[0], acc_ref[1]), part_out, send_out)


def ffn(core, x, own, other, gain, w):
    cols = pl.BlockSpec((TOK, PART), lambda c, _: (0, c))
    return call(
        ffn_kernel,
        (core, x, own, other, gain, w[0], w[1], w[0], w[1]),
        [
            sds((TOK, D), F32),
            sds((2, TOK, PART), BF16),
            sds((TOK, QUAD * PART), F32),
            sds((TOK, QUAD * PART), BF16),
            sds((TOK, D), F32),
            sds((TOK, D), BF16),
        ],
        grid=(QUAD,),
        specs={4: ffn_spec(UP), 5: ffn_spec(UP), 6: ffn_spec(DOWN), 7: ffn_spec(DOWN)},
        out_specs={2: cols, 3: cols},
        scratch=[pltpu.VMEM((2, TOK, PART), BF16), pltpu.VMEM((2, TOK, PART), F32)],
        prefetch=1,
        name="ffn",
    )


def ffn_back_kernel(pending, core_ref, *refs):
    if pending:
        g_ref, own_ref, other_ref, x_ref, gain_ref, *rest = refs
    else:
        g_ref, *rest = refs
    pre_ref, up_own, up_other, down_own, down_other, *rest = rest
    g_out, back_out, da_out, part_out, send_out, dgain_out, back_ref, acc_ref = rest
    c = pl.program_id(0)
    core = core_ref[0]

    @pl.when(c == 0)
    def _():
        g = g_ref[...]
        if pending:
            xhat, rstd = norm_parts(x_ref[...])
            add, dgain = norm_back(
                own_ref[...] + other_ref[...].astype(F32), gain_ref[...], xhat, rstd
            )
            g = g + add
            dgain_out[...] = dgain
        else:
            dgain_out[...] = jnp.zeros_like(dgain_out)
        g_out[...] = g
        first, second = g[:, :PART], g[:, PART:]
        back_out[0] = first.astype(BF16)
        back_out[1] = second.astype(BF16)
        own, other = halves(core, first, second)
        back_ref[0] = own.astype(BF16)
        back_ref[1] = other.astype(BF16)
        acc_ref[...] = jnp.zeros_like(acc_ref)

    d_act = dot(back_ref[0], flat(down_own), 1, 0) + dot(back_ref[1], flat(down_other), 1, 0)
    pre = pre_ref[...]
    slope = 0.5 * (1.0 + lax.erf(pre * (0.5**0.5))) + pre * (
        jnp.exp(-0.5 * pre * pre) * np.float32(1.0 / np.sqrt(2.0 * np.pi))
    )
    d_pre = (d_act * slope).astype(BF16)
    da_out[...] = d_pre
    acc_ref[0] += dot(d_pre, flat(up_own), 1, 1)
    acc_ref[1] += dot(d_pre, flat(up_other), 1, 1)

    @pl.when(c == QUAD - 1)
    def _():
        put_halves(halves(core, acc_ref[0], acc_ref[1]), part_out, send_out)


def ffn_back(core, g, pending, pre, w):
    cols = pl.BlockSpec((TOK, PART), lambda c, _: (0, c))
    args = [core, g, *(pending or ()), pre, w[0], w[1], w[0], w[1]]
    at = len(args) - 6
    specs = {at: cols}
    for i, index in enumerate((UP, UP, DOWN, DOWN)):
        specs[at + 1 + i] = ffn_spec(index)
    return call(
        functools.partial(ffn_back_kernel, pending is not None),
        args,
        [
            sds((TOK, D), F32),
            sds((2, TOK, PART), BF16),
            sds((TOK, QUAD * PART), BF16),
            sds((TOK, D), F32),
            sds((TOK, D), BF16),
            sds((1, D), F32),
        ],
        grid=(QUAD,),
        specs=specs,
        out_specs={2: cols},
        scratch=[pltpu.VMEM((2, TOK, PART), BF16), pltpu.VMEM((2, TOK, PART), F32)],
        prefetch=1,
        name="ffn_back",
    )


def merge_back_kernel(
    core_ref, g_ref, own_ref, other_ref, y_ref, gain_ref, w_own, w_other, o_ref, share_ref, rank_row_ref,
    g_out, back_out, send_out, dgain_out
):
    xhat, rstd = norm_parts(y_ref[...])
    add, dgain = norm_back(own_ref[...] + other_ref[...].astype(F32), gain_ref[...], xhat, rstd)
    dgain_out[...] = dgain
    g = g_ref[...] + add
    g_out[...] = g
    back_out[0] = g[:, :PART].astype(BF16)
    back_out[1] = g[:, PART:].astype(BF16)
    dout = into(core_ref[0], g, (flat(w_own), flat(w_other)))
    share = share_ref[...]
    o0 = o_ref[0].astype(F32)
    o1 = o_ref[1].astype(F32)
    lanes = iota((TOK, TOK), 1)
    parts = [[], []]
    logs = [[], []]
    for h in range(HN):
        cols = slice(h * DH, (h + 1) * DH)
        s0 = share[:, h : h + 1]
        s1 = share[:, HN + h : HN + h + 1]
        dh = dout[:, cols]
        t0 = jnp.sum(dh * o0[:, cols], axis=-1, keepdims=True)
        t1 = jnp.sum(dh * o1[:, cols], axis=-1, keepdims=True)
        mean = s0 * t0 + s1 * t1
        parts[0].append(s0 * dh)
        parts[1].append(s1 * dh)
        logs[0].append(spread(s0 * (t0 - mean), lanes))
        logs[1].append(spread(s1 * (t1 - mean), lanes))
    lanes = iota((NW, TOK), 1)
    for r in range(ROUNDS):
        moved = dot(
            send_hots(rank_row_ref[r : r + 1, :], 2),
            jnp.concatenate(parts[r] + logs[r], 1).astype(BF16),
            1,
            0,
        )
        even, odd = moved[:NW], moved[NW:]
        for h in range(HN):
            rows = slice((r * HN + h) * NW, (r * HN + h + 1) * NW)
            cols = slice(h * DH, (h + 1) * DH)
            aux = slice(PART + h * DH, PART + (h + 1) * DH)
            send_out[rows, :DH] = even[:, cols].astype(BF16)
            send_out[rows, DH : 2 * DH] = odd[:, cols].astype(BF16)
            send_out[rows, 2 * DH :] = either(lanes, even[:, aux], odd[:, aux]).astype(BF16)


def merge_back(core, g, own, other, y, gain, wo, o, share, rank_row):
    args = [core, g, own, other, y, gain, *wo, o, share, rank_row]
    specs = attn_specs(args, (6, 7))
    return call(
        merge_back_kernel,
        args,
        [
            sds((TOK, D), F32),
            sds((2, TOK, PART), BF16),
            sds((ROWS, O_LANES), BF16),
            sds((1, D), F32),
        ],
        specs=specs,
        prefetch=1,
        name="merge_back",
    )


def attend_back_kernel(moved_ref, sorted_ref, place_row_ref, place_col_ref, send_out):
    lanes = iota((ROWS, TOK), 1)
    aux = moved_ref[:, 2 * DH :].astype(F32)
    got = jnp.zeros((1024, 2 * DH), F32)
    for j in range(2):
        here = jnp.where(lanes >> 3 == j, aux, 0.0).astype(BF16)
        pair = jnp.concatenate([moved_ref[:, j * DH : (j + 1) * DH], here], 1)
        got = got + arrive(place_row_ref, j, pair)
    d_out = got[:, :DH].astype(BF16)
    d_log = jnp.sum(got[:, DH:], axis=-1, keepdims=True)
    rows = sorted_ref[...]
    keys, inv, unit, own, _, exact = scores_of(rows)
    probs = exact.astype(BF16)
    g_probs = jnp.concatenate(
        [
            dot(d_out[c * SPAN : (c + 1) * SPAN], rows[c * SPAN : (c + 2) * SPAN, DH:], 1, 1)
            for c in range(16)
        ],
        0,
    )
    inner_sum = jnp.sum(g_probs * exact, axis=-1, keepdims=True)
    g_scores = exact * (g_probs - inner_sum + d_log)
    g_scores = jnp.where(own, 0.0, g_scores).astype(BF16)
    d_query, d_unit, d_value = [], [], []
    for c in range(16):
        here = slice(c * SPAN, (c + 1) * SPAN)
        both = slice(c * SPAN, (c + 2) * SPAN)
        after = slice((c + 1) * SPAN, (c + 2) * SPAN)
        d_query.append(dot(g_scores[here], unit[both], 1, 0))
        d_unit.append(dot(g_scores[here], rows[after, :DH], 0, 0))
        d_value.append(dot(probs[here], d_out[here], 0, 0))

    def overlap(parts):
        out = [parts[0][:SPAN]]
        for c in range(15):
            out.append(parts[c][SPAN:] + parts[c + 1][:SPAN])
        out.append(parts[15][SPAN:])
        return jnp.concatenate(out, 0)

    g_unit = overlap(d_unit)
    along = jnp.sum(g_unit * keys, axis=-1, keepdims=True)
    g_keys = inv * g_unit - keys * (inv * inv * inv) * along
    g_query = jnp.concatenate([jnp.zeros((SPAN, DH), F32)] + d_query, 0) + g_keys
    grads = jnp.concatenate([g_query, overlap(d_value)], 1).astype(BF16)
    for j in range(2):
        cols = slice(j * 2 * DH, (j + 1) * 2 * DH)
        send_out[:, cols] = leave(place_col_ref, j, grads[SPAN:]).astype(BF16)
    lent = leave(place_col_ref, 2, grads[:SPAN, :DH]) + leave(place_col_ref, 3, grads[:SPAN, DH:])
    send_out[:, 4 * DH :] = lent.astype(BF16)


def attend_back(moved, rows, place_row, place_col):
    return call(
        attend_back_kernel,
        (moved, rows, place_row, place_col),
        [sds((ROWS, QV_LANES), BF16)],
        name="attend_back",
    )[0]


def project_back_kernel(
    core_ref, moved_ref, rank_col_ref, q_own, q_other, v_own, v_other, part_out, send_out, dq_out, dv_out
):
    total = jnp.zeros((TOK, HN * 2 * DH), F32)
    lent_q = jnp.zeros((TOK, PART), F32)
    lent_v = jnp.zeros((TOK, PART), F32)
    for r in range(ROUNDS):
        hots = return_hots(rank_col_ref[:, r : r + 1])
        total = total + dot(hots[:, :NW], by_head(moved_ref, r, slice(0, 2 * DH)), 1, 0)
        total = total + dot(hots[:, NW : 2 * NW], by_head(moved_ref, r, slice(2 * DH, 4 * DH)), 1, 0)
        lent = by_head(moved_ref, r, slice(4 * DH, 5 * DH))
        lent_q = lent_q + dot(hots[:, 2 * NW : 3 * NW], lent, 1, 0)
        lent_v = lent_v + dot(hots[:, 3 * NW :], lent, 1, 0)
    d_q = jnp.concatenate([total[:, h * 2 * DH : h * 2 * DH + DH] for h in range(HN)], 1)
    d_v = jnp.concatenate([total[:, h * 2 * DH + DH : (h + 1) * 2 * DH] for h in range(HN)], 1)
    d_q = (d_q + lent_q).astype(BF16)
    d_v = (d_v + lent_v).astype(BF16)
    dq_out[...] = d_q
    dv_out[...] = d_v
    core = core_ref[0]
    from_q = out_of(core, d_q, (flat(q_own), flat(q_other)))
    from_v = out_of(core, d_v, (flat(v_own), flat(v_other)))
    put_halves([a + b for a, b in zip(from_q, from_v)], part_out, send_out)


def project_back(core, moved, rank_col, wq, wv):
    args = [core, moved, rank_col, *wq, *wv]
    specs = attn_specs(args, range(3, 7))
    return call(
        project_back_kernel,
        args,
        [
            sds((TOK, D), F32),
            sds((TOK, D), BF16),
            sds((TOK, PART), BF16),
            sds((TOK, PART), BF16),
        ],
        specs=specs,
        prefetch=1,
        name="project_back",
    )


def last_kernel(g_ref, own_ref, other_ref, x_ref, gain_ref, g_out, dgain_out):
    xhat, rstd = norm_parts(x_ref[...])
    add, dgain = norm_back(own_ref[...] + other_ref[...].astype(F32), gain_ref[...], xhat, rstd)
    g_out[...] = g_ref[...] + add
    dgain_out[...] = dgain


def last(g, own, other, x, gain):
    return call(
        last_kernel, (g, own, other, x, gain), [sds((TOK, D), F32), sds((1, D), F32)], name="last"
    )


def pair_dot(left_a, left_b, right_a, right_b):
    left = jnp.concatenate([left_a, left_b], 0)
    right = jnp.concatenate([right_a, right_b], 0)
    return dot(left, right, 0, 0).astype(BF16)


def ffn_grad_kernel(core_ref, hf_a, hf_b, back_a, back_b, da_a, da_b, u_a, u_b, out_ref):
    up = pair_dot(hf_a[0], hf_b[0], da_a[...], da_b[...])
    down = pair_dot(back_a[0], back_b[0], u_a[...], u_b[...])
    out_ref[0, :, :64] = up.reshape(8, 64, PART)
    out_ref[0, :, 64:] = down.reshape(8, 64, PART)


def ffn_grad(core, hf, back, da, act):
    half = pl.BlockSpec((1, TOK, PART), lambda c, core: (core[0], 0, 0))
    cols = pl.BlockSpec((TOK, PART), lambda c, core: (0, c))
    return call(
        ffn_grad_kernel,
        (core, *hf, *back, *da, *act),
        [sds((QUAD, 8, 128, PART), BF16)],
        grid=(QUAD,),
        specs={0: half, 1: half, 2: half, 3: half, 4: cols, 5: cols, 6: cols, 7: cols},
        out_specs={0: pl.BlockSpec((1, 8, 128, PART), lambda c, core: (c, 0, 0, 0))},
        prefetch=1,
        name="ffn_grad",
    )[0]


def attn_grad_kernel(count, split, core_ref, *refs):
    out_ref = refs[-1]
    for i in range(count):
        la, lb, ra, rb = refs[4 * i : 4 * i + 4]
        got = pair_dot(la[0], lb[0], ra[...], rb[...])
        if split:
            got = got.reshape(8, QUAD, 16, PART)
            for tau in range(QUAD):
                out_ref[tau, :, i * 16 : (i + 1) * 16] = got[:, tau]
        else:
            out_ref[:, i * 16 : (i + 1) * 16] = got.reshape(32, 16, PART)


def attn_grad(core, pairs, split):
    half = pl.BlockSpec((1, TOK, PART), lambda i, core: (core[0], 0, 0))
    args = [a for left, right in pairs for a in (*left, *right)]
    specs = {4 * i + j: half for i in range(len(pairs)) for j in range(2)}
    return call(
        functools.partial(attn_grad_kernel, len(pairs), split),
        (core, *args),
        [sds(((QUAD, 8) if split else (32,)) + (16 * len(pairs), PART), BF16)],
        specs=specs,
        prefetch=1,
        name="attn_grad",
    )[0]


def swap_narrow(values):
    return lax.ppermute(values, "narrow", [(0, 1), (1, 0)])


def with_core(values):
    other = lax.ppermute(values, "wide", [(i, i ^ 1) for i in range(NW)])
    return values, other


def to_all(values):
    return lax.all_to_all(values, "wide", split_axis=0, concat_axis=0, tiled=True)


SAME_CORE = [[2 * k + c for k in range(NW // 2)] for c in range(2)]


def summed(values):
    return jnp.sum(to_same_core(values).astype(F32), axis=0).astype(BF16)


ALONG_X = [[hi * 8 + x * 2 + c for x in range(4)] for hi in range(8) for c in range(2)]
ACROSS_X = [[hi * 8 + x * 2 + c for hi in range(8)] for x in range(4) for c in range(2)]


def summed_along_x(values):
    return lax.psum_scatter(
        values, "wide", scatter_dimension=0, tiled=True, axis_index_groups=ALONG_X
    ).reshape(values.shape[1:])


def summed_across_x(values):
    moved = lax.all_to_all(
        values, "wide", split_axis=0, concat_axis=0, tiled=True, axis_index_groups=ACROSS_X
    )
    return jnp.sum(moved.astype(F32), axis=0).astype(BF16)


def to_same_core(values):
    return lax.all_to_all(
        values, "wide", split_axis=0, concat_axis=0, tiled=True, axis_index_groups=SAME_CORE
    )


def after(values, *others):
    return lax.optimization_barrier((values, others))[0]


def same_core_gather(rows):
    got = lax.all_gather(rows, "wide", axis=0, tiled=True, axis_index_groups=SAME_CORE)
    return got.reshape(NW // 2, rows.shape[0], PART)


def moved_rows(rows):
    return to_all(rows.reshape(NW, 8, -1)).reshape(ROWS, -1)


def on_device(
    x_first,
    x_second,
    grad_first,
    grad_second,
    sort_target,
    owner,
    master,
    moment_first,
    moment_second,
    gains,
    gain_first,
    gain_second,
):
    me = lax.axis_index("wide").astype(I32)
    half = lax.axis_index("narrow").astype(I32).reshape(1)
    core = (me & 1).reshape(1)

    tiles, parity = tile_rows()
    tile_of_row = np.concatenate([tiles, tiles + 88])
    code = owner[tile_of_row] * 2 + np.concatenate([parity, parity])
    code_col = code.reshape(-1, 1)
    code_row = code.reshape(1, -1)
    is_ffn = (np.arange(176) % 88 >= 24)[None, :]
    slots = me * CAP + jnp.arange(CAP, dtype=I32)
    kind = jnp.any((owner[None, :] == slots[:, None]) & is_ffn, axis=1).astype(I32)
    mine = lax.dynamic_slice_in_dim(sort_target, me * TOK, TOK, axis=2)
    ranks = jnp.sum((mine[:, :, None, :] < mine[:, :, :, None]).astype(I32), axis=3)
    rank_rows = [ranks[l] for l in range(LAYERS)]
    rank_cols = [ranks[l].T for l in range(LAYERS)]
    rnd, group = me >> 5, me & 7
    by_source = lax.dynamic_slice_in_dim(sort_target, rnd, 1, axis=1).reshape(LAYERS, NW, 1, TOK)
    blocks = jnp.concatenate([group * 8 + jnp.arange(8, dtype=I32), ((group * 8 - 1) & 63).reshape(1)])
    inside = (by_source >> 7) == blocks[None, None, :, None]
    low = jnp.min(jnp.where(inside, by_source & 127, TOK), axis=3)
    high = jnp.max(jnp.where(inside, by_source & 127, -1), axis=3)
    base = TOK * np.arange(8, dtype=np.int32)
    b = np.arange(8)[None, None, :]
    low9, high9 = low[:, :, 8:] - SPAN, high[:, :, 8:] - SPAN
    columns = (
        low[:, :, :8] + base,
        high[:, :, :8] + base,
        jnp.where(b == 0, low9, jnp.where(b == 2, high9, -1)),
        jnp.where(b == 1, low9, jnp.where(b == 3, high9, -1)),
    )
    place_rows = jnp.stack([c.reshape(LAYERS, ROWS) for c in columns], 1)
    place_cols = jnp.transpose(place_rows, (0, 2, 1))

    moved = to_all(route_out(kind, master))
    first_rows, early_rows, late_rows = pick(code_col, moved)
    first_w = with_core(to_same_core(first_rows))
    early_own = same_core_gather(early_rows)
    late_own = same_core_gather(late_rows)

    def rows_at(w, *indices):
        return tuple(tuple((a, index) for a in w) for index in indices)

    flat_gains = gains.reshape(LAYERS * 2, PART)
    x_two, gain_rows = inner(
        half, [(x_second, swap_narrow(x_second)), (flat_gains, swap_narrow(flat_gains))], "inner_a"
    )
    x_one, g_one, g_two = inner(
        half, [(a, swap_narrow(a)) for a in (x_first, grad_first, grad_second)], "inner_b"
    )
    x_two = after(x_two, x_one, g_one, g_two)
    gain = [[gain_rows[2 * l + i].reshape(1, D) for i in range(2)] for l in range(LAYERS)]

    saved = []
    pending = None
    w_qk, w_value = rows_at(first_w, 0, 1)
    for l in range(LAYERS):
        x_two, hn, send = project(core, x_two, pending, gain[l][0], w_qk, w_value, rank_rows[l])
        rows, send = attend(moved_rows(send), place_rows[l], place_cols[l])
        if l == 0:
            early_w = with_core(after(early_own, send))
            w_out, next_out, next_qk, next_value = rows_at(early_w, 8, 9, 10, 11)
            w_ffn = [a.reshape(8, QUAD, EARLY_ROWS, PART) for a in early_w]
        else:
            late_w = with_core(after(late_own, send))
            w_ffn = [a.reshape(8, QUAD, FFN_ROWS, PART) for a in late_w]
        own, send, o, share, merged = merge(core, moved_rows(send), rank_cols[l], w_out)
        x_one, hf, pre, act, own_f, send_f = ffn(
            core, x_one, own, swap_narrow(send), gain[l][1], w_ffn
        )
        pending = (own_f, swap_narrow(send_f))
        saved.append(
            (x_two, x_one, hn, rows, o, share, merged, hf, pre, act, w_qk, w_value, w_out, w_ffn)
        )
        w_qk, w_value, w_out = next_qk, next_value, next_out
    y_two = x_two + (pending[0] + pending[1].astype(F32))
    y_first, y_second = outer(half, (x_one, y_two), "outer_y")

    pending = None
    reduced = [None] * LAYERS
    dgains = [[None, None], [None, None]]
    for l in reversed(range(LAYERS)):
        x_in, y_mid, hn, rows, o, share, merged, hf, pre, act, w_qk, w_value, w_out, w_ffn = saved[l]
        g_two, back, da, own, send, dgain = ffn_back(core, g_two, pending, pre, w_ffn)
        if l == 0:
            dgains[1][0] = dgain
        other = swap_narrow(send)
        ffn_part = ffn_grad(core, with_core(hf), with_core(back), with_core(da), with_core(act))
        other = after(other, ffn_part)
        ffn_part = summed_along_x(ffn_part)
        if l == 0:
            other = after(other, ffn_rows)
        g_one, back, send, dgains[l][1] = merge_back(
            core, g_one, own, other, y_mid, gain[l][1], w_out, o, share, rank_rows[l]
        )
        send = attend_back(moved_rows(send), rows, place_rows[l], place_cols[l])
        arrived = moved_rows(send)
        own, send, dq, dv = project_back(core, arrived, rank_cols[l], w_qk, w_value)
        other = swap_narrow(send)
        hn2 = with_core(hn)
        pairs = [(with_core(back), with_core(merged)), (hn2, with_core(dq)), (hn2, with_core(dv))]
        attn_part = attn_grad(core, pairs, l > 0)
        if l > 0:
            other = after(other, attn_part)
            ffn_rows = summed_across_x(after(ffn_part, send))
            attn_part = summed_along_x(attn_part)
            attn_before = attn_part
        else:
            both = jnp.concatenate([after(ffn_part, arrived), after(attn_before, arrived)], 1)
            both = summed_across_x(both)
            attn_rows = summed(attn_part)
        pending = (own, other, x_in, gain[l][0])
    reduced = (both[:FFN_ROWS], attn_rows, ffn_rows, both[FFN_ROWS:])
    g_two, dgains[0][0] = last(g_two, *pending)
    dx_first, dx_second = outer(half, (g_one, g_two), "outer_dx")

    back_rows = to_all(
        route_back(
            code_row,
            jnp.concatenate(reduced, 0),
            jnp.concatenate([d for pair in dgains for d in pair], 0),
        )
    )
    slot_grad, slot_first, slot_second, slot_new = slots_update(
        kind, back_rows, master, moment_first, moment_second
    )
    gain_sum = jnp.sum(back_rows[:, CAP * 2 * PART :].astype(F32), axis=0).reshape(2 * LAYERS, D)
    gain_grad = outer(half, (gain_sum,), "outer_gain")[0].reshape(LAYERS, 2, PART)
    gain_first_new, gain_second_new, gain_new = adam(
        gain_grad, gain_first, gain_second, gains, RATE_GAIN
    )
    return (
        y_first,
        y_second,
        dx_first,
        dx_second,
        slot_grad,
        slot_first,
        slot_second,
        slot_new,
        gain_grad,
        gain_first_new,
        gain_second_new,
        gain_new,
    )


def solution(mesh):
    rows = P("wide", "narrow")
    tiles = P("wide", None, "narrow")
    gains = P(None, None, "narrow")
    return jax.shard_map(
        on_device,
        mesh=mesh,
        in_specs=(rows,) * 4 + (P(), P()) + (tiles,) * 3 + (gains,) * 3,
        out_specs=(rows,) * 4 + (tiles,) * 4 + (gains,) * 4,
        check_vma=False,
    )
```

```python
import functools

import jax
import jax.numpy as jnp
import numpy as np
from jax import lax
from jax.experimental import pallas as pl
from jax.experimental.pallas import tpu as pltpu
from jax.sharding import PartitionSpec as P

D = 1024
PART = 512
DH = 128
HN = 4
SPAN = 64
TR = 128
CAP = 5
TILES = 176
TOK = 128
NW = 64
LAYERS = 2
ROUNDS = 2
STEP = 5
GROUPS = 8
QV_LANES = 5 * DH
O_LANES = 3 * DH
ROWS = NW * 8
PACK = 16
QUAD = 4
UP, DOWN = 0, 1
LAYER_ROWS = 176
ATTN_ROWS = 48
FFN_ROWS = 128
EARLY_ROWS = 192

MASK_FILL = -1000000000.0
NORM_EPS = 1e-05
BETA_ONE = 0.5
BETA_TWO = 0.5
RATE_WEIGHT = 0.05
RATE_GAIN = 0.2
DECAY = 0.01
EPSILON = 1e-08

F32 = jnp.float32
BF16 = jnp.bfloat16
I32 = jnp.int32
VMEM_BYTES = 20 * 1024 * 1024


def feature_of(p):
    c0 = p >> 9
    z = (p >> 7) & 3
    tau = (p >> 5) & 3
    y = (p >> 4) & 1
    t = (p >> 1) & 7
    e = p & 1
    return t * 128 + tau * 32 + c0 * 16 + (y * 4 + z) * 2 + e


def iota(shape, dim):
    return lax.broadcasted_iota(I32, shape, dim)


def hot(mask):
    return jnp.where(mask, 1.0, 0.0).astype(BF16)


def dot(a, b, ca, cb):
    return lax.dot_general(a, b, (((ca,), (cb,)), ((), ())), preferred_element_type=F32)


def in_hbm(array):
    return pltpu.with_memory_space_constraint(array, pltpu.MemorySpace.HBM)


def call(
    kernel, args, outs, grid=(1,), specs=None, out_specs=None, scratch=(), prefetch=0, in_place=(), name=None
):
    specs = specs or {}
    out_specs = out_specs or {}
    def whole(shape):
        zeros = (0,) * len(shape)
        return pl.BlockSpec(shape, lambda *_: zeros)
    in_list = [specs.get(i, whole(a.shape)) for i, a in enumerate(args[prefetch:])]
    args = [in_hbm(a) if i - prefetch in in_place else a for i, a in enumerate(args)]
    out_list = [out_specs.get(i, whole(o.shape)) for i, o in enumerate(outs)]
    return pl.pallas_call(
        kernel,
        out_shape=outs,
        grid_spec=pltpu.PrefetchScalarGridSpec(
            num_scalar_prefetch=prefetch,
            grid=grid,
            in_specs=in_list,
            out_specs=out_list,
            scratch_shapes=list(scratch),
        ),
        compiler_params=pltpu.CompilerParams(vmem_limit_bytes=VMEM_BYTES),
        name=name,
    )(*args)


def sds(shape, dtype):
    return jax.ShapeDtypeStruct(shape, dtype)


def kept(shape, dtype):
    return pltpu.MemorySpace.HBM(shape, dtype)


def norm_parts(values):
    mean = jnp.mean(values, axis=-1, keepdims=True)
    var = jnp.mean(values * values, axis=-1, keepdims=True) - mean * mean
    rstd = lax.rsqrt(var + NORM_EPS)
    return (values - mean) * rstd, rstd


def norm_back(upstream, gain, xhat, rstd):
    gh = upstream * gain
    m1 = jnp.mean(gh, axis=-1, keepdims=True)
    m2 = jnp.mean(gh * xhat, axis=-1, keepdims=True)
    return rstd * (gh - m1 - xhat * m2), jnp.sum(upstream * xhat, axis=0, keepdims=True)


def flat(ref):
    return ref[...].reshape(PART, PART)


def halves(core, first, second):
    mine = core == 0
    return jnp.where(mine, first, second), jnp.where(mine, second, first)


class Weight:
    def __init__(self, index, *arrays):
        self.index = index
        self.arrays = arrays

    def parts(self):
        index = self.index
        if len(self.arrays) == 2:
            return [
                (a, pl.BlockSpec((8, 16, PART), lambda *_, z=z: (z, index, 0)))
                for a in self.arrays
                for z in range(4)
            ]
        return [
            (self.arrays[0], pl.BlockSpec((1, QUAD, 2, 32, PART), lambda *_, z=z: (z, 0, 0, index, 0)))
            for z in range(4)
        ]


def rows_of(refs):
    return jnp.concatenate([r[...].reshape(-1, PART) for r in refs], 0)


def weight_halves(core, refs):
    if len(refs) == 4:
        return [
            jnp.concatenate([r[0, :, c0].reshape(-1, PART) for r in refs], 0) for c0 in range(2)
        ]
    return rows_of(refs[:4]), rows_of(refs[4:])


def into(core, full, refs):
    first, second = full[:, :PART], full[:, PART:]
    if len(refs) == 8:
        first, second = halves(core, first, second)
    w = weight_halves(core, refs)
    return dot(first.astype(BF16), w[0], 1, 0) + dot(second.astype(BF16), w[1], 1, 0)


def out_of(core, part, refs):
    w = weight_halves(core, refs)
    pair = dot(part, w[0], 1, 1), dot(part, w[1], 1, 1)
    return pair if len(refs) == 4 else halves(core, *pair)


def unpacked(args, prefetch):
    out, specs = [], {}
    for a in args:
        if isinstance(a, Weight):
            for array, spec in a.parts():
                specs[len(out) - prefetch] = spec
                out.append(array)
        else:
            out.append(a)
    return out, specs


def wanted(shape, dim):
    m = iota(shape, dim)
    g16 = (m >> 3) * 16
    b = m & 7
    before = (g16 - 2) & 127
    lent = before + (b >> 1)
    return (
        g16 + 2 * b,
        g16 + 2 * b + 1,
        jnp.where((b == 0) | (b == 2), lent, -1),
        jnp.where((b == 1) | (b == 3), lent, -1),
    )


def send_hots(rank_row, count=4):
    return hot(jnp.concatenate(wanted((NW, 1), 0)[:count], 0) == rank_row)


def return_hots(rank_col, count=4):
    return hot(rank_col == jnp.concatenate(wanted((1, NW), 1)[:count], 1))


def spread(col, lanes):
    hi, mid, lo = pieces(col)
    k = lanes & 7
    return jnp.where(k == 0, hi, jnp.where(k == 1, mid, jnp.where(k == 2, lo, 0.0)))


def pieces(col):
    hi = col.astype(BF16).astype(F32)
    rest = col - hi
    mid = rest.astype(BF16).astype(F32)
    return hi, mid, rest - mid


def either(lanes, even, odd):
    return jnp.where(lanes < 8, even, jnp.where(lanes < 16, odd, 0.0))


def slot_kinds(owner_ref, me):
    lane = iota((1, TILES), 1)
    ffn = jnp.where(lane >= TILES // LAYERS, lane - TILES // LAYERS, lane) >= 24
    return [
        jnp.max(
            jnp.where((owner_ref[...] == me * CAP + s) & ffn, 1, 0), axis=1, keepdims=True
        )
        for s in range(CAP)
    ]


def row_of_slots(kinds):
    r = iota((1, TR), 1)
    attn = (((r >> 1) & 7) * 8 + (r >> 5) * 2 + ((r >> 4) & 1)) * PACK + (r & 1)
    low = r >> 2
    ffn = (((low >> 1) & 7) * 8 + (r & 3) * 2 + (low >> 4)) * PACK + (low & 1)
    return jnp.concatenate([jnp.where(k == 1, ffn, attn) + 2 * s for s, k in enumerate(kinds)], 1)


def slot_of_row(kinds):
    r = iota((1, NW * PACK), 1)
    d, m = r >> 4, r & (PACK - 1)
    s, e = m >> 1, m & 1
    tau = (d >> 1) & 3
    low = (d & 1) * 16 + (d >> 3) * 2 + e
    out = jnp.full((1, NW * PACK), -1, I32)
    for i, k in enumerate(kinds):
        out = jnp.where(s == i, i * TR + jnp.where(k == 1, low * 4 + tau, tau * 32 + low), out)
    return out


def route_out_kernel(me_ref, owner_ref, master_ref, out_ref):
    tiles = master_ref[...].reshape(CAP * TR, PART).astype(BF16)
    place = row_of_slots(slot_kinds(owner_ref, me_ref[0]))
    out_ref[...] = dot(hot(iota((NW * PACK, 1), 0) == place), tiles, 1, 0).astype(BF16)


def route_out(me, owner_row, master):
    return call(
        route_out_kernel,
        (me, owner_row, master),
        [kept((NW * PACK, PART), BF16)],
        prefetch=1,
        in_place=(1,),
        name="route_out",
    )[0]


def pick_kernel(code_ref, moved_ref, first_ref, early_ref, late_ref):
    picked = hot(code_ref[...] == iota((1, NW * PACK), 1))
    rows = dot(picked, moved_ref[...], 1, 0).astype(BF16)
    late_ref[...] = rows[LAYER_ROWS : LAYER_ROWS + FFN_ROWS]
    early_ref[: FFN_ROWS + 16] = rows[: FFN_ROWS + 16]
    early_ref[FFN_ROWS + 16 :] = rows[LAYER_ROWS + FFN_ROWS :]
    first_ref[...] = jnp.broadcast_to(rows[FFN_ROWS + 16 : LAYER_ROWS][None], first_ref.shape)


def pick(code_col, moved):
    return call(
        pick_kernel,
        (code_col, moved),
        [kept((32, 32, PART), BF16), kept((EARLY_ROWS, PART), BF16), kept((FFN_ROWS, PART), BF16)],
        name="pick",
    )


def route_back_kernel(code_ref, *refs):
    *parts, gain_a, gain_b, gain_c, out_ref = refs
    rows = jnp.concatenate([p[...] for p in parts], 0)
    place = iota((NW * PACK, 1), 0)
    out = dot(hot(place == code_ref[...]), rows, 1, 0)
    gains = jnp.concatenate(
        [
            half
            for g in (gain_a, gain_b, gain_c)
            for half in (g[:, :PART], g[:, PART:])
        ]
        + [jnp.zeros((2, PART), F32)],
        0,
    ).astype(BF16)
    spare = hot((place & (PACK - 1)) - 2 * CAP == iota((1, 8), 1))
    out_ref[...] = (out + dot(spare, gains, 1, 0)).astype(BF16)


def route_back(code_row, parts, gains):
    return call(
        route_back_kernel,
        (code_row, *parts, *gains),
        [kept((NW * PACK, PART), BF16)],
        name="route_back",
    )[0]


def adam(grad, first, second, weights, rate):
    first_new = BETA_ONE * first + (1.0 - BETA_ONE) * grad
    second_new = BETA_TWO * second + (1.0 - BETA_TWO) * grad * grad
    step = (
        first_new
        / (1.0 - BETA_ONE**STEP)
        / (jnp.sqrt(second_new / (1.0 - BETA_TWO**STEP)) + EPSILON)
    )
    return first_new, second_new, weights - rate * (step + DECAY * weights)


def slots_kernel(
    half_ref, me_ref, owner_ref, moved_ref, ready_ref, m_ref, a_ref, b_ref, gains_ref, ga_ref, gb_ref,
    grad_ref, first_ref, second_ref, new_ref, gg_ref, gf_ref, gs_ref, gn_ref, all_ref
):
    s = pl.program_id(0)

    @pl.when(s == 0)
    def _():
        placed = hot(iota((CAP * TR, 1), 0) == slot_of_row(slot_kinds(owner_ref, me_ref[0])))
        all_ref[...] = dot(placed, moved_ref[...], 1, 0).reshape(CAP, TR, PART)
        spare = hot((iota((1, NW * PACK), 1) & (PACK - 1)) - 2 * CAP == iota((8, 1), 0))
        sums = dot(spare, moved_ref[...], 1, 0)
        gains = [jnp.concatenate([sums[q : q + 1], sums[q + 1 : q + 2]], 1) for q in (4, 2, 0)]
        inner_sum = jnp.concatenate(gains + [ready_ref[...]], 0)
        back = hot(feature_of(iota((1, D), 1)) == iota((PART, 1), 0) + half_ref[0] * PART)
        parts = dot(jnp.concatenate(pieces(inner_sum), 0).astype(BF16), back, 1, 1)
        n = 2 * LAYERS
        total = parts[:n] + parts[n : 2 * n] + parts[2 * n :]
        for l in range(LAYERS):
            gain_grad = total[2 * l : 2 * l + 2]
            gg_ref[l] = gain_grad
            gf_ref[l], gs_ref[l], gn_ref[l] = adam(
                gain_grad, ga_ref[l], gb_ref[l], gains_ref[l], RATE_GAIN
            )

    grad = all_ref[s]
    grad_ref[0] = grad
    first_ref[0], second_ref[0], new_ref[0] = adam(grad, a_ref[0], b_ref[0], m_ref[0], RATE_WEIGHT)


def slots_update(half, me, owner_row, moved, ready, master, first, second, gains, gain_first, gain_second):
    tile = pl.BlockSpec((1, TR, PART), lambda s, *_: (s, 0, 0))
    return call(
        slots_kernel,
        (half, me, owner_row, moved, ready, master, first, second, gains, gain_first, gain_second),
        [sds((CAP, TR, PART), F32)] * 4 + [sds((LAYERS, 2, PART), F32)] * 4,
        grid=(CAP,),
        specs={3: tile, 4: tile, 5: tile},
        out_specs={i: tile for i in range(4)},
        scratch=[pltpu.VMEM((CAP, TR, PART), F32)],
        prefetch=2,
        in_place=(3, 4, 5),
        name="slots_update",
    )


def turned(col):
    same = iota((TOK, TOK), 0) == iota((TOK, TOK), 1)
    return jnp.sum(jnp.where(same, col, 0), axis=0, keepdims=True)


def plan_kernel(group_ref, mine_ref, source_ref, *outs):
    same = iota((TOK, TOK), 0) == iota((TOK, TOK), 1)
    b = iota((ROWS, 1), 0) & 7
    block = group_ref[0] * 8 + b
    before = (group_ref[0] * 8 - 1) & 63
    lanes = iota((ROWS, TOK), 1)
    for l in range(LAYERS):
        rank_row, rank_col, place_row, place_col = outs[4 * l : 4 * l + 4]
        cols = jnp.zeros((TOK, TOK), I32)
        for r in range(ROUNDS):
            row = mine_ref[l * ROUNDS + r : l * ROUNDS + r + 1, :]
            col = jnp.sum(jnp.where(same, row, 0), axis=1, keepdims=True)
            rank_row[r : r + 1, :] = jnp.sum(jnp.where(col < row, 1, 0), axis=0, keepdims=True)
            rank = jnp.sum(jnp.where(row < col, 1, 0), axis=1, keepdims=True)
            cols = jnp.where(lanes[:TOK] == r, rank, cols)
        rank_col[...] = cols
        source = source_ref[l]
        target = jnp.broadcast_to(source[:, None, :], (NW, 8, TOK)).reshape(ROWS, TOK)
        place = target & (TOK - 1)
        got = []
        for want in (block, before):
            inside = (target >> 7) == want
            got.append(jnp.min(jnp.where(inside, place, TOK), axis=1, keepdims=True))
            got.append(jnp.max(jnp.where(inside, place, -1), axis=1, keepdims=True))
        low, high, low_lent, high_lent = got
        columns = (
            low + TOK * b,
            high + TOK * b,
            jnp.where(b == 0, low_lent - SPAN, jnp.where(b == 2, high_lent - SPAN, -1)),
            jnp.where(b == 1, low_lent - SPAN, jnp.where(b == 3, high_lent - SPAN, -1)),
        )
        cols = jnp.zeros((ROWS, TOK), I32)
        for j, column in enumerate(columns):
            cols = jnp.where(lanes == j, column, cols)
            for q in range(4):
                at = slice(q * TOK, (q + 1) * TOK)
                place_row[j : j + 1, at] = turned(column[at])
        place_col[...] = cols


def plan(group, mine, source):
    layer = [kept((ROUNDS, TOK), I32), kept((TOK, TOK), I32), kept((4, ROWS), I32), kept((ROWS, TOK), I32)]
    return call(plan_kernel, (group, mine, source), layer * LAYERS, prefetch=1, name="plan")


def inner_kernel(half_ref, *refs):
    count = len(refs) // 3
    n = half_ref[0]
    feature = feature_of(iota((1, D), 1))
    mine = hot(feature == iota((PART, 1), 0) + n * PART)
    theirs = hot(feature == iota((PART, 1), 0) + (1 - n) * PART)
    for i in range(count):
        own, other, out = refs[2 * i], refs[2 * i + 1], refs[2 * count + i]
        if own.dtype == BF16:
            out[...] = dot(own[...], mine, 1, 0) + dot(other[...], theirs, 1, 0)
        else:
            total = jnp.zeros(out.shape, F32)
            for a, b in zip(pieces(own[...]), pieces(other[...])):
                total = total + (dot(a.astype(BF16), mine, 1, 0) + dot(b.astype(BF16), theirs, 1, 0))
            out[...] = total


def inner(half, pairs, name):
    flat = [a for pair in pairs for a in pair]
    outs = [sds((own.shape[0], D), F32) for own, _ in pairs]
    return call(inner_kernel, (half, *flat), outs, prefetch=1, name=name)


def outer_kernel(count, half_ref, *refs):
    n = half_ref[0]
    feature = feature_of(iota((1, D), 1))
    back = hot(feature == iota((PART, 1), 0) + n * PART)
    for i in range(count):
        total = jnp.zeros(refs[count + i].shape, F32)
        for part in pieces(refs[i][...]):
            total = total + dot(part.astype(BF16), back, 1, 1)
        refs[count + i][...] = total


def outer(half, arrays, name):
    outs = [sds((a.shape[0], PART), F32) for a in arrays]
    return call(
        functools.partial(outer_kernel, len(arrays)), (half, *arrays), outs, prefetch=1, name=name
    )


def project_kernel(pending, count, core_ref, *refs):
    if pending:
        x_ref, own_ref, other_ref, *rest = refs
        x = x_ref[...] + (own_ref[...] + other_ref[...].astype(F32))
    else:
        x_ref, *rest = refs
        x = x_ref[...]
    gain_ref, *rest = rest
    q_refs, v_refs = rest[:count], rest[count : 2 * count]
    rank_ref, x_out, hn_out, send_out = rest[2 * count :]
    core = core_ref[0]
    x_out[...] = x
    xhat, _ = norm_parts(x)
    hn = xhat * gain_ref[...]
    hn_out[0] = hn[:, :PART].astype(BF16)
    hn_out[1] = hn[:, PART:].astype(BF16)
    q = into(core, hn, q_refs).astype(BF16)
    v = into(core, hn, v_refs).astype(BF16)
    qv = jnp.concatenate([m[:, h * DH : (h + 1) * DH] for h in range(HN) for m in (q, v)], 1)
    for r in range(ROUNDS):
        moved = dot(send_hots(rank_ref[r : r + 1, :]), qv, 1, 0)
        even, odd = moved[:NW].astype(BF16), moved[NW : 2 * NW].astype(BF16)
        lent_q, lent_v = moved[2 * NW : 3 * NW], moved[3 * NW :]
        for h in range(HN):
            rows = slice((r * HN + h) * NW, (r * HN + h + 1) * NW)
            at = h * 2 * DH
            send_out[rows, : 2 * DH] = even[:, at : at + 2 * DH]
            send_out[rows, 2 * DH : 4 * DH] = odd[:, at : at + 2 * DH]
            send_out[rows, 4 * DH :] = (
                lent_q[:, at : at + DH] + lent_v[:, at + DH : at + 2 * DH]
            ).astype(BF16)


def project(core, x, pending, gain, wq, wv, rank_row):
    args, specs = unpacked([core, x, *(pending or ()), gain, wq, wv, rank_row], 1)
    return call(
        functools.partial(project_kernel, pending is not None, len(wq.parts())),
        args,
        [kept((TOK, D), F32), kept((2, TOK, PART), BF16), kept((ROWS, QV_LANES), BF16)],
        specs=specs,
        in_place=(0, *(tuple(specs) if len(wq.parts()) == 4 else ())),
        prefetch=1,
        name="project",
    )


def scores_of(rows):
    keys = rows[:, :DH].astype(F32)
    inv = lax.rsqrt(jnp.sum(keys * keys, axis=-1, keepdims=True) + 1e-06)
    unit = (keys * inv).astype(BF16)
    scores = jnp.concatenate(
        [
            dot(
                rows[(c + 1) * SPAN : (c + 2) * SPAN, :DH],
                unit[c * SPAN : (c + 2) * SPAN],
                1,
                1,
            )
            for c in range(16)
        ],
        0,
    )
    own = iota((1024, TOK), 1) == (iota((1024, TOK), 0) & (SPAN - 1)) + SPAN
    scores = jnp.where(own, MASK_FILL, scores)
    peak = jnp.max(scores, axis=-1, keepdims=True)
    total = peak + jnp.log(jnp.sum(jnp.exp(scores - peak), axis=-1, keepdims=True))
    exact = jnp.exp(scores - total)
    return keys, inv, unit, own, total, exact


def arrive(place_row_ref, j, rows):
    count = 1024 if j < 2 else SPAN
    return dot(hot(iota((count, 1), 0) == place_row_ref[j : j + 1, :]), rows, 1, 0)


def leave(place_col_ref, j, rows):
    return dot(hot(place_col_ref[:, j : j + 1] == iota((1, rows.shape[0]), 1)), rows, 1, 0)


def attend_kernel(moved_ref, place_row_ref, place_col_ref, sorted_out, send_out):
    q_lent = arrive(place_row_ref, 2, moved_ref[:, 4 * DH :])
    v_lent = arrive(place_row_ref, 3, moved_ref[:, 4 * DH :])
    main = arrive(place_row_ref, 0, moved_ref[:, : 2 * DH]) + arrive(
        place_row_ref, 1, moved_ref[:, 2 * DH : 4 * DH]
    )
    rows = jnp.concatenate([jnp.concatenate([q_lent, v_lent], 1), main], 0).astype(BF16)
    sorted_out[...] = rows
    _, _, _, _, total, exact = scores_of(rows)
    probs = exact.astype(BF16)
    outs = jnp.concatenate(
        [
            dot(probs[c * SPAN : (c + 1) * SPAN], rows[c * SPAN : (c + 2) * SPAN, DH:], 1, 0)
            for c in range(16)
        ],
        0,
    )
    aux = spread(total, iota((1024, TOK), 1))
    both = jnp.concatenate([outs, aux], 1).astype(BF16)
    even = leave(place_col_ref, 0, both)
    odd = leave(place_col_ref, 1, both)
    send_out[:, :DH] = even[:, :DH].astype(BF16)
    send_out[:, DH : 2 * DH] = odd[:, :DH].astype(BF16)
    lanes = iota((ROWS, TOK), 1)
    send_out[:, 2 * DH :] = either(lanes, even[:, DH:], odd[:, DH:]).astype(BF16)


def attend(moved, place_row, place_col):
    return call(
        attend_kernel,
        (moved, place_row, place_col),
        [kept((1088, 2 * DH), BF16), kept((ROWS, O_LANES), BF16)],
        in_place=(1, 2),
        name="attend",
    )


def by_head(ref, r, cols):
    return jnp.concatenate(
        [ref[(r * HN + h) * NW : (r * HN + h + 1) * NW, cols] for h in range(HN)], 1
    )


def merge_kernel(count, core_ref, moved_ref, rank_col_ref, *refs):
    w_refs, refs = refs[:count], refs[count:]
    part_out, send_out, o_out, share_out, merged_out = refs
    lanes = iota((TOK, TOK), 1)
    outs, logs = [], []
    for r in range(ROUNDS):
        hots = return_hots(rank_col_ref[:, r : r + 1], 2)
        aux = by_head(moved_ref, r, slice(2 * DH, 3 * DH))
        even = dot(
            hots[:, :NW], jnp.concatenate([by_head(moved_ref, r, slice(0, DH)), aux], 1), 1, 0
        )
        odd = dot(
            hots[:, NW:], jnp.concatenate([by_head(moved_ref, r, slice(DH, 2 * DH)), aux], 1), 1, 0
        )
        outs.append(even[:, :PART] + odd[:, :PART])
        o_out[r] = outs[r].astype(BF16)
        logs.append(
            [
                jnp.sum(
                    either(
                        lanes,
                        even[:, PART + h * DH : PART + (h + 1) * DH],
                        odd[:, PART + h * DH : PART + (h + 1) * DH],
                    ),
                    axis=-1,
                    keepdims=True,
                )
                for h in range(HN)
            ]
        )
    merged = []
    share_all = jnp.zeros((TOK, TOK), F32)
    for h in range(HN):
        top = jnp.maximum(logs[0][h], logs[1][h])
        e0 = jnp.exp(logs[0][h] - top)
        e1 = jnp.exp(logs[1][h] - top)
        total = e0 + e1
        cols = slice(h * DH, (h + 1) * DH)
        s0, s1 = e0 / total, e1 / total
        merged.append(s0 * outs[0][:, cols] + s1 * outs[1][:, cols])
        share_all = jnp.where(lanes == h, s0, jnp.where(lanes == HN + h, s1, share_all))
    share_out[...] = share_all
    merged = jnp.concatenate(merged, 1).astype(BF16)
    merged_out[...] = merged
    put_halves(out_of(core_ref[0], merged, w_refs), part_out, send_out)


def put_halves(pair, part_out, send_out):
    for i in range(2):
        cols = slice(i * PART, (i + 1) * PART)
        part_out[:, cols] = pair[i]
        send_out[:, cols] = pair[i].astype(BF16)


def merge(core, moved, rank_col, wo):
    args, specs = unpacked([core, moved, rank_col, wo], 1)
    return call(
        functools.partial(merge_kernel, len(wo.parts())),
        args,
        [
            sds((TOK, D), F32),
            kept((TOK, D), BF16),
            kept((ROUNDS, TOK, PART), BF16),
            kept((TOK, TOK), F32),
            kept((TOK, PART), BF16),
        ],
        specs=specs,
        in_place=(1, *specs),
        prefetch=1,
        name="merge",
    )


def ffn_specs(at, index):
    return {
        at + z: pl.BlockSpec((1, 1, 2, FFN_ROWS, PART), lambda c, z=z: (z, c, 0, index, 0))
        for z in range(4)
    }


def ffn_half(refs, c0):
    return jnp.concatenate([r[0, 0, c0] for r in refs], 0)


def ffn_kernel(
    x_ref, own_ref, other_ref, gain_ref, *refs
):
    up_ref, down_ref = refs[:4], refs[4:8]
    y_out, hf_out, pre_out, act_out, part_out, send_out, hf_ref, acc_ref = refs[8:]
    c = pl.program_id(0)

    @pl.when(c == 0)
    def _():
        y = x_ref[...] + (own_ref[...] + other_ref[...].astype(F32))
        y_out[...] = y
        xhat, _ = norm_parts(y)
        hf = (xhat * gain_ref[...]).astype(BF16)
        for c0 in range(2):
            hf_ref[c0] = hf[:, c0 * PART : (c0 + 1) * PART]
        hf_out[...] = hf_ref[...]
        acc_ref[...] = jnp.zeros_like(acc_ref)

    pre = dot(hf_ref[0], ffn_half(up_ref, 0), 1, 0) + dot(hf_ref[1], ffn_half(up_ref, 1), 1, 0)
    pre_out[...] = pre
    act = (0.5 * pre * (1.0 + lax.erf(pre * (0.5**0.5)))).astype(BF16)
    act_out[...] = act
    for c0 in range(2):
        acc_ref[c0] += dot(act, ffn_half(down_ref, c0), 1, 1)

    @pl.when(c == QUAD - 1)
    def _():
        put_halves((acc_ref[0], acc_ref[1]), part_out, send_out)


def ffn(x, own, other, gain, w):
    cols = pl.BlockSpec((TOK, PART), lambda c: (0, c))
    return call(
        ffn_kernel,
        (x, own, other, gain, *[w] * 8),
        [
            kept((TOK, D), F32),
            kept((2, TOK, PART), BF16),
            kept((TOK, QUAD * PART), F32),
            kept((TOK, QUAD * PART), BF16),
            sds((TOK, D), F32),
            kept((TOK, D), BF16),
        ],
        grid=(QUAD,),
        specs={**ffn_specs(4, UP), **ffn_specs(8, DOWN)},
        in_place=(0, *range(4, 12)),
        out_specs={2: cols, 3: cols},
        scratch=[pltpu.VMEM((2, TOK, PART), BF16), pltpu.VMEM((2, TOK, PART), F32)],
        name="ffn",
    )


def put_pieces(out_ref, at, row, rows, grad):
    for piece in range(32):
        z, tau, y = piece >> 3, (piece >> 1) & 3, piece & 1
        got = grad[piece * 16 : (piece + 1) * 16]
        if rows == 16:
            out_ref[2 * tau + at, z * 2 + y, row : row + 16] = got
        else:
            out_ref[at, z * 2 + y, row + tau * 16 : row + (tau + 1) * 16] = got


def ffn_back_kernel(pending, *refs):
    if pending:
        g_ref, own_ref, other_ref, x_ref, gain_ref, *rest = refs
    else:
        g_ref, *rest = refs
    pre_ref, hf_ref, act_ref, *rest = rest
    up_ref, down_ref, rest = rest[:4], rest[4:8], rest[8:]
    g_out, part_out, send_out, dgain_out, grad_out, back_ref, acc_ref = rest
    c = pl.program_id(0)

    @pl.when(c == 0)
    def _():
        g = g_ref[...]
        if pending:
            xhat, rstd = norm_parts(x_ref[...])
            add, dgain = norm_back(
                own_ref[...] + other_ref[...].astype(F32), gain_ref[...], xhat, rstd
            )
            g = g + add
            dgain_out[...] = dgain
        else:
            dgain_out[...] = jnp.zeros_like(dgain_out)
        g_out[...] = g
        back = g.astype(BF16)
        for c0 in range(2):
            back_ref[c0] = back[:, c0 * PART : (c0 + 1) * PART]
        acc_ref[...] = jnp.zeros_like(acc_ref)

    d_act = dot(back_ref[0], ffn_half(down_ref, 0), 1, 0) + dot(
        back_ref[1], ffn_half(down_ref, 1), 1, 0
    )
    pre = pre_ref[...]
    slope = 0.5 * (1.0 + lax.erf(pre * (0.5**0.5))) + pre * (
        jnp.exp(-0.5 * pre * pre) * np.float32(1.0 / np.sqrt(2.0 * np.pi))
    )
    d_pre = (d_act * slope).astype(BF16)
    for c0 in range(2):
        acc_ref[c0] += dot(d_pre, ffn_half(up_ref, c0), 1, 1)
        put_pieces(grad_out, c0, 0, 64, dot(hf_ref[c0], d_pre, 0, 0).astype(BF16))
        put_pieces(grad_out, c0, 64, 64, dot(back_ref[c0], act_ref[...], 0, 0).astype(BF16))

    @pl.when(c == QUAD - 1)
    def _():
        put_halves((acc_ref[0], acc_ref[1]), part_out, send_out)


def ffn_back(g, pending, pre, hf, act, w):
    cols = pl.BlockSpec((TOK, PART), lambda c: (0, c))
    args = [g, *(pending or ()), pre, hf, act, *[w] * 8]
    at = len(args) - 11
    specs = {at: cols, at + 2: cols, **ffn_specs(at + 3, UP), **ffn_specs(at + 7, DOWN)}
    in_place = (0, *((3,) if pending else ()), *range(at, at + 11))
    return call(
        functools.partial(ffn_back_kernel, pending is not None),
        args,
        [
            kept((TOK, D), F32),
            sds((TOK, D), F32),
            kept((TOK, D), BF16),
            sds((1, D), F32),
            kept((2 * QUAD, 8, FFN_ROWS, PART), BF16),
        ],
        grid=(QUAD,),
        specs=specs,
        in_place=in_place,
        out_specs={4: pl.BlockSpec((2, 8, FFN_ROWS, PART), lambda c: (c, 0, 0, 0))},
        scratch=[pltpu.VMEM((2, TOK, PART), BF16), pltpu.VMEM((2, TOK, PART), F32)],
        name="ffn_back",
    )


def merge_back_kernel(count, core_ref, g_ref, own_ref, other_ref, y_ref, gain_ref, *refs):
    w_refs, refs = refs[:count], refs[count:]
    o_ref, share_ref, rank_row_ref, g_out, back_out, send_out, dgain_out = refs
    xhat, rstd = norm_parts(y_ref[...])
    add, dgain = norm_back(own_ref[...] + other_ref[...].astype(F32), gain_ref[...], xhat, rstd)
    dgain_out[...] = dgain
    g = g_ref[...] + add
    g_out[...] = g
    back_out[0] = g[:, :PART].astype(BF16)
    back_out[1] = g[:, PART:].astype(BF16)
    dout = into(core_ref[0], g, w_refs)
    share = share_ref[...]
    o0 = o_ref[0].astype(F32)
    o1 = o_ref[1].astype(F32)
    lanes = iota((TOK, TOK), 1)
    parts = [[], []]
    logs = [[], []]
    for h in range(HN):
        cols = slice(h * DH, (h + 1) * DH)
        s0 = share[:, h : h + 1]
        s1 = share[:, HN + h : HN + h + 1]
        dh = dout[:, cols]
        t0 = jnp.sum(dh * o0[:, cols], axis=-1, keepdims=True)
        t1 = jnp.sum(dh * o1[:, cols], axis=-1, keepdims=True)
        mean = s0 * t0 + s1 * t1
        parts[0].append(s0 * dh)
        parts[1].append(s1 * dh)
        logs[0].append(spread(s0 * (t0 - mean), lanes))
        logs[1].append(spread(s1 * (t1 - mean), lanes))
    lanes = iota((NW, TOK), 1)
    for r in range(ROUNDS):
        moved = dot(
            send_hots(rank_row_ref[r : r + 1, :], 2),
            jnp.concatenate(parts[r] + logs[r], 1).astype(BF16),
            1,
            0,
        )
        even, odd = moved[:NW], moved[NW:]
        for h in range(HN):
            rows = slice((r * HN + h) * NW, (r * HN + h + 1) * NW)
            cols = slice(h * DH, (h + 1) * DH)
            aux = slice(PART + h * DH, PART + (h + 1) * DH)
            send_out[rows, :DH] = even[:, cols].astype(BF16)
            send_out[rows, DH : 2 * DH] = odd[:, cols].astype(BF16)
            send_out[rows, 2 * DH :] = either(lanes, even[:, aux], odd[:, aux]).astype(BF16)


def merge_back(core, g, own, other, y, gain, wo, o, share, rank_row):
    args, specs = unpacked([core, g, own, other, y, gain, wo, o, share, rank_row], 1)
    return call(
        functools.partial(merge_back_kernel, len(wo.parts())),
        args,
        [
            kept((TOK, D), F32),
            kept((2, TOK, PART), BF16),
            kept((ROWS, O_LANES), BF16),
            sds((1, D), F32),
        ],
        specs=specs,
        in_place=(0, 3, *specs, *range(len(args) - 4, len(args) - 1)),
        prefetch=1,
        name="merge_back",
    )


def attend_back_kernel(moved_ref, sorted_ref, place_row_ref, place_col_ref, gain_ref, send_out):
    lanes = iota((ROWS, TOK), 1)
    aux = moved_ref[:, 2 * DH :].astype(F32)
    got = jnp.zeros((1024, 2 * DH), F32)
    for j in range(2):
        here = jnp.where(lanes >> 3 == j, aux, 0.0).astype(BF16)
        pair = jnp.concatenate([moved_ref[:, j * DH : (j + 1) * DH], here], 1)
        got = got + arrive(place_row_ref, j, pair)
    d_out = got[:, :DH].astype(BF16)
    d_log = jnp.sum(got[:, DH:], axis=-1, keepdims=True)
    rows = sorted_ref[...]
    keys, inv, unit, own, _, exact = scores_of(rows)
    probs = exact.astype(BF16)
    g_probs = jnp.concatenate(
        [
            dot(d_out[c * SPAN : (c + 1) * SPAN], rows[c * SPAN : (c + 2) * SPAN, DH:], 1, 1)
            for c in range(16)
        ],
        0,
    )
    inner_sum = jnp.sum(g_probs * exact, axis=-1, keepdims=True)
    g_scores = exact * (g_probs - inner_sum + d_log)
    g_scores = jnp.where(own, 0.0, g_scores).astype(BF16)
    d_query, d_unit, d_value = [], [], []
    for c in range(16):
        here = slice(c * SPAN, (c + 1) * SPAN)
        both = slice(c * SPAN, (c + 2) * SPAN)
        after = slice((c + 1) * SPAN, (c + 2) * SPAN)
        d_query.append(dot(g_scores[here], unit[both], 1, 0))
        d_unit.append(dot(g_scores[here], rows[after, :DH], 0, 0))
        d_value.append(dot(probs[here], d_out[here], 0, 0))

    def overlap(parts):
        out = [parts[0][:SPAN]]
        for c in range(15):
            out.append(parts[c][SPAN:] + parts[c + 1][:SPAN])
        out.append(parts[15][SPAN:])
        return jnp.concatenate(out, 0)

    g_unit = overlap(d_unit)
    along = jnp.sum(g_unit * keys, axis=-1, keepdims=True)
    g_keys = inv * g_unit - keys * (inv * inv * inv) * along
    g_query = jnp.concatenate([jnp.zeros((SPAN, DH), F32)] + d_query, 0) + g_keys
    grads = jnp.concatenate([g_query, overlap(d_value)], 1).astype(BF16)
    for j in range(2):
        cols = slice(j * 2 * DH, (j + 1) * 2 * DH)
        send_out[:, cols] = leave(place_col_ref, j, grads[SPAN:]).astype(BF16)
    lent = leave(place_col_ref, 2, grads[:SPAN, :DH]) + leave(place_col_ref, 3, grads[:SPAN, DH:])
    b = iota((ROWS, 1), 0) & 7
    for q in range(4):
        lent = jnp.where(b == 4 + q, gain_ref[:, q * DH : (q + 1) * DH], lent)
    send_out[:, 4 * DH :] = lent.astype(BF16)


def attend_back(moved, rows, place_row, place_col, gain):
    return call(
        attend_back_kernel,
        (moved, rows, place_row, place_col, gain),
        [kept((ROWS, QV_LANES), BF16)],
        in_place=(1, 2, 3),
        name="attend_back",
    )[0]


def project_back_kernel(count, grads, core_ref, moved_ref, rank_col_ref, *refs):
    q_refs, v_refs = refs[:count], refs[count : 2 * count]
    refs = refs[2 * count :]
    if grads:
        back_ref, merged_ref, hn_ref, *refs = refs
        part_out, send_out, grad_out, gain_out = refs
    else:
        part_out, send_out, dq_out, dv_out, gain_out = refs
    gain_out[...] = dot(
        hot(iota((8, 1), 0) == (iota((1, ROWS), 1) & 7)), moved_ref[:, 4 * DH :], 1, 0
    )
    total = jnp.zeros((TOK, HN * 2 * DH), F32)
    lent_q = jnp.zeros((TOK, PART), F32)
    lent_v = jnp.zeros((TOK, PART), F32)
    for r in range(ROUNDS):
        hots = return_hots(rank_col_ref[:, r : r + 1])
        total = total + dot(hots[:, :NW], by_head(moved_ref, r, slice(0, 2 * DH)), 1, 0)
        total = total + dot(hots[:, NW : 2 * NW], by_head(moved_ref, r, slice(2 * DH, 4 * DH)), 1, 0)
        lent = by_head(moved_ref, r, slice(4 * DH, 5 * DH))
        lent_q = lent_q + dot(hots[:, 2 * NW : 3 * NW], lent, 1, 0)
        lent_v = lent_v + dot(hots[:, 3 * NW :], lent, 1, 0)
    d_q = jnp.concatenate([total[:, h * 2 * DH : h * 2 * DH + DH] for h in range(HN)], 1)
    d_v = jnp.concatenate([total[:, h * 2 * DH + DH : (h + 1) * 2 * DH] for h in range(HN)], 1)
    d_q = (d_q + lent_q).astype(BF16)
    d_v = (d_v + lent_v).astype(BF16)
    if grads:
        for c0 in range(2):
            for i, (left, right) in enumerate(
                ((back_ref, merged_ref[...]), (hn_ref, d_q), (hn_ref, d_v))
            ):
                put_pieces(grad_out, c0, i * 16, 16, dot(left[c0], right, 0, 0).astype(BF16))
    else:
        dq_out[...] = d_q
        dv_out[...] = d_v
    core = core_ref[0]
    from_q = out_of(core, d_q, q_refs)
    from_v = out_of(core, d_v, v_refs)
    put_halves([a + b for a, b in zip(from_q, from_v)], part_out, send_out)


def project_back(core, moved, rank_col, wq, wv, lefts=None):
    args, specs = unpacked([core, moved, rank_col, wq, wv, *(lefts or ())], 1)
    if lefts:
        outs = [kept((2 * QUAD, 8, ATTN_ROWS, PART), BF16)]
    else:
        outs = [kept((TOK, PART), BF16)] * 2
    return call(
        functools.partial(project_back_kernel, len(wq.parts()), lefts is not None),
        args,
        [sds((TOK, D), F32), kept((TOK, D), BF16), *outs, sds((8, DH), F32)],
        specs=specs,
        in_place=range(1, len(args) - 1),
        prefetch=1,
        name="project_back",
    )


def last_kernel(g_ref, own_ref, other_ref, x_ref, gain_ref, g_out, dgain_out):
    xhat, rstd = norm_parts(x_ref[...])
    add, dgain = norm_back(own_ref[...] + other_ref[...].astype(F32), gain_ref[...], xhat, rstd)
    g_out[...] = g_ref[...] + add
    dgain_out[...] = dgain


def last(g, own, other, x, gain):
    return call(
        last_kernel,
        (g, own, other, x, gain),
        [kept((TOK, D), F32), sds((1, D), F32)],
        in_place=(0, 3),
        name="last",
    )


def pair_dot(left_a, left_b, right_a, right_b):
    left = jnp.concatenate([left_a, left_b], 0)
    right = jnp.concatenate([right_a, right_b], 0)
    return dot(left, right, 0, 0).astype(BF16)


def attn_grad_kernel(count, core_ref, *refs):
    out_ref = refs[-1]
    for i in range(count):
        la, lb, ra, rb = refs[4 * i : 4 * i + 4]
        got = pair_dot(la[0], lb[0], ra[...], rb[...])
        out_ref[:, i * 16 : (i + 1) * 16] = got.reshape(32, 16, PART)


def attn_grad(core, pairs):
    half = pl.BlockSpec((1, TOK, PART), lambda i, core: (core[0], 0, 0))
    args = [a for left, right in pairs for a in (*left, *right)]
    specs = {4 * i + j: half for i in range(len(pairs)) for j in range(2)}
    return call(
        functools.partial(attn_grad_kernel, len(pairs)),
        (core, *args),
        [kept((32, 16 * len(pairs), PART), BF16)],
        specs=specs,
        prefetch=1,
        in_place=range(0, len(args), 2),
        name="attn_grad",
    )[0]


def join_kernel(*refs):
    at = 0
    for ref in refs[:-1]:
        refs[-1][:, at : at + ref.shape[1]] = ref[...]
        at += ref.shape[1]


def join(arrays):
    rows = sum(a.shape[1] for a in arrays)
    return call(
        join_kernel,
        arrays,
        [kept((8, rows, PART), BF16)],
        grid=(4,),
        specs={
            i: pl.BlockSpec((2, a.shape[1], PART), lambda g: (g, 0, 0)) for i, a in enumerate(arrays)
        },
        out_specs={0: pl.BlockSpec((2, rows, PART), lambda g: (g, 0, 0))},
        in_place=range(len(arrays)),
        name="join",
    )[0]


def swap_narrow(values):
    return lax.ppermute(values, "narrow", [(0, 1), (1, 0)])


def with_core(values):
    other = lax.ppermute(values, "wide", [(i, i ^ 1) for i in range(NW)])
    return values, other


def to_all(values):
    return lax.all_to_all(values, "wide", split_axis=0, concat_axis=0, tiled=True)


SAME_CORE = [
    [y * 32 + z * 8 + x * 2 + c for z in range(4) for x in range(4) for y in range(2)]
    for c in range(2)
]
LAYER_OF_Y = [[y * 32 + i for i in range(NW // 2)] for y in range(2)]


def summed(values):
    return jnp.sum(to_same_core(values).astype(F32), axis=0).astype(BF16)


ALONG_X_AND_CORE = [[hi * 8 + i for i in range(8)] for hi in range(8)]
ALONG_Z_AND_Y = [
    [y * 32 + z * 8 + i for z in range(4) for y in range(2)] for i in range(8)
]
ALONG_Z = [
    [y * 32 + z * 8 + x * 2 + c for z in range(4)] for y in range(2) for x in range(4) for c in range(2)
]


def summed_along_x(values):
    return lax.psum_scatter(
        values, "wide", scatter_dimension=0, tiled=True, axis_index_groups=ALONG_X_AND_CORE
    ).reshape(values.shape[1:])


def summed_across_x(values):
    moved = lax.all_to_all(
        values, "wide", split_axis=0, concat_axis=0, tiled=True, axis_index_groups=ALONG_Z_AND_Y
    )
    return jnp.sum(moved.astype(F32), axis=0).astype(BF16)


def summed_along_z(values):
    return lax.psum_scatter(
        values, "wide", scatter_dimension=0, tiled=True, axis_index_groups=ALONG_Z
    )


def summed_along_y(values):
    y = lax.axis_index("wide") >> 5
    mine = lax.dynamic_index_in_dim(values, y, keepdims=False)
    theirs = lax.dynamic_index_in_dim(values, 1 - y, keepdims=False)
    got = lax.ppermute(theirs, "wide", [(i, i ^ 32) for i in range(NW)])
    return (mine.astype(F32) + got.astype(F32)).astype(BF16)


def to_same_core(values):
    return lax.all_to_all(
        values, "wide", split_axis=0, concat_axis=0, tiled=True, axis_index_groups=SAME_CORE
    )


def after(values, *others):
    return lax.optimization_barrier((values, others))[0]


def gathered(rows):
    other = lax.ppermute(rows, "wide", [(i, i ^ 32) for i in range(NW)])
    low = lax.axis_index("wide") < 32
    both = jnp.stack(
        [
            jnp.where(low, a, b).reshape(-1, 16, PART) for a, b in ((rows, other), (other, rows))
        ],
        1,
    ).reshape(-1, PART)
    got = lax.all_gather(both, "wide", axis=0, tiled=True, axis_index_groups=LAYER_OF_Y)
    return got.reshape(QUAD, QUAD, 2, both.shape[0], PART)


def moved_rows(rows):
    return to_all(rows.reshape(NW, rows.shape[0] // NW, -1)).reshape(rows.shape)


def on_device(
    x_first,
    x_second,
    grad_first,
    grad_second,
    sort_target,
    owner,
    master,
    moment_first,
    moment_second,
    gains,
    gain_first,
    gain_second,
):
    me = lax.axis_index("wide").astype(I32)
    half = lax.axis_index("narrow").astype(I32).reshape(1)
    core = (me & 1).reshape(1)
    owner_row = owner.reshape(1, TILES)

    routed = route_out(me.reshape(1), owner_row, master)
    sort_target, held = after((sort_target, owner), routed)
    moved = moved_rows(routed)
    held_by = []
    for l in range(LAYERS):
        of = held[l * 88 : (l + 1) * 88]
        held_by += [of[at : at + 32].reshape(8, 4).T.reshape(32) for at in (24, 56)]
        held_by += [of[16:24], of[:16]]
    held_by = jnp.repeat(jnp.concatenate(held_by), 2)
    code = (held_by // CAP) * PACK + (held_by % CAP) * 2 + np.arange(2 * TILES, dtype=np.int32) % 2
    code_col = code.reshape(-1, 1)
    code_row = code.reshape(1, -1)
    mine = lax.dynamic_slice_in_dim(sort_target, me * TOK, TOK, axis=2).reshape(-1, TOK)
    by_source = lax.dynamic_index_in_dim(sort_target, me >> 5, 1, keepdims=False)
    plans = plan((me & 7).reshape(1), mine, by_source.reshape(LAYERS, NW, TOK))
    rank_rows, rank_cols, place_rows, place_cols = [plans[i::4] for i in range(4)]
    flat_gains = gains.reshape(LAYERS * 2, PART)
    x_two, gain_rows = inner(
        half, [(x_second, swap_narrow(x_second)), (flat_gains, swap_narrow(flat_gains))], "inner_a"
    )
    moved = after(moved, code_col, code_row, plans, x_two, gain_rows)
    first_rows, early_rows, late_rows = pick(code_col, moved)
    x_first, grad_first, grad_second = after((x_first, grad_first, grad_second), x_two)
    pairs = [(a, swap_narrow(a)) for a in (x_first, grad_first, grad_second)]
    first_w = with_core(after(to_same_core(first_rows), pairs))
    early = gathered(early_rows)
    late = gathered(after(late_rows, first_w))
    x_one, g_one, g_two = inner(half, pairs, "inner_b")
    w_ffn = [early, late]
    w_attn = [
        [Weight(8, early), Weight(0, *first_w), Weight(1, *first_w)],
        [Weight(9, early), Weight(10, early), Weight(11, early)],
    ]
    gain = [[gain_rows[2 * l + i].reshape(1, D) for i in range(2)] for l in range(LAYERS)]

    saved = []
    pending = None
    for l in range(LAYERS):
        w_out, w_qk, w_value = w_attn[l]
        x_two, hn, send = project(core, x_two, pending, gain[l][0], w_qk, w_value, rank_rows[l])
        moved = moved_rows(send)
        if l == 0:
            moved = after(moved, x_one, g_one, g_two)
        rows, send = attend(moved, place_rows[l], place_cols[l])
        moved = moved_rows(send)
        own, send, o, share, merged = merge(core, moved, rank_cols[l], w_out)
        x_one, hf, pre, act, own_f, send_f = ffn(
            x_one, own, swap_narrow(send), gain[l][1], w_ffn[l]
        )
        pending = (own_f, swap_narrow(send_f))
        saved.append((x_two, x_one, hn, rows, o, share, merged, hf, pre, act))
    y_two = x_two + (pending[0] + pending[1].astype(F32))
    y_first, y_second = outer(half, (x_one, y_two), "outer_y")

    pending = None
    dgains = [[None, None], [None, None]]
    gain_sums = []
    for l in reversed(range(LAYERS)):
        x_in, y_mid, hn, rows, o, share, merged, hf, pre, act = saved[l]
        w_out, w_qk, w_value = w_attn[l]
        g_two, own, send, dgain, ffn_part = ffn_back(g_two, pending, pre, hf, act, w_ffn[l])
        if l == 0:
            dgains[1][0] = dgain
        other = swap_narrow(send)
        ffn_part = summed_along_x(ffn_part)
        g_one, back, send, dgains[l][1] = merge_back(
            core, g_one, own, other, y_mid, gain[l][1], w_out, o, share, rank_rows[l]
        )
        moved = moved_rows(send)
        if l > 0:
            moved = after(moved, y_first, y_second)
            half_gain = dgains[1][1][:, :PART]
        else:
            dx_first = outer(half, (g_one,), "outer_dx_first")[0]
            joined = join([ffn_before, attn_before])
            moved = after(moved, dx_first, joined)
            half_gain = dgains[1][1][:, PART:]
        send = attend_back(moved, rows, place_rows[l], place_cols[l], half_gain)
        moved = moved_rows(send)
        if l > 0:
            moved = after(moved, ffn_part)
        if l > 0:
            own, send, attn_part, gain_sum = project_back(
                core, moved, rank_cols[l], w_qk, w_value, (back, merged, hn)
            )
            attn_before = summed_along_x(attn_part)
            ffn_before = ffn_part
        else:
            own, send, dq, dv, gain_sum = project_back(core, moved, rank_cols[l], w_qk, w_value)
            hn2 = with_core(hn)
            pairs = [(with_core(back), with_core(merged)), (hn2, with_core(dq)), (hn2, with_core(dv))]
            attn_part = attn_grad(core, pairs)
            attn_rows = summed(attn_part)
            ffn_rows = summed_across_x(after(ffn_part, attn_part))
            reduced = summed_along_y(after(summed_along_z(joined), attn_part))
        other = swap_narrow(send)
        gain_sums.append(gain_sum[4:].reshape(1, PART))
        pending = (own, other, x_in, gain[l][0])
    g_two, dgains[0][0] = last(g_two, *pending)
    dx_second = outer(half, (g_two,), "outer_dx_second")[0]
    parts = (ffn_rows, attn_rows, reduced)
    back_rows = moved_rows(
        route_back(code_row, parts, (dgains[1][0], dgains[0][1], dgains[0][0]))
    )
    back_rows = after(back_rows, dx_second)
    slot_grad, slot_first, slot_second, slot_new, *gain_news = slots_update(
        half,
        me.reshape(1),
        owner_row,
        back_rows,
        jnp.concatenate(gain_sums, 1),
        master,
        moment_first,
        moment_second,
        gains,
        gain_first,
        gain_second,
    )
    gain_grad, gain_first_new, gain_second_new, gain_new = gain_news
    return (
        y_first,
        y_second,
        dx_first,
        dx_second,
        slot_grad,
        slot_first,
        slot_second,
        slot_new,
        gain_grad,
        gain_first_new,
        gain_second_new,
        gain_new,
    )


def solution(mesh):
    rows = P("wide", "narrow")
    tiles = P("wide", None, "narrow")
    gains = P(None, None, "narrow")
    return jax.shard_map(
        on_device,
        mesh=mesh,
        in_specs=(rows,) * 4 + (P(), P()) + (tiles,) * 3 + (gains,) * 3,
        out_specs=(rows,) * 4 + (tiles,) * 4 + (gains,) * 4,
        check_vma=False,
    )
```

```python
import functools

import jax
import jax.numpy as jnp
import numpy as np
from jax import lax
from jax.experimental import pallas as pl
from jax.experimental.pallas import tpu as pltpu
from jax.sharding import PartitionSpec as P

D = 1024
PART = 512
DH = 128
HN = 4
SPAN = 64
TR = 128
CAP = 5
TILES = 176
TOK = 128
NW = 64
LAYERS = 2
ROUNDS = 2
STEP = 5
GROUPS = 8
QV_LANES = 5 * DH
O_LANES = 3 * DH
ROWS = NW * 8
PACK = 16
WIDE_PACK = 24
PAIR_ROWS = WIDE_PACK * (NW // 2)
QUAD = 4
UP, DOWN = 0, 1
LAYER_ROWS = 176
ATTN_ROWS = 48
FFN_ROWS = 128
EARLY_ROWS = 384

MASK_FILL = -1000000000.0
NORM_EPS = 1e-05
BETA_ONE = 0.5
BETA_TWO = 0.5
RATE_WEIGHT = 0.05
RATE_GAIN = 0.2
DECAY = 0.01
EPSILON = 1e-08

F32 = jnp.float32
BF16 = jnp.bfloat16
I32 = jnp.int32
VMEM_BYTES = 20 * 1024 * 1024
BIG_VMEM_BYTES = 32 * 1024 * 1024


def feature_of(p):
    c0 = p >> 9
    z = (p >> 7) & 3
    tau = (p >> 5) & 3
    y = (p >> 4) & 1
    t = (p >> 1) & 7
    e = p & 1
    return t * 128 + tau * 32 + c0 * 16 + (y * 4 + z) * 2 + e


def iota(shape, dim):
    return lax.broadcasted_iota(I32, shape, dim)


def hot(mask):
    return jnp.where(mask, 1.0, 0.0).astype(BF16)


def dot(a, b, ca, cb):
    return lax.dot_general(a, b, (((ca,), (cb,)), ((), ())), preferred_element_type=F32)


def in_hbm(array):
    return pltpu.with_memory_space_constraint(array, pltpu.MemorySpace.HBM)


def call(
    kernel, args, outs, grid=(1,), specs=None, out_specs=None, scratch=(), prefetch=0, in_place=(), name=None
):
    specs = specs or {}
    out_specs = out_specs or {}
    def whole(shape):
        zeros = (0,) * len(shape)
        return pl.BlockSpec(shape, lambda *_: zeros)
    in_list = [specs.get(i, whole(a.shape)) for i, a in enumerate(args[prefetch:])]
    args = [in_hbm(a) if i - prefetch in in_place else a for i, a in enumerate(args)]
    out_list = [out_specs.get(i, whole(o.shape)) for i, o in enumerate(outs)]
    return pl.pallas_call(
        kernel,
        out_shape=outs,
        grid_spec=pltpu.PrefetchScalarGridSpec(
            num_scalar_prefetch=prefetch,
            grid=grid,
            in_specs=in_list,
            out_specs=out_list,
            scratch_shapes=list(scratch),
        ),
        compiler_params=pltpu.CompilerParams(vmem_limit_bytes=VMEM_BYTES),
        name=name,
    )(*args)


def sds(shape, dtype):
    return jax.ShapeDtypeStruct(shape, dtype)


def kept(shape, dtype):
    return pltpu.MemorySpace.HBM(shape, dtype)


def norm_parts(values):
    mean = jnp.mean(values, axis=-1, keepdims=True)
    var = jnp.mean(values * values, axis=-1, keepdims=True) - mean * mean
    rstd = lax.rsqrt(var + NORM_EPS)
    return (values - mean) * rstd, rstd


def norm_back(upstream, gain, xhat, rstd):
    gh = upstream * gain
    m1 = jnp.mean(gh, axis=-1, keepdims=True)
    m2 = jnp.mean(gh * xhat, axis=-1, keepdims=True)
    return rstd * (gh - m1 - xhat * m2), jnp.sum(upstream * xhat, axis=0, keepdims=True)


def flat(ref):
    return ref[...].reshape(PART, PART)


def halves(core, first, second):
    mine = core == 0
    return jnp.where(mine, first, second), jnp.where(mine, second, first)


class Far:
    def __init__(self, array):
        self.operands = [in_hbm(array)]
        self.scratch = [pltpu.VMEM(array.shape, array.dtype), pltpu.SemaphoreType.DMA((1,))]

    def fetch(self, refs, buffer, sems):
        return [pltpu.make_async_copy(refs[0], buffer, sems.at[0])]


class FfnWeight(Far):
    def __init__(self, array):
        self.operands = [in_hbm(array)]
        self.scratch = [
            pltpu.VMEM((2, QUAD, 2, QUAD, FFN_ROWS, PART), BF16),
            pltpu.SemaphoreType.DMA((16,)),
        ]

    def fetch(self, refs, buffer, sems):
        copies = []
        for c in range(QUAD):
            for part in range(2):
                for c0 in range(2):
                    source = refs[0].at[:, c, c0, pl.ds(part * FFN_ROWS, FFN_ROWS), :]
                    copies.append(
                        pltpu.make_async_copy(source, buffer.at[part, c, c0], sems.at[len(copies)])
                    )
        return copies


class Direct(Far):
    def __init__(self, array):
        self.operands = [in_hbm(array)]
        self.scratch = []


class FarSlots(Far):
    def __init__(self, array):
        self.operands = [in_hbm(array)]
        self.scratch = [pltpu.VMEM(array.shape, array.dtype), pltpu.SemaphoreType.DMA((CAP,))]

    def fetch(self, refs, buffer, sems):
        return [
            pltpu.make_async_copy(refs[0].at[s], buffer.at[s], sems.at[s]) for s in range(CAP)
        ]


class Fetched:
    def __init__(self, copies, buffer):
        self.copies = list(copies)
        self.buffer = buffer
        for copy in self.copies:
            copy.start()

    def wait(self, count=None):
        count = len(self.copies) if count is None else count
        for copy in self.copies[:count]:
            copy.wait()
        self.copies = self.copies[count:]

    def __getitem__(self, index):
        self.wait()
        return self.buffer[index]

    def halves(self):
        self.wait()
        return [self.buffer[i].reshape(PART, PART) for i in range(2)]

    def block(self, part, c, c0):
        return self.buffer[part, c, c0].reshape(PART, PART)


class Sent:
    def __init__(self, shape, dtype, pieces=1):
        self.shape, self.dtype, self.pieces = shape, dtype, pieces


class Sending:
    def __init__(self, target, buffer, sems, pieces):
        self.target, self.buffer, self.sems, self.pieces = target, buffer, sems, pieces
        self.copies = []

    def __setitem__(self, index, value):
        self.buffer[index] = value

    def flush(self):
        k = len(self.copies)
        size = self.target.shape[0] // self.pieces
        rows = pl.ds(k * size, size)
        source, target = self.buffer.at[rows], self.target.at[rows]
        if source.shape != target.shape:
            target = target.at[:, :, pl.ds(0, self.buffer.shape[2]), :]
        copy = pltpu.make_async_copy(source, target, self.sems.at[k])
        copy.start()
        self.copies.append(copy)

    def flush_all(self):
        while len(self.copies) < self.pieces:
            self.flush()

    def wait(self):
        for copy in self.copies:
            copy.wait()


def run(kernel, args, outs, prefetch=0, name=None, vmem=None, partial=None, temps=(), aliases=None):
    operands, in_specs, scratch = [], [], []
    for i, a in enumerate(args):
        if isinstance(a, Far):
            operands += a.operands
            in_specs += [pl.BlockSpec(memory_space=pl.ANY)] * len(a.operands)
            scratch += a.scratch
        else:
            operands.append(a)
            if i >= prefetch:
                zeros = (0,) * a.ndim
                in_specs.append(pl.BlockSpec(a.shape, lambda *_, zeros=zeros: zeros))
    out_shapes, out_specs = [], []
    for i, o in enumerate(outs):
        if isinstance(o, Sent):
            out_shapes.append(kept(o.shape, o.dtype))
            out_specs.append(pl.BlockSpec(memory_space=pl.ANY))
            shape = (partial or {}).get(i, o.shape)
            scratch += [pltpu.VMEM(shape, o.dtype), pltpu.SemaphoreType.DMA((o.pieces,))]
        else:
            zeros = (0,) * len(o.shape)
            out_shapes.append(o)
            out_specs.append(pl.BlockSpec(o.shape, lambda *_, zeros=zeros: zeros))

    def body(*refs):
        ins, rest = list(refs[: len(operands)]), list(refs[len(operands) :])
        out_refs, temps = rest[: len(outs)], rest[len(outs) :]
        seen = []
        for a in args:
            if isinstance(a, Far):
                mine = [ins.pop(0) for _ in a.operands]
                if a.scratch:
                    buffer, sems = temps.pop(0), temps.pop(0)
                    seen.append(Fetched(a.fetch(mine, buffer, sems), buffer))
                else:
                    seen.append(mine[0])
            else:
                seen.append(ins.pop(0))
        sending = []
        for o, ref in zip(outs, out_refs):
            if isinstance(o, Sent):
                ref = Sending(ref, temps.pop(0), temps.pop(0), o.pieces)
                sending.append(ref)
            seen.append(ref)
        kernel(*seen, *temps)
        for ref in sending:
            ref.flush_all()
        for ref in sending:
            ref.wait()

    return pl.pallas_call(
        body,
        out_shape=out_shapes,
        grid_spec=pltpu.PrefetchScalarGridSpec(
            num_scalar_prefetch=prefetch,
            grid=(1,),
            in_specs=in_specs,
            out_specs=out_specs,
            scratch_shapes=[*scratch, *temps],
        ),
        compiler_params=pltpu.CompilerParams(vmem_limit_bytes=vmem or VMEM_BYTES),
        input_output_aliases=aliases or {},
        name=name,
    )(*operands)


class Weight:
    def __init__(self, index, *arrays):
        self.index = index
        self.arrays = arrays

    def parts(self):
        index = self.index
        if len(self.arrays) == 2:
            return [
                (a, pl.BlockSpec((8, 16, PART), lambda *_, z=z: (z, index, 0)))
                for a in self.arrays
                for z in range(4)
            ]
        return [
            (self.arrays[0], pl.BlockSpec((1, QUAD, 2, 32, PART), lambda *_, z=z: (z, 0, 0, index, 0)))
            for z in range(4)
        ]


def rows_of(refs):
    return jnp.concatenate([r[...].reshape(-1, PART) for r in refs], 0)


def weight_halves(core, refs):
    if len(refs) == 4:
        return [
            jnp.concatenate([r[0, :, c0].reshape(-1, PART) for r in refs], 0) for c0 in range(2)
        ]
    return rows_of(refs[:4]), rows_of(refs[4:])


def into(core, full, refs):
    first, second = full[:, :PART], full[:, PART:]
    if len(refs) == 8:
        first, second = halves(core, first, second)
    w = weight_halves(core, refs)
    return dot(first.astype(BF16), w[0], 1, 0) + dot(second.astype(BF16), w[1], 1, 0)


def out_of(core, part, refs):
    w = weight_halves(core, refs)
    pair = dot(part, w[0], 1, 1), dot(part, w[1], 1, 1)
    return pair if len(refs) == 4 else halves(core, *pair)


def unpacked(args, prefetch):
    out, specs = [], {}
    for a in args:
        if isinstance(a, Weight):
            for array, spec in a.parts():
                specs[len(out) - prefetch] = spec
                out.append(array)
        else:
            out.append(a)
    return out, specs


def wanted(shape, dim):
    m = iota(shape, dim)
    g16 = (m >> 3) * 16
    b = m & 7
    before = (g16 - 2) & 127
    lent = before + (b >> 1)
    return (
        g16 + 2 * b,
        g16 + 2 * b + 1,
        jnp.where((b == 0) | (b == 2), lent, -1),
        jnp.where((b == 1) | (b == 3), lent, -1),
    )


def send_hots(rank_row, count=4):
    return hot(jnp.concatenate(wanted((NW, 1), 0)[:count], 0) == rank_row)


def return_hots(rank_col, count=4):
    return hot(rank_col == jnp.concatenate(wanted((1, NW), 1)[:count], 1))


def spread(col, lanes):
    hi, mid, lo = pieces(col)
    k = lanes & 7
    return jnp.where(k == 0, hi, jnp.where(k == 1, mid, jnp.where(k == 2, lo, 0.0)))


def pieces(col):
    hi = col.astype(BF16).astype(F32)
    rest = col - hi
    mid = rest.astype(BF16).astype(F32)
    return hi, mid, rest - mid


def either(lanes, even, odd):
    return jnp.where(lanes < 8, even, jnp.where(lanes < 16, odd, 0.0))


def slot_kinds(owner_ref, me):
    lane = iota((1, TILES), 1)
    ffn = jnp.where(lane >= TILES // LAYERS, lane - TILES // LAYERS, lane) >= 24
    return [
        jnp.max(
            jnp.where((owner_ref[...] == me * CAP + s) & ffn, 1, 0), axis=1, keepdims=True
        )
        for s in range(CAP)
    ]


def row_of_slots(kinds):
    r = iota((1, TR), 1)

    def place(low, x):
        j3 = (low >> 1) & 7
        device = (j3 & 3) * 8 + x * 2 + (low >> 4)
        return device * WIDE_PACK + (j3 >> 2) * 2 + (low & 1)

    attn = place(r & 31, r >> 5)
    ffn = place(r >> 2, r & 3)
    return jnp.concatenate([jnp.where(k == 1, ffn, attn) + 4 * s for s, k in enumerate(kinds)], 1)


def slot_of_row(kinds):
    r = iota((1, NW * PACK), 1)
    d, m = r >> 4, r & (PACK - 1)
    s, e = m >> 1, m & 1
    tau = (d >> 1) & 3
    low = (d & 1) * 16 + (d >> 3) * 2 + e
    out = jnp.full((1, NW * PACK), -1, I32)
    for i, k in enumerate(kinds):
        out = jnp.where(s == i, i * TR + jnp.where(k == 1, low * 4 + tau, tau * 32 + low), out)
    return out


def route_out_kernel(me_ref, owner_ref, master_ref, out_ref):
    tiles = master_ref[...].reshape(CAP * TR, PART).astype(BF16)
    place = row_of_slots(slot_kinds(owner_ref, me_ref[0]))
    rows = dot(hot(iota((PAIR_ROWS, 1), 0) == place), tiles, 1, 0).astype(BF16)
    out_ref[:PAIR_ROWS] = rows
    out_ref[PAIR_ROWS:] = rows


def route_out(me, owner_row, master):
    return call(
        route_out_kernel,
        (me, owner_row, master),
        [kept((2 * PAIR_ROWS, PART), BF16)],
        prefetch=1,
        in_place=(1,),
        name="route_out",
    )[0]


def pick_kernel(code_ref, moved_ref, first_ref, early_ref, late_ref):
    picked = hot(code_ref[...] == iota((1, 2 * PAIR_ROWS), 1))
    rows = dot(picked, moved_ref[...], 1, 0).astype(BF16)
    early_ref[...] = rows[:EARLY_ROWS]
    late_ref[...] = rows[EARLY_ROWS : EARLY_ROWS + 2 * FFN_ROWS]
    first = rows[EARLY_ROWS + 2 * FFN_ROWS :]
    first_ref[...] = jnp.broadcast_to(first[None], first_ref.shape)


def pick(code_col, moved):
    return call(
        pick_kernel,
        (code_col, moved),
        [
            kept((32, 32, PART), BF16),
            kept((EARLY_ROWS, PART), BF16),
            kept((2 * FFN_ROWS, PART), BF16),
        ],
        name="pick",
    )


def route_back_kernel(code_ref, *refs):
    *parts, gain_a, gain_b, gain_c, out_ref = refs
    rows = jnp.concatenate([p[...] for p in parts], 0)
    place = iota((NW * PACK, 1), 0)
    out = dot(hot(place == code_ref[...]), rows, 1, 0)
    gains = jnp.concatenate(
        [
            half
            for g in (gain_a, gain_b, gain_c)
            for half in (g[:, :PART], g[:, PART:])
        ]
        + [jnp.zeros((2, PART), F32)],
        0,
    ).astype(BF16)
    spare = hot((place & (PACK - 1)) - 2 * CAP == iota((1, 8), 1))
    out_ref[...] = (out + dot(spare, gains, 1, 0)).astype(BF16)


def route_back(code_row, parts, gains):
    return call(
        route_back_kernel,
        (code_row, *parts, *gains),
        [kept((NW * PACK, PART), BF16)],
        name="route_back",
    )[0]


def adam(grad, first, second, weights, rate):
    first_new = BETA_ONE * first + (1.0 - BETA_ONE) * grad
    second_new = BETA_TWO * second + (1.0 - BETA_TWO) * grad * grad
    step = (
        first_new
        / (1.0 - BETA_ONE**STEP)
        / (jnp.sqrt(second_new / (1.0 - BETA_TWO**STEP)) + EPSILON)
    )
    return first_new, second_new, weights - rate * (step + DECAY * weights)


def slots_kernel(
    half_ref, me_ref, owner_ref, moved_ref, ready_ref, m_ref, a_ref, b_ref, gains_ref, ga_ref, gb_ref,
    grad_out, first_out, second_out, new_out, gg_out, gf_out, gs_out, gn_out
):
    rows = moved_ref[...]
    placed = hot(iota((CAP * TR, 1), 0) == slot_of_row(slot_kinds(owner_ref, me_ref[0])))
    grads = dot(placed, rows, 1, 0)
    for s in range(CAP):
        for ref in (m_ref, a_ref, b_ref):
            ref.wait(1)
        grad = grads[s * TR : (s + 1) * TR]
        grad_out[s] = grad
        first_out[s], second_out[s], new_out[s] = adam(
            grad, a_ref.buffer[s], b_ref.buffer[s], m_ref.buffer[s], RATE_WEIGHT
        )
        for out in (grad_out, first_out, second_out, new_out):
            out.flush()
    spare = hot((iota((1, NW * PACK), 1) & (PACK - 1)) - 2 * CAP == iota((8, 1), 0))
    sums = dot(spare, rows, 1, 0)
    gains = [jnp.concatenate([sums[q : q + 1], sums[q + 1 : q + 2]], 1) for q in (4, 2, 0)]
    inner_sum = jnp.concatenate(gains + [ready_ref[...]], 0)
    back = hot(feature_of(iota((1, D), 1)) == iota((PART, 1), 0) + half_ref[0] * PART)
    parts = dot(jnp.concatenate(pieces(inner_sum), 0).astype(BF16), back, 1, 1)
    n = 2 * LAYERS
    total = parts[:n] + parts[n : 2 * n] + parts[2 * n :]
    for l in range(LAYERS):
        gain_grad = total[2 * l : 2 * l + 2]
        gg_out[l] = gain_grad
        gf_out[l], gs_out[l], gn_out[l] = adam(
            gain_grad, ga_ref[l], gb_ref[l], gains_ref[l], RATE_GAIN
        )


def slots_update(half, me, owner_row, moved, ready, master, first, second, gains, gain_first, gain_second):
    return run(
        slots_kernel,
        [
            half, me, owner_row, moved, ready,
            FarSlots(master), FarSlots(first), FarSlots(second),
            gains, gain_first, gain_second,
        ],
        [Sent((CAP, TR, PART), F32, CAP)] * 4 + [sds((LAYERS, 2, PART), F32)] * 4,
        prefetch=2,
        name="slots_update",
    )


def turned(col):
    same = iota((TOK, TOK), 0) == iota((TOK, TOK), 1)
    return jnp.sum(jnp.where(same, col, 0), axis=0, keepdims=True)


def plan_kernel(group_ref, mine_ref, source_ref, *outs):
    same = iota((TOK, TOK), 0) == iota((TOK, TOK), 1)
    b = iota((ROWS, 1), 0) & 7
    block = group_ref[0] * 8 + b
    before = (group_ref[0] * 8 - 1) & 63
    lanes = iota((TOK, TOK), 1)
    for l in range(LAYERS):
        rank_row, rank_col, place_row = outs[3 * l : 3 * l + 3]
        cols = jnp.zeros((TOK, TOK), I32)
        for r in range(ROUNDS):
            row = mine_ref[l * ROUNDS + r : l * ROUNDS + r + 1, :]
            col = jnp.sum(jnp.where(same, row, 0), axis=1, keepdims=True)
            rank_row[r : r + 1, :] = jnp.sum(jnp.where(col < row, 1, 0), axis=0, keepdims=True)
            rank = jnp.sum(jnp.where(row < col, 1, 0), axis=1, keepdims=True)
            cols = jnp.where(lanes == r, rank, cols)
        rank_col[...] = cols
        source = source_ref[l]
        target = jnp.broadcast_to(source[:, None, :], (NW, 8, TOK)).reshape(ROWS, TOK)
        place = target & (TOK - 1)
        got = []
        for want in (block, before):
            inside = (target >> 7) == want
            got.append(jnp.min(jnp.where(inside, place, TOK), axis=1, keepdims=True))
            got.append(jnp.max(jnp.where(inside, place, -1), axis=1, keepdims=True))
        low, high, low_lent, high_lent = got
        columns = (
            low + TOK * b,
            high + TOK * b,
            jnp.where(b == 0, low_lent - SPAN, jnp.where(b == 2, high_lent - SPAN, -1)),
            jnp.where(b == 1, low_lent - SPAN, jnp.where(b == 3, high_lent - SPAN, -1)),
        )
        for j, column in enumerate(columns):
            for q in range(4):
                at = slice(q * TOK, (q + 1) * TOK)
                place_row[j : j + 1, at] = turned(column[at])


def plan(group, mine, source):
    layer = [kept((ROUNDS, TOK), I32), kept((TOK, TOK), I32), kept((4, ROWS), I32)]
    return call(plan_kernel, (group, mine, source), layer * LAYERS, prefetch=1, name="plan")


def inner_kernel(half_ref, *refs):
    count = len(refs) // 3
    n = half_ref[0]
    feature = feature_of(iota((1, D), 1))
    mine = hot(feature == iota((PART, 1), 0) + n * PART)
    theirs = hot(feature == iota((PART, 1), 0) + (1 - n) * PART)
    for i in range(count):
        own, other, out = refs[2 * i], refs[2 * i + 1], refs[2 * count + i]
        if own.dtype == BF16:
            out[...] = dot(own[...], mine, 1, 0) + dot(other[...], theirs, 1, 0)
        else:
            total = jnp.zeros(out.shape, F32)
            for a, b in zip(pieces(own[...]), pieces(other[...])):
                total = total + (dot(a.astype(BF16), mine, 1, 0) + dot(b.astype(BF16), theirs, 1, 0))
            out[...] = total


def inner(half, pairs, name):
    flat = [a for pair in pairs for a in pair]
    outs = [sds((own.shape[0], D), F32) for own, _ in pairs]
    return call(inner_kernel, (half, *flat), outs, prefetch=1, name=name)


def outer_kernel(count, half_ref, *refs):
    n = half_ref[0]
    feature = feature_of(iota((1, D), 1))
    back = hot(feature == iota((PART, 1), 0) + n * PART)
    for i in range(count):
        total = jnp.zeros(refs[count + i].shape, F32)
        for part in pieces(refs[i][...]):
            total = total + dot(part.astype(BF16), back, 1, 1)
        refs[count + i][...] = total


def outer(half, arrays, name):
    outs = [sds((a.shape[0], PART), F32) for a in arrays]
    return call(
        functools.partial(outer_kernel, len(arrays)), (half, *arrays), outs, prefetch=1, name=name
    )


def project_kernel(pending, count, core_ref, *refs):
    if pending:
        x_ref, own_ref, other_ref, *rest = refs
        x = x_ref[...] + (own_ref[...].astype(F32) + other_ref[...].astype(F32))
    else:
        x_ref, *rest = refs
        x = x_ref[...]
    gain_ref, *rest = rest
    q_refs, v_refs = rest[:count], rest[count : 2 * count]
    rank_ref, x_out, hn_out, send_out = rest[2 * count :]
    core = core_ref[0]
    x_out[...] = x
    xhat, _ = norm_parts(x)
    hn = xhat * gain_ref[...]
    hn_out[0] = hn[:, :PART].astype(BF16)
    hn_out[1] = hn[:, PART:].astype(BF16)
    q = into(core, hn, q_refs).astype(BF16)
    v = into(core, hn, v_refs).astype(BF16)
    qv = jnp.concatenate([m[:, h * DH : (h + 1) * DH] for h in range(HN) for m in (q, v)], 1)
    for r in range(ROUNDS):
        moved = dot(send_hots(rank_ref[r : r + 1, :]), qv, 1, 0)
        even, odd = moved[:NW].astype(BF16), moved[NW : 2 * NW].astype(BF16)
        lent_q, lent_v = moved[2 * NW : 3 * NW], moved[3 * NW :]
        for h in range(HN):
            rows = slice((r * HN + h) * NW, (r * HN + h + 1) * NW)
            at = h * 2 * DH
            send_out[rows, : 2 * DH] = even[:, at : at + 2 * DH]
            send_out[rows, 2 * DH : 4 * DH] = odd[:, at : at + 2 * DH]
            send_out[rows, 4 * DH :] = (
                lent_q[:, at : at + DH] + lent_v[:, at + DH : at + 2 * DH]
            ).astype(BF16)


def project(core, x, pending, gain, wq, wv, rank_row):
    args, specs = unpacked([core, x, *(pending or ()), gain, wq, wv, rank_row], 1)
    return call(
        functools.partial(project_kernel, pending is not None, len(wq.parts())),
        args,
        [kept((TOK, D), F32), kept((2, TOK, PART), BF16), kept((ROWS, QV_LANES), BF16)],
        specs=specs,
        in_place=(0, *((1,) if pending else ()), *(tuple(specs) if len(wq.parts()) == 4 else ())),
        prefetch=1,
        name="project",
    )


def scores_of(rows):
    keys = rows[:, :DH].astype(F32)
    inv = lax.rsqrt(jnp.sum(keys * keys, axis=-1, keepdims=True) + 1e-06)
    unit = (keys * inv).astype(BF16)
    scores = jnp.concatenate(
        [
            dot(
                rows[(c + 1) * SPAN : (c + 2) * SPAN, :DH],
                unit[c * SPAN : (c + 2) * SPAN],
                1,
                1,
            )
            for c in range(16)
        ],
        0,
    )
    own = iota((1024, TOK), 1) == (iota((1024, TOK), 0) & (SPAN - 1)) + SPAN
    scores = jnp.where(own, MASK_FILL, scores)
    peak = jnp.max(scores, axis=-1, keepdims=True)
    total = peak + jnp.log(jnp.sum(jnp.exp(scores - peak), axis=-1, keepdims=True))
    exact = jnp.exp(scores - total)
    return keys, inv, unit, own, total, exact


def arrive(place_row_ref, j, rows):
    count = 1024 if j < 2 else SPAN
    return dot(hot(iota((count, 1), 0) == place_row_ref[j : j + 1, :]), rows, 1, 0)


def leave(place_row_ref, j, rows):
    at = hot(iota((rows.shape[0], 1), 0) == place_row_ref[j : j + 1, :])
    return dot(at, rows, 0, 0)


def attend_kernel(moved_ref, place_row_ref, sorted_out, send_out):
    q_lent = arrive(place_row_ref, 2, moved_ref[:, 4 * DH :])
    v_lent = arrive(place_row_ref, 3, moved_ref[:, 4 * DH :])
    main = arrive(place_row_ref, 0, moved_ref[:, : 2 * DH]) + arrive(
        place_row_ref, 1, moved_ref[:, 2 * DH : 4 * DH]
    )
    rows = jnp.concatenate([jnp.concatenate([q_lent, v_lent], 1), main], 0).astype(BF16)
    sorted_out[...] = rows
    _, _, _, _, total, exact = scores_of(rows)
    probs = exact.astype(BF16)
    outs = jnp.concatenate(
        [
            dot(probs[c * SPAN : (c + 1) * SPAN], rows[c * SPAN : (c + 2) * SPAN, DH:], 1, 0)
            for c in range(16)
        ],
        0,
    )
    aux = spread(total, iota((1024, TOK), 1))
    both = jnp.concatenate([outs, aux], 1).astype(BF16)
    even = leave(place_row_ref, 0, both)
    odd = leave(place_row_ref, 1, both)
    send_out[:, :DH] = even[:, :DH].astype(BF16)
    send_out[:, DH : 2 * DH] = odd[:, :DH].astype(BF16)
    lanes = iota((ROWS, TOK), 1)
    send_out[:, 2 * DH :] = either(lanes, even[:, DH:], odd[:, DH:]).astype(BF16)


def attend(moved, place_row):
    return call(
        attend_kernel,
        (moved, place_row),
        [kept((1088, 2 * DH), BF16), kept((ROWS, O_LANES), BF16)],
        in_place=(1,),
        name="attend",
    )


def by_head(ref, r, cols):
    return jnp.concatenate(
        [ref[(r * HN + h) * NW : (r * HN + h + 1) * NW, cols] for h in range(HN)], 1
    )


def merge_kernel(count, core_ref, moved_ref, rank_col_ref, *refs):
    w_refs, refs = refs[:count], refs[count:]
    send_out, o_out, share_out, merged_out = refs
    lanes = iota((TOK, TOK), 1)
    outs, logs = [], []
    for r in range(ROUNDS):
        hots = return_hots(rank_col_ref[:, r : r + 1], 2)
        aux = by_head(moved_ref, r, slice(2 * DH, 3 * DH))
        even = dot(
            hots[:, :NW], jnp.concatenate([by_head(moved_ref, r, slice(0, DH)), aux], 1), 1, 0
        )
        odd = dot(
            hots[:, NW:], jnp.concatenate([by_head(moved_ref, r, slice(DH, 2 * DH)), aux], 1), 1, 0
        )
        outs.append(even[:, :PART] + odd[:, :PART])
        o_out[r] = outs[r].astype(BF16)
        logs.append(
            [
                jnp.sum(
                    either(
                        lanes,
                        even[:, PART + h * DH : PART + (h + 1) * DH],
                        odd[:, PART + h * DH : PART + (h + 1) * DH],
                    ),
                    axis=-1,
                    keepdims=True,
                )
                for h in range(HN)
            ]
        )
    merged = []
    share_all = jnp.zeros((TOK, TOK), F32)
    for h in range(HN):
        top = jnp.maximum(logs[0][h], logs[1][h])
        e0 = jnp.exp(logs[0][h] - top)
        e1 = jnp.exp(logs[1][h] - top)
        total = e0 + e1
        cols = slice(h * DH, (h + 1) * DH)
        s0, s1 = e0 / total, e1 / total
        merged.append(s0 * outs[0][:, cols] + s1 * outs[1][:, cols])
        share_all = jnp.where(lanes == h, s0, jnp.where(lanes == HN + h, s1, share_all))
    share_out[...] = share_all
    merged = jnp.concatenate(merged, 1).astype(BF16)
    merged_out[...] = merged
    put_halves(out_of(core_ref[0], merged, w_refs), send_out)


def put_halves(pair, send_out):
    for i in range(2):
        send_out[:, i * PART : (i + 1) * PART] = pair[i].astype(BF16)


def merge(core, moved, rank_col, wo):
    args, specs = unpacked([core, moved, rank_col, wo], 1)
    return call(
        functools.partial(merge_kernel, len(wo.parts())),
        args,
        [
            kept((TOK, D), BF16),
            kept((ROUNDS, TOK, PART), BF16),
            kept((TOK, TOK), F32),
            kept((TOK, PART), BF16),
        ],
        specs=specs,
        in_place=(1, *specs),
        prefetch=1,
        name="merge",
    )


def gelu_parts(pre):
    half = 0.5 * (1.0 + lax.erf(pre * (0.5**0.5)))
    slope = half + pre * (jnp.exp(-0.5 * pre * pre) * np.float32(1.0 / np.sqrt(2.0 * np.pi)))
    return (pre * half).astype(BF16), slope.astype(BF16)


def add_up(total, more):
    return more if total is None else [a + b for a, b in zip(total, more)]


def ffn_forward(x_ref, own_ref, other_ref, gain_ref, w_ref, y_out, hf_out, act_out, slope_out):
    y = x_ref[...] + (own_ref[...].astype(F32) + other_ref[...].astype(F32))
    y_out[...] = y
    y_out.flush()
    xhat, _ = norm_parts(y)
    hf = (xhat * gain_ref[...]).astype(BF16)
    hf_out[0], hf_out[1] = hf[:, :PART], hf[:, PART:]
    total = None
    for c in range(QUAD):
        w_ref.wait(4)
        pre = dot(hf[:, :PART], w_ref.block(UP, c, 0), 1, 0) + dot(
            hf[:, PART:], w_ref.block(UP, c, 1), 1, 0
        )
        act, slope = gelu_parts(pre)
        act_out[:, c * PART : (c + 1) * PART] = act
        slope_out[:, c * PART : (c + 1) * PART] = slope
        total = add_up(total, [dot(act, w_ref.block(DOWN, c, c0), 1, 1) for c0 in range(2)])
    return total


def ffn_kernel(
    x_ref, own_ref, other_ref, gain_ref, w_ref, y_out, hf_out, act_out, slope_out, send_out
):
    put_halves(
        ffn_forward(
            x_ref, own_ref, other_ref, gain_ref, w_ref, y_out, hf_out, act_out, slope_out
        ),
        send_out,
    )


def ffn(x, own, other, gain, w):
    return run(
        ffn_kernel,
        [Far(x), Far(own), other, Far(gain), FfnWeight(w)],
        [
            Sent((TOK, D), F32),
            Sent((2, TOK, PART), BF16),
            Sent((TOK, QUAD * PART), BF16),
            Sent((TOK, QUAD * PART), BF16),
            Sent((TOK, D), BF16),
        ],
        name="ffn",
    )


def put_pieces(out_ref, at, row, rows, grad):
    for piece in range(32):
        z, tau, y = piece >> 3, (piece >> 1) & 3, piece & 1
        got = grad[piece * 16 : (piece + 1) * 16]
        if rows == 16:
            out_ref[2 * tau + at, z * 2 + y, row : row + 16] = got
        else:
            out_ref[at, z * 2 + y, row + tau * 16 : row + (tau + 1) * 16] = got


def ffn_backward(back, waits, w_ref, hf_ref, act_ref, slope_ref, send_out, grad_out):
    total = None
    for c in range(QUAD):
        if waits:
            w_ref.wait(4)
        cols = slice(c * PART, (c + 1) * PART)
        d_act = dot(back[0], w_ref.block(DOWN, c, 0), 1, 0) + dot(
            back[1], w_ref.block(DOWN, c, 1), 1, 0
        )
        d_pre = (d_act * slope_ref[:, cols].astype(F32)).astype(BF16)
        total = add_up(total, [dot(d_pre, w_ref.block(UP, c, c0), 1, 1) for c0 in range(2)])
        act = act_ref[:, cols]
        for c0 in range(2):
            put_pieces(grad_out, 2 * c + c0, 0, 64, dot(hf_ref[c0], d_pre, 0, 0).astype(BF16))
            put_pieces(grad_out, 2 * c + c0, 64, 64, dot(back[c0], act, 0, 0).astype(BF16))
        grad_out.flush()
    put_halves(total, send_out)


def turn_kernel(
    x_ref, own_ref, other_ref, gain_ref, g_ref, w_ref,
    y_out, forth_out, send_out, grad_out, hf_ref, act_ref, slope_ref
):
    put_halves(
        ffn_forward(
            x_ref, own_ref, other_ref, gain_ref, w_ref, y_out, hf_ref, act_ref, slope_ref
        ),
        forth_out,
    )
    forth_out.flush()
    back = g_ref[...].astype(BF16)
    back = [back[:, :PART], back[:, PART:]]
    ffn_backward(back, False, w_ref, hf_ref, act_ref, slope_ref, send_out, grad_out)


def turn(x, own, other, gain, g, w):
    return run(
        turn_kernel,
        [Far(x), Far(own), other, Far(gain), Far(g), FfnWeight(w)],
        [
            Sent((TOK, D), F32),
            Sent((TOK, D), BF16),
            Sent((TOK, D), BF16),
            Sent((2 * QUAD, 8, FFN_ROWS, PART), BF16, QUAD),
        ],
        temps=[
            pltpu.VMEM((2, TOK, PART), BF16),
            pltpu.VMEM((TOK, QUAD * PART), BF16),
            pltpu.VMEM((TOK, QUAD * PART), BF16),
        ],
        name="turn",
        vmem=BIG_VMEM_BYTES,
    )


def ffn_back_kernel(
    g_ref, own_ref, other_ref, x_ref, gain_ref, hf_ref, act_ref, slope_ref, w_ref, unused_ref,
    g_out, send_out, grad_out, dgain_out
):
    xhat, rstd = norm_parts(x_ref[...])
    add, dgain = norm_back(
        own_ref[...].astype(F32) + other_ref[...].astype(F32), gain_ref[...], xhat, rstd
    )
    dgain_out[...] = dgain
    g = g_ref[...] + add
    g_out[...] = g
    g_out.flush()
    back = g.astype(BF16)
    back = [back[:, :PART], back[:, PART:]]
    ffn_backward(back, True, w_ref, hf_ref, act_ref, slope_ref, send_out, grad_out)


def ffn_back(g, own, other, x, gain, more, hf, act, slope, w):
    return run(
        ffn_back_kernel,
        [
            Far(g), Far(own), other, Far(x), Far(gain),
            Far(hf), Far(act), Far(slope), FfnWeight(w), Direct(more),
        ],
        [
            Sent((TOK, D), F32),
            Sent((TOK, D), BF16),
            Sent((2 * QUAD, 8, FFN_ROWS + ATTN_ROWS, PART), BF16, QUAD),
            sds((1, D), F32),
        ],
        partial={2: (2 * QUAD, 8, FFN_ROWS, PART)},
        aliases={9: 2},
        name="ffn_back",
        vmem=BIG_VMEM_BYTES,
    )


def merge_back_kernel(count, core_ref, g_ref, own_ref, other_ref, y_ref, gain_ref, *refs):
    w_refs, refs = refs[:count], refs[count:]
    o_ref, share_ref, rank_row_ref, g_out, back_out, send_out, dgain_out = refs
    xhat, rstd = norm_parts(y_ref[...])
    add, dgain = norm_back(own_ref[...].astype(F32) + other_ref[...].astype(F32), gain_ref[...], xhat, rstd)
    dgain_out[...] = dgain
    g = g_ref[...] + add
    g_out[...] = g
    back_out[0] = g[:, :PART].astype(BF16)
    back_out[1] = g[:, PART:].astype(BF16)
    dout = into(core_ref[0], g, w_refs)
    share = share_ref[...]
    o0 = o_ref[0].astype(F32)
    o1 = o_ref[1].astype(F32)
    lanes = iota((TOK, TOK), 1)
    parts = [[], []]
    logs = [[], []]
    for h in range(HN):
        cols = slice(h * DH, (h + 1) * DH)
        s0 = share[:, h : h + 1]
        s1 = share[:, HN + h : HN + h + 1]
        dh = dout[:, cols]
        t0 = jnp.sum(dh * o0[:, cols], axis=-1, keepdims=True)
        t1 = jnp.sum(dh * o1[:, cols], axis=-1, keepdims=True)
        mean = s0 * t0 + s1 * t1
        parts[0].append(s0 * dh)
        parts[1].append(s1 * dh)
        logs[0].append(spread(s0 * (t0 - mean), lanes))
        logs[1].append(spread(s1 * (t1 - mean), lanes))
    lanes = iota((NW, TOK), 1)
    for r in range(ROUNDS):
        moved = dot(
            send_hots(rank_row_ref[r : r + 1, :], 2),
            jnp.concatenate(parts[r] + logs[r], 1).astype(BF16),
            1,
            0,
        )
        even, odd = moved[:NW], moved[NW:]
        for h in range(HN):
            rows = slice((r * HN + h) * NW, (r * HN + h + 1) * NW)
            cols = slice(h * DH, (h + 1) * DH)
            aux = slice(PART + h * DH, PART + (h + 1) * DH)
            send_out[rows, :DH] = even[:, cols].astype(BF16)
            send_out[rows, DH : 2 * DH] = odd[:, cols].astype(BF16)
            send_out[rows, 2 * DH :] = either(lanes, even[:, aux], odd[:, aux]).astype(BF16)


def merge_back(core, g, own, other, y, gain, wo, o, share, rank_row):
    args, specs = unpacked([core, g, own, other, y, gain, wo, o, share, rank_row], 1)
    return call(
        functools.partial(merge_back_kernel, len(wo.parts())),
        args,
        [
            kept((TOK, D), F32),
            kept((2, TOK, PART), BF16),
            kept((ROWS, O_LANES), BF16),
            sds((1, D), F32),
        ],
        specs=specs,
        in_place=(0, 1, 3, *specs, *range(len(args) - 4, len(args) - 1)),
        prefetch=1,
        name="merge_back",
    )


def attend_back_kernel(moved_ref, sorted_ref, place_row_ref, gain_ref, send_out):
    lanes = iota((ROWS, TOK), 1)
    aux = moved_ref[:, 2 * DH :].astype(F32)
    got = jnp.zeros((1024, 2 * DH), F32)
    for j in range(2):
        here = jnp.where(lanes >> 3 == j, aux, 0.0).astype(BF16)
        pair = jnp.concatenate([moved_ref[:, j * DH : (j + 1) * DH], here], 1)
        got = got + arrive(place_row_ref, j, pair)
    d_out = got[:, :DH].astype(BF16)
    d_log = jnp.sum(got[:, DH:], axis=-1, keepdims=True)
    rows = sorted_ref[...]
    keys, inv, unit, own, _, exact = scores_of(rows)
    probs = exact.astype(BF16)
    g_probs = jnp.concatenate(
        [
            dot(d_out[c * SPAN : (c + 1) * SPAN], rows[c * SPAN : (c + 2) * SPAN, DH:], 1, 1)
            for c in range(16)
        ],
        0,
    )
    inner_sum = jnp.sum(g_probs * exact, axis=-1, keepdims=True)
    g_scores = exact * (g_probs - inner_sum + d_log)
    g_scores = jnp.where(own, 0.0, g_scores).astype(BF16)
    d_query, d_unit, d_value = [], [], []
    for c in range(16):
        here = slice(c * SPAN, (c + 1) * SPAN)
        both = slice(c * SPAN, (c + 2) * SPAN)
        after = slice((c + 1) * SPAN, (c + 2) * SPAN)
        d_query.append(dot(g_scores[here], unit[both], 1, 0))
        d_unit.append(dot(g_scores[here], rows[after, :DH], 0, 0))
        d_value.append(dot(probs[here], d_out[here], 0, 0))

    def overlap(parts):
        out = [parts[0][:SPAN]]
        for c in range(15):
            out.append(parts[c][SPAN:] + parts[c + 1][:SPAN])
        out.append(parts[15][SPAN:])
        return jnp.concatenate(out, 0)

    g_unit = overlap(d_unit)
    along = jnp.sum(g_unit * keys, axis=-1, keepdims=True)
    g_keys = inv * g_unit - keys * (inv * inv * inv) * along
    g_query = jnp.concatenate([jnp.zeros((SPAN, DH), F32)] + d_query, 0) + g_keys
    grads = jnp.concatenate([g_query, overlap(d_value)], 1).astype(BF16)
    for j in range(2):
        cols = slice(j * 2 * DH, (j + 1) * 2 * DH)
        send_out[:, cols] = leave(place_row_ref, j, grads[SPAN:]).astype(BF16)
    lent = leave(place_row_ref, 2, grads[:SPAN, :DH]) + leave(place_row_ref, 3, grads[:SPAN, DH:])
    b = iota((ROWS, 1), 0) & 7
    for q in range(4):
        lent = jnp.where(b == 4 + q, gain_ref[:, q * DH : (q + 1) * DH], lent)
    send_out[:, 4 * DH :] = lent.astype(BF16)


def attend_back(moved, rows, place_row, gain):
    return call(
        attend_back_kernel,
        (moved, rows, place_row, gain),
        [kept((ROWS, QV_LANES), BF16)],
        in_place=(1, 2),
        name="attend_back",
    )[0]


def project_back_kernel(count, grads, core_ref, moved_ref, rank_col_ref, *refs):
    q_refs, v_refs = refs[:count], refs[count : 2 * count]
    refs = refs[2 * count :]
    if grads:
        back_ref, merged_ref, hn_ref, *refs = refs
        send_out, grad_out, gain_out, grad_ref, sems = refs
    else:
        send_out, dq_out, dv_out, gain_out = refs
    gain_out[...] = dot(
        hot(iota((8, 1), 0) == (iota((1, ROWS), 1) & 7)), moved_ref[:, 4 * DH :], 1, 0
    )
    total = jnp.zeros((TOK, HN * 2 * DH), F32)
    lent_q = jnp.zeros((TOK, PART), F32)
    lent_v = jnp.zeros((TOK, PART), F32)
    for r in range(ROUNDS):
        hots = return_hots(rank_col_ref[:, r : r + 1])
        total = total + dot(hots[:, :NW], by_head(moved_ref, r, slice(0, 2 * DH)), 1, 0)
        total = total + dot(hots[:, NW : 2 * NW], by_head(moved_ref, r, slice(2 * DH, 4 * DH)), 1, 0)
        lent = by_head(moved_ref, r, slice(4 * DH, 5 * DH))
        lent_q = lent_q + dot(hots[:, 2 * NW : 3 * NW], lent, 1, 0)
        lent_v = lent_v + dot(hots[:, 3 * NW :], lent, 1, 0)
    d_q = jnp.concatenate([total[:, h * 2 * DH : h * 2 * DH + DH] for h in range(HN)], 1)
    d_v = jnp.concatenate([total[:, h * 2 * DH + DH : (h + 1) * 2 * DH] for h in range(HN)], 1)
    d_q = (d_q + lent_q).astype(BF16)
    d_v = (d_v + lent_v).astype(BF16)
    if grads:
        for c0 in range(2):
            for i, (left, right) in enumerate(
                ((back_ref, merged_ref[...]), (hn_ref, d_q), (hn_ref, d_v))
            ):
                put_pieces(grad_ref, c0, i * 16, 16, dot(left[c0], right, 0, 0).astype(BF16))
        sending = pltpu.make_async_copy(
            grad_ref, grad_out.at[:, :, pl.ds(FFN_ROWS, ATTN_ROWS), :], sems.at[0]
        )
        sending.start()
    else:
        dq_out[...] = d_q
        dv_out[...] = d_v
    core = core_ref[0]
    from_q = out_of(core, d_q, q_refs)
    from_v = out_of(core, d_v, v_refs)
    put_halves([a + b for a, b in zip(from_q, from_v)], send_out)
    if grads:
        sending.wait()


def project_back(core, moved, rank_col, wq, wv, lefts=None):
    args, specs = unpacked([core, moved, rank_col, wq, wv, *(lefts or ())], 1)
    out_specs = {}
    if lefts:
        rows = FFN_ROWS + ATTN_ROWS
        outs = [kept((2 * QUAD, 8, rows, PART), BF16)]
        out_specs = {1: pl.BlockSpec(memory_space=pl.ANY)}
        temps = [pltpu.VMEM((2 * QUAD, 8, ATTN_ROWS, PART), BF16), pltpu.SemaphoreType.DMA((1,))]
    else:
        outs = [kept((TOK, PART), BF16)] * 2
        temps = []
    return call(
        functools.partial(project_back_kernel, len(wq.parts()), lefts is not None),
        args,
        [kept((TOK, D), BF16), *outs, sds((8, DH), F32)],
        specs=specs,
        out_specs=out_specs,
        scratch=temps,
        in_place=range(1, len(args) - 1),
        prefetch=1,
        name="project_back",
    )


def last_kernel(g_ref, own_ref, other_ref, x_ref, gain_ref, g_out, dgain_out):
    xhat, rstd = norm_parts(x_ref[...])
    add, dgain = norm_back(own_ref[...].astype(F32) + other_ref[...].astype(F32), gain_ref[...], xhat, rstd)
    g_out[...] = g_ref[...] + add
    dgain_out[...] = dgain


def last(g, own, other, x, gain):
    return call(
        last_kernel,
        (g, own, other, x, gain),
        [kept((TOK, D), F32), sds((1, D), F32)],
        in_place=(0, 1, 3),
        name="last",
    )


def pair_dot(left_a, left_b, right_a, right_b):
    left = jnp.concatenate([left_a, left_b], 0)
    right = jnp.concatenate([right_a, right_b], 0)
    return dot(left, right, 0, 0).astype(BF16)


def attn_grad_kernel(count, core_ref, *refs):
    out_ref = refs[-1]
    for i in range(count):
        la, lb, ra, rb = refs[4 * i : 4 * i + 4]
        got = pair_dot(la[0], lb[0], ra[...], rb[...])
        out_ref[:, i * 16 : (i + 1) * 16] = got.reshape(32, 16, PART)


def attn_grad(core, pairs):
    half = pl.BlockSpec((1, TOK, PART), lambda i, core: (core[0], 0, 0))
    args = [a for left, right in pairs for a in (*left, *right)]
    specs = {4 * i + j: half for i in range(len(pairs)) for j in range(2)}
    return call(
        functools.partial(attn_grad_kernel, len(pairs)),
        (core, *args),
        [kept((32, 16 * len(pairs), PART), BF16)],
        specs=specs,
        prefetch=1,
        in_place=range(0, len(args), 2),
        name="attn_grad",
    )[0]


def swap_narrow(values):
    return lax.ppermute(values, "narrow", [(0, 1), (1, 0)])


def with_core(values):
    other = lax.ppermute(values, "wide", [(i, i ^ 1) for i in range(NW)])
    return values, other


def to_all(values):
    return lax.all_to_all(values, "wide", split_axis=0, concat_axis=0, tiled=True)


SAME_CORE = [
    [y * 32 + z * 8 + x * 2 + c for z in range(4) for x in range(4) for y in range(2)]
    for c in range(2)
]
LAYER_OF_Y = [[y * 32 + i for i in range(NW // 2)] for y in range(2)]


def summed(values):
    return jnp.sum(to_same_core(values).astype(F32), axis=0).astype(BF16)


ALONG_X_AND_CORE = [[hi * 8 + i for i in range(8)] for hi in range(8)]
ALONG_Z_AND_Y = [
    [y * 32 + z * 8 + i for z in range(4) for y in range(2)] for i in range(8)
]
ALONG_Z = [
    [y * 32 + z * 8 + x * 2 + c for z in range(4)] for y in range(2) for x in range(4) for c in range(2)
]


def summed_along_x(values):
    return lax.psum_scatter(
        values, "wide", scatter_dimension=0, tiled=True, axis_index_groups=ALONG_X_AND_CORE
    ).reshape(values.shape[1:])


def summed_across_x(values):
    moved = lax.all_to_all(
        values, "wide", split_axis=0, concat_axis=0, tiled=True, axis_index_groups=ALONG_Z_AND_Y
    )
    return jnp.sum(moved.astype(F32), axis=0).astype(BF16)


def summed_along_z(values):
    return lax.psum_scatter(
        values, "wide", scatter_dimension=0, tiled=True, axis_index_groups=ALONG_Z
    )


def summed_along_y(values):
    y = lax.axis_index("wide") >> 5
    mine = lax.dynamic_index_in_dim(values, y, keepdims=False)
    theirs = lax.dynamic_index_in_dim(values, 1 - y, keepdims=False)
    got = lax.ppermute(theirs, "wide", [(i, i ^ 32) for i in range(NW)])
    return (mine.astype(F32) + got.astype(F32)).astype(BF16)


def to_same_core(values):
    return lax.all_to_all(
        values, "wide", split_axis=0, concat_axis=0, tiled=True, axis_index_groups=SAME_CORE
    )


def after(values, *others):
    return lax.optimization_barrier((values, others))[0]


def gathered(rows):
    got = lax.all_gather(rows, "wide", axis=0, tiled=True, axis_index_groups=LAYER_OF_Y)
    return got.reshape(QUAD, QUAD, 2, rows.shape[0], PART)


def moved_rows(rows):
    return to_all(rows.reshape(NW, rows.shape[0] // NW, -1)).reshape(rows.shape)


def on_device(
    x_first,
    x_second,
    grad_first,
    grad_second,
    sort_target,
    owner,
    master,
    moment_first,
    moment_second,
    gains,
    gain_first,
    gain_second,
):
    me = lax.axis_index("wide").astype(I32)
    half = lax.axis_index("narrow").astype(I32).reshape(1)
    core = (me & 1).reshape(1)
    owner_row = owner.reshape(1, TILES)

    routed = route_out(me.reshape(1), owner_row, master)
    sort_target, held = after((sort_target, owner), routed)
    moved = moved_rows(routed)
    chunks = []
    for l in range(LAYERS):
        of = held[l * 88 : (l + 1) * 88]
        chunks += [of[at : at + 32].reshape(8, 4).T.reshape(4, 8) for at in (24, 56)]
        chunks += [of[16:24].reshape(1, 8), of[:16].reshape(2, 8)]
    holder = jnp.repeat(jnp.concatenate(chunks), 2, axis=1)
    e = np.arange(16, dtype=np.int32)[None] & 1
    code_row = ((holder // CAP) * PACK + (holder % CAP) * 2 + e).reshape(1, -1)
    there = (holder // CAP) * WIDE_PACK + (holder % CAP) * 4 + e
    both = jnp.stack([there, there + 2], 1)
    mine_only = there + 2 * (me >> 5)
    code_col = jnp.concatenate(
        [
            both[:9].reshape(-1),
            both[19:].reshape(-1),
            both[11:19].reshape(-1),
            mine_only[9:11].reshape(-1),
        ]
    ).reshape(-1, 1)
    mine = lax.dynamic_slice_in_dim(sort_target, me * TOK, TOK, axis=2).reshape(-1, TOK)
    by_source = lax.dynamic_index_in_dim(sort_target, me >> 5, 1, keepdims=False)
    plans = plan((me & 7).reshape(1), mine, by_source.reshape(LAYERS, NW, TOK))
    rank_rows, rank_cols, place_rows = [plans[i::3] for i in range(3)]
    flat_gains = gains.reshape(LAYERS * 2, PART)
    x_two, gain_rows = inner(
        half, [(x_second, swap_narrow(x_second)), (flat_gains, swap_narrow(flat_gains))], "inner_a"
    )
    moved = after(moved, code_col, code_row, plans, x_two, gain_rows)
    first_rows, early_rows, late_rows = pick(code_col, moved)
    x_first, grad_first, grad_second = after((x_first, grad_first, grad_second), x_two)
    pairs = [(a, swap_narrow(a)) for a in (x_first, grad_first, grad_second)]
    first_w = with_core(after(to_same_core(first_rows), pairs))
    early = gathered(early_rows)
    late = gathered(late_rows)
    x_one, g_one, g_two = inner(half, pairs, "inner_b")
    w_ffn = [early, late]
    w_attn = [
        [Weight(8, early), Weight(0, *first_w), Weight(1, *first_w)],
        [Weight(9, early), Weight(10, early), Weight(11, early)],
    ]
    gain = [[gain_rows[2 * l + i].reshape(1, D) for i in range(2)] for l in range(LAYERS)]

    saved = []
    pending = None
    for l in range(LAYERS):
        w_out, w_qk, w_value = w_attn[l]
        x_two, hn, send = project(core, x_two, pending, gain[l][0], w_qk, w_value, rank_rows[l])
        moved = moved_rows(send)
        if l == 0:
            moved = after(moved, x_one, g_one, g_two)
        rows, send = attend(moved, place_rows[l])
        moved = moved_rows(send)
        send, o, share, merged = merge(core, moved, rank_cols[l], w_out)
        stream = (x_one, send, swap_narrow(send), gain[l][1])
        if l < LAYERS - 1:
            x_one, *for_ffn, send_f = ffn(*stream, w_ffn[l])
        else:
            x_one, send_f, send, ffn_part = turn(*stream, g_two, w_ffn[l])
        pending = (send_f, swap_narrow(send_f))
        saved.append((x_two, x_one, hn, rows, o, share, merged))
    y_two = x_two + (pending[0].astype(F32) + pending[1].astype(F32))
    y_first, y_second = outer(half, (x_one, y_two), "outer_y")

    pending = None
    dgains = [[None, None], [None, None]]
    gain_sums = []
    for l in reversed(range(LAYERS)):
        x_in, y_mid, hn, rows, o, share, merged = saved[l]
        w_out, w_qk, w_value = w_attn[l]
        if l < LAYERS - 1:
            g_two, send, ffn_part, dgains[l + 1][0] = ffn_back(
                g_two, *pending, *for_ffn, w_ffn[l]
            )
        other = swap_narrow(send)
        ffn_part = summed_along_x(ffn_part)
        if l == 0:
            other = after(other, ffn_rows)
            ffn_rows = summed_along_y(ffn_rows)
        g_one, back, send, dgains[l][1] = merge_back(
            core, g_one, send, other, y_mid, gain[l][1], w_out, o, share, rank_rows[l]
        )
        moved = moved_rows(send)
        if l > 0:
            moved = after(moved, y_first, y_second)
            half_gain = dgains[1][1][:, :PART]
        else:
            dx_first = outer(half, (g_one,), "outer_dx_first")[0]
            moved = after(moved, dx_first, ffn_rows)
            half_gain = dgains[1][1][:, PART:]
        send = attend_back(moved, rows, place_rows[l], half_gain)
        moved = moved_rows(send)
        if l > 0:
            moved = after(moved, ffn_part)
        if l > 0:
            send, attn_part, gain_sum = project_back(
                core, moved, rank_cols[l], w_qk, w_value, (back, merged, hn)
            )
            ffn_rows = summed_along_z(after(ffn_part, moved))
        else:
            send, dq, dv, gain_sum = project_back(core, moved, rank_cols[l], w_qk, w_value)
            hn2 = with_core(hn)
            pairs = [(with_core(back), with_core(merged)), (hn2, with_core(dq)), (hn2, with_core(dv))]
            attn_part = attn_grad(core, pairs)
            attn_rows = summed(attn_part)
        other = swap_narrow(send)
        if l == 0:
            ffn_part = after(ffn_part, attn_part)
            last_rows = summed_along_y(summed_along_z(ffn_part[:, FFN_ROWS:]))
            both_rows = summed_across_x(after(ffn_part[:, :FFN_ROWS], other))
        gain_sums.append(gain_sum[4:].reshape(1, PART))
        pending = (send, other, x_in, gain[l][0], attn_part)
    g_two, dgains[0][0] = last(g_two, *pending[:4])
    dx_second = outer(half, (g_two,), "outer_dx_second")[0]
    parts = (both_rows, attn_rows, ffn_rows, last_rows)
    back_rows = moved_rows(
        route_back(code_row, parts, (dgains[1][0], dgains[0][1], dgains[0][0]))
    )
    back_rows = after(back_rows, dx_second)
    slot_grad, slot_first, slot_second, slot_new, *gain_news = slots_update(
        half,
        me.reshape(1),
        owner_row,
        back_rows,
        jnp.concatenate(gain_sums, 1),
        master,
        moment_first,
        moment_second,
        gains,
        gain_first,
        gain_second,
    )
    gain_grad, gain_first_new, gain_second_new, gain_new = gain_news
    return (
        y_first,
        y_second,
        dx_first,
        dx_second,
        slot_grad,
        slot_first,
        slot_second,
        slot_new,
        gain_grad,
        gain_first_new,
        gain_second_new,
        gain_new,
    )


def solution(mesh):
    rows = P("wide", "narrow")
    tiles = P("wide", None, "narrow")
    gains = P(None, None, "narrow")
    return jax.shard_map(
        on_device,
        mesh=mesh,
        in_specs=(rows,) * 4 + (P(), P()) + (tiles,) * 3 + (gains,) * 3,
        out_specs=(rows,) * 4 + (tiles,) * 4 + (gains,) * 4,
        check_vma=False,
    )
```

```python
import functools

import jax
import jax.numpy as jnp
import numpy as np
from jax import lax
from jax.experimental import pallas as pl
from jax.experimental.pallas import tpu as pltpu
from jax.sharding import PartitionSpec as P

D = 1024
PART = 512
DH = 128
HN = 4
SPAN = 64
TR = 128
CAP = 5
TILES = 176
TOK = 128
NW = 64
LAYERS = 2
ROUNDS = 2
STEP = 5
GROUPS = 8
QV_LANES = 5 * DH
O_LANES = 3 * DH
ROWS = NW * 8
PACK = 16
WIDE_PACK = 24
PAIR_ROWS = WIDE_PACK * (NW // 2)
QUAD = 4
UP, DOWN = 0, 1
LAYER_ROWS = 176
ATTN_ROWS = 48
FFN_ROWS = 128
SPLIT = 96
EARLY_ROWS = 384

MASK_FILL = -1000000000.0
NORM_EPS = 1e-05
BETA_ONE = 0.5
BETA_TWO = 0.5
RATE_WEIGHT = 0.05
RATE_GAIN = 0.2
DECAY = 0.01
EPSILON = 1e-08

F32 = jnp.float32
BF16 = jnp.bfloat16
I32 = jnp.int32
VMEM_BYTES = 20 * 1024 * 1024
BIG_VMEM_BYTES = 32 * 1024 * 1024


def feature_of(p):
    c0 = p >> 9
    z = (p >> 7) & 3
    tau = (p >> 5) & 3
    y = (p >> 4) & 1
    t = (p >> 1) & 7
    e = p & 1
    return t * 128 + tau * 32 + c0 * 16 + (y * 4 + z) * 2 + e


def iota(shape, dim):
    return lax.broadcasted_iota(I32, shape, dim)


def hot(mask):
    return jnp.where(mask, 1.0, 0.0).astype(BF16)


def dot(a, b, ca, cb):
    return lax.dot_general(a, b, (((ca,), (cb,)), ((), ())), preferred_element_type=F32)


def in_hbm(array):
    return pltpu.with_memory_space_constraint(array, pltpu.MemorySpace.HBM)


def call(
    kernel, args, outs, grid=(1,), specs=None, out_specs=None, scratch=(), prefetch=0, in_place=(), name=None
):
    specs = specs or {}
    out_specs = out_specs or {}
    gains = {i: a.index for i, a in enumerate(args) if isinstance(a, Gain)}
    args = [a.rows if isinstance(a, Gain) else a for a in args]
    if gains:
        inner_kernel_body = kernel

        def kernel(*refs):
            inner_kernel_body(
                *[GainRow(r, gains[i]) if i in gains else r for i, r in enumerate(refs)]
            )

    def whole(shape):
        zeros = (0,) * len(shape)
        return pl.BlockSpec(shape, lambda *_: zeros)
    in_list = [specs.get(i, whole(a.shape)) for i, a in enumerate(args[prefetch:])]
    args = [in_hbm(a) if i - prefetch in in_place else a for i, a in enumerate(args)]
    out_list = [out_specs.get(i, whole(o.shape)) for i, o in enumerate(outs)]
    return pl.pallas_call(
        kernel,
        out_shape=outs,
        grid_spec=pltpu.PrefetchScalarGridSpec(
            num_scalar_prefetch=prefetch,
            grid=grid,
            in_specs=in_list,
            out_specs=out_list,
            scratch_shapes=list(scratch),
        ),
        compiler_params=pltpu.CompilerParams(vmem_limit_bytes=VMEM_BYTES),
        name=name,
    )(*args)


def sds(shape, dtype):
    return jax.ShapeDtypeStruct(shape, dtype)


def kept(shape, dtype):
    return pltpu.MemorySpace.HBM(shape, dtype)


def norm_parts(values):
    mean = jnp.mean(values, axis=-1, keepdims=True)
    var = jnp.mean(values * values, axis=-1, keepdims=True) - mean * mean
    rstd = lax.rsqrt(var + NORM_EPS)
    return (values - mean) * rstd, rstd


def norm_back(upstream, gain, xhat, rstd):
    gh = upstream * gain
    m1 = jnp.mean(gh, axis=-1, keepdims=True)
    m2 = jnp.mean(gh * xhat, axis=-1, keepdims=True)
    return rstd * (gh - m1 - xhat * m2), jnp.sum(upstream * xhat, axis=0, keepdims=True)


def flat(ref):
    return ref[...].reshape(PART, PART)


def halves(core, first, second):
    mine = core == 0
    return jnp.where(mine, first, second), jnp.where(mine, second, first)


class Gain:
    def __init__(self, rows, index):
        self.rows, self.index = rows, index


class GainRow:
    def __init__(self, ref, index):
        self.ref, self.index = ref, index

    def __getitem__(self, index):
        return self.ref[self.index : self.index + 1, :]


class Far:
    def __init__(self, array):
        self.row = None
        if isinstance(array, Gain):
            array, self.row = array.rows, array.index
        self.operands = [in_hbm(array)]
        self.scratch = [pltpu.VMEM(array.shape, array.dtype), pltpu.SemaphoreType.DMA((1,))]

    def fetch(self, refs, buffer, sems):
        return [pltpu.make_async_copy(refs[0], buffer, sems.at[0])]


class FfnWeight(Far):
    def __init__(self, array):
        self.operands = [in_hbm(array)]
        self.scratch = [
            pltpu.VMEM((2, QUAD, 2, QUAD, FFN_ROWS, PART), BF16),
            pltpu.SemaphoreType.DMA((16,)),
        ]

    def fetch(self, refs, buffer, sems):
        copies = []
        for c in range(QUAD):
            for part in range(2):
                for c0 in range(2):
                    source = refs[0].at[:, c, c0, pl.ds(part * FFN_ROWS, FFN_ROWS), :]
                    copies.append(
                        pltpu.make_async_copy(source, buffer.at[part, c, c0], sems.at[len(copies)])
                    )
        return copies


class Direct(Far):
    def __init__(self, array):
        self.operands = [in_hbm(array)]
        self.scratch = []


class FarSlots(Far):
    def __init__(self, array):
        self.operands = [in_hbm(array)]
        self.scratch = [pltpu.VMEM(array.shape, array.dtype), pltpu.SemaphoreType.DMA((CAP,))]

    def fetch(self, refs, buffer, sems):
        return [
            pltpu.make_async_copy(refs[0].at[s], buffer.at[s], sems.at[s]) for s in range(CAP)
        ]


class Fetched:
    def __init__(self, copies, buffer):
        self.copies = list(copies)
        self.buffer = buffer
        for copy in self.copies:
            copy.start()

    def wait(self, count=None):
        count = len(self.copies) if count is None else count
        for copy in self.copies[:count]:
            copy.wait()
        self.copies = self.copies[count:]

    def __getitem__(self, index):
        self.wait()
        return self.buffer[index]

    def halves(self):
        self.wait()
        return [self.buffer[i].reshape(PART, PART) for i in range(2)]

    def block(self, part, c, c0):
        return self.buffer[part, c, c0].reshape(PART, PART)


class Sent:
    def __init__(self, shape, dtype, pieces=1):
        self.shape, self.dtype, self.pieces = shape, dtype, pieces


class Sending:
    def __init__(self, target, buffer, sems, pieces):
        self.target, self.buffer, self.sems, self.pieces = target, buffer, sems, pieces
        self.copies = []

    def __setitem__(self, index, value):
        self.buffer[index] = value

    def flush(self):
        k = len(self.copies)
        size = self.target.shape[0] // self.pieces
        rows = pl.ds(k * size, size)
        source, target = self.buffer.at[rows], self.target.at[rows]
        if source.shape != target.shape:
            target = target.at[:, :, pl.ds(0, self.buffer.shape[2]), :]
        copy = pltpu.make_async_copy(source, target, self.sems.at[k])
        copy.start()
        self.copies.append(copy)

    def flush_all(self):
        while len(self.copies) < self.pieces:
            self.flush()

    def wait(self):
        for copy in self.copies:
            copy.wait()


def run(kernel, args, outs, prefetch=0, name=None, vmem=None, partial=None, temps=(), aliases=None):
    operands, in_specs, scratch = [], [], []
    for i, a in enumerate(args):
        if isinstance(a, Far):
            operands += a.operands
            in_specs += [pl.BlockSpec(memory_space=pl.ANY)] * len(a.operands)
            scratch += a.scratch
        else:
            operands.append(a)
            if i >= prefetch:
                zeros = (0,) * a.ndim
                in_specs.append(pl.BlockSpec(a.shape, lambda *_, zeros=zeros: zeros))
    out_shapes, out_specs = [], []
    for i, o in enumerate(outs):
        if isinstance(o, Sent):
            out_shapes.append(kept(o.shape, o.dtype))
            out_specs.append(pl.BlockSpec(memory_space=pl.ANY))
            shape = (partial or {}).get(i, o.shape)
            scratch += [pltpu.VMEM(shape, o.dtype), pltpu.SemaphoreType.DMA((o.pieces,))]
        else:
            zeros = (0,) * len(o.shape)
            out_shapes.append(o)
            out_specs.append(pl.BlockSpec(o.shape, lambda *_, zeros=zeros: zeros))

    def body(*refs):
        ins, rest = list(refs[: len(operands)]), list(refs[len(operands) :])
        out_refs, temps = rest[: len(outs)], rest[len(outs) :]
        seen = []
        for a in args:
            if isinstance(a, Far):
                mine = [ins.pop(0) for _ in a.operands]
                if a.scratch:
                    buffer, sems = temps.pop(0), temps.pop(0)
                    got = Fetched(a.fetch(mine, buffer, sems), buffer)
                    row = getattr(a, "row", None)
                    seen.append(got if row is None else GainRow(got, row))
                else:
                    seen.append(mine[0])
            else:
                seen.append(ins.pop(0))
        sending = []
        for o, ref in zip(outs, out_refs):
            if isinstance(o, Sent):
                ref = Sending(ref, temps.pop(0), temps.pop(0), o.pieces)
                sending.append(ref)
            seen.append(ref)
        kernel(*seen, *temps)
        for ref in sending:
            ref.flush_all()
        for ref in sending:
            ref.wait()

    return pl.pallas_call(
        body,
        out_shape=out_shapes,
        grid_spec=pltpu.PrefetchScalarGridSpec(
            num_scalar_prefetch=prefetch,
            grid=(1,),
            in_specs=in_specs,
            out_specs=out_specs,
            scratch_shapes=[*scratch, *temps],
        ),
        compiler_params=pltpu.CompilerParams(vmem_limit_bytes=vmem or VMEM_BYTES),
        input_output_aliases=aliases or {},
        name=name,
    )(*operands)


class Weight:
    def __init__(self, index, *arrays):
        self.index = index
        self.arrays = arrays

    def parts(self):
        index = self.index
        if len(self.arrays) == 2:
            return [
                (a, pl.BlockSpec((8, 16, PART), lambda *_, z=z: (z, index, 0)))
                for a in self.arrays
                for z in range(4)
            ]
        return [
            (self.arrays[0], pl.BlockSpec((1, QUAD, 2, 32, PART), lambda *_, z=z: (z, 0, 0, index, 0)))
            for z in range(4)
        ]


def rows_of(refs):
    return jnp.concatenate([r[...].reshape(-1, PART) for r in refs], 0)


def weight_halves(core, refs):
    if len(refs) == 4:
        return [
            jnp.concatenate([r[0, :, c0].reshape(-1, PART) for r in refs], 0) for c0 in range(2)
        ]
    return rows_of(refs[:4]), rows_of(refs[4:])


def into(core, full, refs):
    first, second = full[:, :PART], full[:, PART:]
    if len(refs) == 8:
        first, second = halves(core, first, second)
    w = weight_halves(core, refs)
    return dot(first.astype(BF16), w[0], 1, 0) + dot(second.astype(BF16), w[1], 1, 0)


def out_of(core, part, refs):
    w = weight_halves(core, refs)
    pair = dot(part, w[0], 1, 1), dot(part, w[1], 1, 1)
    return pair if len(refs) == 4 else halves(core, *pair)


def unpacked(args, prefetch):
    out, specs = [], {}
    for a in args:
        if isinstance(a, Weight):
            for array, spec in a.parts():
                specs[len(out) - prefetch] = spec
                out.append(array)
        else:
            out.append(a)
    return out, specs


def wanted(shape, dim):
    m = iota(shape, dim)
    g16 = (m >> 3) * 16
    b = m & 7
    before = (g16 - 2) & 127
    lent = before + (b >> 1)
    return (
        g16 + 2 * b,
        g16 + 2 * b + 1,
        jnp.where((b == 0) | (b == 2), lent, -1),
        jnp.where((b == 1) | (b == 3), lent, -1),
    )


def send_hots(rank_row, count=4):
    return hot(jnp.concatenate(wanted((NW, 1), 0)[:count], 0) == rank_row)


def return_hots(rank_col, count=4):
    return hot(rank_col == jnp.concatenate(wanted((1, NW), 1)[:count], 1))


def spread(col, lanes):
    hi, mid, lo = pieces(col)
    k = lanes & 7
    return jnp.where(k == 0, hi, jnp.where(k == 1, mid, jnp.where(k == 2, lo, 0.0)))


def pieces(col):
    hi = col.astype(BF16).astype(F32)
    rest = col - hi
    mid = rest.astype(BF16).astype(F32)
    return hi, mid, rest - mid


def either(lanes, even, odd):
    return jnp.where(lanes < 8, even, jnp.where(lanes < 16, odd, 0.0))


def slot_kinds(owner_ref, me):
    lane = iota((1, TILES), 1)
    ffn = jnp.where(lane >= TILES // LAYERS, lane - TILES // LAYERS, lane) >= 24
    return [
        jnp.max(
            jnp.where((owner_ref[...] == me * CAP + s) & ffn, 1, 0), axis=1, keepdims=True
        )
        for s in range(CAP)
    ]


def row_of_slots(kinds):
    r = iota((1, TR), 1)

    def place(low, x):
        j3 = (low >> 1) & 7
        device = (j3 & 3) * 8 + x * 2 + (low >> 4)
        return device * WIDE_PACK + (j3 >> 2) * 2 + (low & 1)

    attn = place(r & 31, r >> 5)
    ffn = place(r >> 2, r & 3)
    return jnp.concatenate([jnp.where(k == 1, ffn, attn) + 4 * s for s, k in enumerate(kinds)], 1)


def slot_of_row(kinds):
    r = iota((1, NW * PACK), 1)
    d, m = r >> 4, r & (PACK - 1)
    s, e = m >> 1, m & 1
    tau = (d >> 1) & 3
    low = (d & 1) * 16 + (d >> 3) * 2 + e
    out = jnp.full((1, NW * PACK), -1, I32)
    for i, k in enumerate(kinds):
        out = jnp.where(s == i, i * TR + jnp.where(k == 1, low * 4 + tau, tau * 32 + low), out)
    return out


def route_out_kernel(me_ref, owner_ref, master_ref, out_ref):
    tiles = master_ref[...].reshape(CAP * TR, PART).astype(BF16)
    place = row_of_slots(slot_kinds(owner_ref, me_ref[0]))
    rows = dot(hot(iota((PAIR_ROWS, 1), 0) == place), tiles, 1, 0).astype(BF16)
    out_ref[:PAIR_ROWS] = rows
    out_ref[PAIR_ROWS:] = rows


def route_out(me, owner_row, master):
    return call(
        route_out_kernel,
        (me, owner_row, master),
        [kept((2 * PAIR_ROWS, PART), BF16)],
        prefetch=1,
        in_place=(1,),
        name="route_out",
    )[0]


def pick_kernel(code_ref, moved_ref, first_ref, early_ref, late_ref):
    picked = hot(code_ref[...] == iota((1, 2 * PAIR_ROWS), 1))
    rows = dot(picked, moved_ref[...], 1, 0).astype(BF16)
    early_ref[...] = rows[:EARLY_ROWS]
    late_ref[...] = rows[EARLY_ROWS : EARLY_ROWS + 2 * FFN_ROWS]
    first = rows[EARLY_ROWS + 2 * FFN_ROWS :]
    first_ref[...] = jnp.broadcast_to(first[None], first_ref.shape)


def pick(code_col, moved):
    return call(
        pick_kernel,
        (code_col, moved),
        [
            kept((32, 32, PART), BF16),
            kept((EARLY_ROWS, PART), BF16),
            kept((2 * FFN_ROWS, PART), BF16),
        ],
        name="pick",
    )


def route_back_kernel(code_ref, *refs):
    first, last_rows, attn, ffn, gain_a, gain_b, gain_c, out_ref = refs
    at = FFN_ROWS - SPLIT
    rows = jnp.concatenate([first[...], last_rows[:at], attn[...], ffn[...], last_rows[at:]], 0)
    place = iota((NW * PACK, 1), 0)
    out = dot(hot(place == code_ref[...]), rows, 1, 0)
    gains = jnp.concatenate(
        [
            half
            for g in (gain_a, gain_b, gain_c)
            for half in (g[:, :PART], g[:, PART:])
        ]
        + [jnp.zeros((2, PART), F32)],
        0,
    ).astype(BF16)
    spare = hot((place & (PACK - 1)) - 2 * CAP == iota((1, 8), 1))
    out_ref[...] = (out + dot(spare, gains, 1, 0)).astype(BF16)


def route_back(code_row, parts, gains):
    return call(
        route_back_kernel,
        (code_row, *parts, *gains),
        [kept((NW * PACK, PART), BF16)],
        name="route_back",
    )[0]


def adam(grad, first, second, weights, rate):
    first_new = BETA_ONE * first + (1.0 - BETA_ONE) * grad
    second_new = BETA_TWO * second + (1.0 - BETA_TWO) * grad * grad
    step = (
        first_new
        / (1.0 - BETA_ONE**STEP)
        / (jnp.sqrt(second_new / (1.0 - BETA_TWO**STEP)) + EPSILON)
    )
    return first_new, second_new, weights - rate * (step + DECAY * weights)


def slots_kernel(
    half_ref, me_ref, owner_ref, moved_ref, ready_ref, m_ref, a_ref, b_ref, gains_ref, ga_ref, gb_ref,
    grad_out, first_out, second_out, new_out, gg_out, gf_out, gs_out, gn_out
):
    rows = moved_ref[...]
    placed = hot(iota((CAP * TR, 1), 0) == slot_of_row(slot_kinds(owner_ref, me_ref[0])))
    grads = dot(placed, rows, 1, 0)
    for s in range(CAP):
        for ref in (m_ref, a_ref, b_ref):
            ref.wait(1)
        grad = grads[s * TR : (s + 1) * TR]
        grad_out[s] = grad
        first_out[s], second_out[s], new_out[s] = adam(
            grad, a_ref.buffer[s], b_ref.buffer[s], m_ref.buffer[s], RATE_WEIGHT
        )
        for out in (grad_out, first_out, second_out, new_out):
            out.flush()
    spare = hot((iota((1, NW * PACK), 1) & (PACK - 1)) - 2 * CAP == iota((8, 1), 0))
    sums = dot(spare, rows, 1, 0)
    gains = [jnp.concatenate([sums[q : q + 1], sums[q + 1 : q + 2]], 1) for q in (4, 2, 0)]
    inner_sum = jnp.concatenate(gains + [ready_ref[...]], 0)
    back = hot(feature_of(iota((1, D), 1)) == iota((PART, 1), 0) + half_ref[0] * PART)
    parts = dot(jnp.concatenate(pieces(inner_sum), 0).astype(BF16), back, 1, 1)
    n = 2 * LAYERS
    total = parts[:n] + parts[n : 2 * n] + parts[2 * n :]
    for l in range(LAYERS):
        gain_grad = total[2 * l : 2 * l + 2]
        gg_out[l] = gain_grad
        gf_out[l], gs_out[l], gn_out[l] = adam(
            gain_grad, ga_ref[l], gb_ref[l], gains_ref[l], RATE_GAIN
        )


def slots_update(half, me, owner_row, moved, ready, master, first, second, gains, gain_first, gain_second):
    return run(
        slots_kernel,
        [
            half, me, owner_row, moved, ready,
            FarSlots(master), FarSlots(first), FarSlots(second),
            gains, gain_first, gain_second,
        ],
        [Sent((CAP, TR, PART), F32, CAP)] * 4 + [sds((LAYERS, 2, PART), F32)] * 4,
        prefetch=2,
        name="slots_update",
    )


def turned(col):
    same = iota((TOK, TOK), 0) == iota((TOK, TOK), 1)
    return jnp.sum(jnp.where(same, col, 0), axis=0, keepdims=True)


def plan_kernel(group_ref, mine_ref, source_ref, *outs):
    same = iota((TOK, TOK), 0) == iota((TOK, TOK), 1)
    b = iota((ROWS, 1), 0) & 7
    block = group_ref[0] * 8 + b
    before = (group_ref[0] * 8 - 1) & 63
    lanes = iota((TOK, TOK), 1)
    for l in range(LAYERS):
        rank_row, rank_col, place_row = outs[3 * l : 3 * l + 3]
        cols = jnp.zeros((TOK, TOK), I32)
        for r in range(ROUNDS):
            row = mine_ref[l * ROUNDS + r : l * ROUNDS + r + 1, :]
            col = jnp.sum(jnp.where(same, row, 0), axis=1, keepdims=True)
            rank_row[r : r + 1, :] = jnp.sum(jnp.where(col < row, 1, 0), axis=0, keepdims=True)
            rank = jnp.sum(jnp.where(row < col, 1, 0), axis=1, keepdims=True)
            cols = jnp.where(lanes == r, rank, cols)
        rank_col[...] = cols
        source = source_ref[l]
        target = jnp.broadcast_to(source[:, None, :], (NW, 8, TOK)).reshape(ROWS, TOK)
        place = target & (TOK - 1)
        got = []
        for want in (block, before):
            inside = (target >> 7) == want
            got.append(jnp.min(jnp.where(inside, place, TOK), axis=1, keepdims=True))
            got.append(jnp.max(jnp.where(inside, place, -1), axis=1, keepdims=True))
        low, high, low_lent, high_lent = got
        columns = (
            low + TOK * b,
            high + TOK * b,
            jnp.where(b == 0, low_lent - SPAN, jnp.where(b == 2, high_lent - SPAN, -1)),
            jnp.where(b == 1, low_lent - SPAN, jnp.where(b == 3, high_lent - SPAN, -1)),
        )
        for j, column in enumerate(columns):
            for q in range(4):
                at = slice(q * TOK, (q + 1) * TOK)
                place_row[j : j + 1, at] = turned(column[at])


def plan(group, mine, source):
    layer = [kept((ROUNDS, TOK), I32), kept((TOK, TOK), I32), kept((4, ROWS), I32)]
    return call(plan_kernel, (group, mine, source), layer * LAYERS, prefetch=1, name="plan")


def inner_kernel(half_ref, *refs):
    count = len(refs) // 3
    n = half_ref[0]
    feature = feature_of(iota((1, D), 1))
    mine = hot(feature == iota((PART, 1), 0) + n * PART)
    theirs = hot(feature == iota((PART, 1), 0) + (1 - n) * PART)
    for i in range(count):
        own, other, out = refs[2 * i], refs[2 * i + 1], refs[2 * count + i]
        if own.dtype == BF16:
            out[...] = dot(own[...], mine, 1, 0) + dot(other[...], theirs, 1, 0)
        else:
            total = jnp.zeros(out.shape, F32)
            for a, b in zip(pieces(own[...]), pieces(other[...])):
                total = total + (dot(a.astype(BF16), mine, 1, 0) + dot(b.astype(BF16), theirs, 1, 0))
            out[...] = total


def inner(half, pairs, name):
    flat = [a for pair in pairs for a in pair]
    outs = [sds((own.shape[0], D), F32) for own, _ in pairs]
    return call(inner_kernel, (half, *flat), outs, prefetch=1, name=name)


def outer_kernel(count, half_ref, *refs):
    n = half_ref[0]
    feature = feature_of(iota((1, D), 1))
    back = hot(feature == iota((PART, 1), 0) + n * PART)
    for i in range(count):
        total = jnp.zeros(refs[count + i].shape, F32)
        for part in pieces(refs[i][...]):
            total = total + dot(part.astype(BF16), back, 1, 1)
        refs[count + i][...] = total


def outer(half, arrays, name):
    outs = [sds((a.shape[0], PART), F32) for a in arrays]
    return call(
        functools.partial(outer_kernel, len(arrays)), (half, *arrays), outs, prefetch=1, name=name
    )


def project_kernel(pending, count, core_ref, *refs):
    if pending:
        x_ref, own_ref, other_ref, *rest = refs
        x = x_ref[...] + (own_ref[...].astype(F32) + other_ref[...].astype(F32))
    else:
        x_ref, *rest = refs
        x = x_ref[...]
    gain_ref, *rest = rest
    q_refs, v_refs = rest[:count], rest[count : 2 * count]
    rank_ref, x_out, hn_out, send_out = rest[2 * count :]
    core = core_ref[0]
    x_out[...] = x
    xhat, _ = norm_parts(x)
    hn = xhat * gain_ref[...]
    hn_out[0] = hn[:, :PART].astype(BF16)
    hn_out[1] = hn[:, PART:].astype(BF16)
    q = into(core, hn, q_refs).astype(BF16)
    v = into(core, hn, v_refs).astype(BF16)
    qv = jnp.concatenate([m[:, h * DH : (h + 1) * DH] for h in range(HN) for m in (q, v)], 1)
    for r in range(ROUNDS):
        moved = dot(send_hots(rank_ref[r : r + 1, :]), qv, 1, 0)
        even, odd = moved[:NW].astype(BF16), moved[NW : 2 * NW].astype(BF16)
        lent_q, lent_v = moved[2 * NW : 3 * NW], moved[3 * NW :]
        for h in range(HN):
            rows = slice((r * HN + h) * NW, (r * HN + h + 1) * NW)
            at = h * 2 * DH
            send_out[rows, : 2 * DH] = even[:, at : at + 2 * DH]
            send_out[rows, 2 * DH : 4 * DH] = odd[:, at : at + 2 * DH]
            send_out[rows, 4 * DH :] = (
                lent_q[:, at : at + DH] + lent_v[:, at + DH : at + 2 * DH]
            ).astype(BF16)


def project(core, x, pending, gain, wq, wv, rank_row):
    args, specs = unpacked([core, x, *(pending or ()), gain, wq, wv, rank_row], 1)
    return call(
        functools.partial(project_kernel, pending is not None, len(wq.parts())),
        args,
        [kept((TOK, D), F32), kept((2, TOK, PART), BF16), kept((ROWS, QV_LANES), BF16)],
        specs=specs,
        in_place=(0, *((1,) if pending else ()), *(tuple(specs) if len(wq.parts()) == 4 else ())),
        prefetch=1,
        name="project",
    )


def scores_of(rows):
    keys = rows[:, :DH].astype(F32)
    inv = lax.rsqrt(jnp.sum(keys * keys, axis=-1, keepdims=True) + 1e-06)
    unit = (keys * inv).astype(BF16)
    scores = jnp.concatenate(
        [
            dot(
                rows[(c + 1) * SPAN : (c + 2) * SPAN, :DH],
                unit[c * SPAN : (c + 2) * SPAN],
                1,
                1,
            )
            for c in range(16)
        ],
        0,
    )
    own = iota((1024, TOK), 1) == (iota((1024, TOK), 0) & (SPAN - 1)) + SPAN
    scores = jnp.where(own, MASK_FILL, scores)
    peak = jnp.max(scores, axis=-1, keepdims=True)
    total = peak + jnp.log(jnp.sum(jnp.exp(scores - peak), axis=-1, keepdims=True))
    exact = jnp.exp(scores - total)
    return keys, inv, unit, own, total, exact


def arrive(place_row_ref, j, rows):
    count = 1024 if j < 2 else SPAN
    return dot(hot(iota((count, 1), 0) == place_row_ref[j : j + 1, :]), rows, 1, 0)


def leave(place_row_ref, j, rows):
    at = hot(iota((rows.shape[0], 1), 0) == place_row_ref[j : j + 1, :])
    return dot(at, rows, 0, 0)


def attend_kernel(moved_ref, place_row_ref, sorted_out, send_out):
    q_lent = arrive(place_row_ref, 2, moved_ref[:, 4 * DH :])
    v_lent = arrive(place_row_ref, 3, moved_ref[:, 4 * DH :])
    main = arrive(place_row_ref, 0, moved_ref[:, : 2 * DH]) + arrive(
        place_row_ref, 1, moved_ref[:, 2 * DH : 4 * DH]
    )
    rows = jnp.concatenate([jnp.concatenate([q_lent, v_lent], 1), main], 0).astype(BF16)
    sorted_out[...] = rows
    _, _, _, _, total, exact = scores_of(rows)
    probs = exact.astype(BF16)
    outs = jnp.concatenate(
        [
            dot(probs[c * SPAN : (c + 1) * SPAN], rows[c * SPAN : (c + 2) * SPAN, DH:], 1, 0)
            for c in range(16)
        ],
        0,
    )
    aux = spread(total, iota((1024, TOK), 1))
    both = jnp.concatenate([outs, aux], 1).astype(BF16)
    even = leave(place_row_ref, 0, both)
    odd = leave(place_row_ref, 1, both)
    send_out[:, :DH] = even[:, :DH].astype(BF16)
    send_out[:, DH : 2 * DH] = odd[:, :DH].astype(BF16)
    lanes = iota((ROWS, TOK), 1)
    send_out[:, 2 * DH :] = either(lanes, even[:, DH:], odd[:, DH:]).astype(BF16)


def attend(moved, place_row):
    return call(
        attend_kernel,
        (moved, place_row),
        [kept((1088, 2 * DH), BF16), kept((ROWS, O_LANES), BF16)],
        in_place=(1,),
        name="attend",
    )


def by_head(ref, r, cols):
    return jnp.concatenate(
        [ref[(r * HN + h) * NW : (r * HN + h + 1) * NW, cols] for h in range(HN)], 1
    )


def merge_kernel(count, core_ref, moved_ref, rank_col_ref, *refs):
    w_refs, refs = refs[:count], refs[count:]
    send_out, o_out, share_out, merged_out = refs
    lanes = iota((TOK, TOK), 1)
    outs, logs = [], []
    for r in range(ROUNDS):
        hots = return_hots(rank_col_ref[:, r : r + 1], 2)
        aux = by_head(moved_ref, r, slice(2 * DH, 3 * DH))
        even = dot(
            hots[:, :NW], jnp.concatenate([by_head(moved_ref, r, slice(0, DH)), aux], 1), 1, 0
        )
        odd = dot(
            hots[:, NW:], jnp.concatenate([by_head(moved_ref, r, slice(DH, 2 * DH)), aux], 1), 1, 0
        )
        outs.append(even[:, :PART] + odd[:, :PART])
        o_out[r] = outs[r].astype(BF16)
        logs.append(
            [
                jnp.sum(
                    either(
                        lanes,
                        even[:, PART + h * DH : PART + (h + 1) * DH],
                        odd[:, PART + h * DH : PART + (h + 1) * DH],
                    ),
                    axis=-1,
                    keepdims=True,
                )
                for h in range(HN)
            ]
        )
    merged = []
    share_all = jnp.zeros((TOK, TOK), F32)
    for h in range(HN):
        top = jnp.maximum(logs[0][h], logs[1][h])
        e0 = jnp.exp(logs[0][h] - top)
        e1 = jnp.exp(logs[1][h] - top)
        total = e0 + e1
        cols = slice(h * DH, (h + 1) * DH)
        s0, s1 = e0 / total, e1 / total
        merged.append(s0 * outs[0][:, cols] + s1 * outs[1][:, cols])
        share_all = jnp.where(lanes == h, s0, jnp.where(lanes == HN + h, s1, share_all))
    share_out[...] = share_all
    merged = jnp.concatenate(merged, 1).astype(BF16)
    merged_out[...] = merged
    put_halves(out_of(core_ref[0], merged, w_refs), send_out)


def put_halves(pair, send_out):
    for i in range(2):
        send_out[:, i * PART : (i + 1) * PART] = pair[i].astype(BF16)


def merge(core, moved, rank_col, wo):
    args, specs = unpacked([core, moved, rank_col, wo], 1)
    return call(
        functools.partial(merge_kernel, len(wo.parts())),
        args,
        [
            kept((TOK, D), BF16),
            kept((ROUNDS, TOK, PART), BF16),
            kept((TOK, TOK), F32),
            kept((TOK, PART), BF16),
        ],
        specs=specs,
        in_place=(1, *specs),
        prefetch=1,
        name="merge",
    )


def gelu_parts(pre):
    half = 0.5 * (1.0 + lax.erf(pre * (0.5**0.5)))
    slope = half + pre * (jnp.exp(-0.5 * pre * pre) * np.float32(1.0 / np.sqrt(2.0 * np.pi)))
    return (pre * half).astype(BF16), slope.astype(BF16)


def add_up(total, more):
    return more if total is None else [a + b for a, b in zip(total, more)]


def ffn_forward(x_ref, own_ref, other_ref, gain_ref, w_ref, y_out, hf_out, act_out, slope_out):
    y = x_ref[...] + (own_ref[...].astype(F32) + other_ref[...].astype(F32))
    y_out[...] = y
    y_out.flush()
    xhat, _ = norm_parts(y)
    hf = (xhat * gain_ref[...]).astype(BF16)
    hf_out[0], hf_out[1] = hf[:, :PART], hf[:, PART:]
    total = None
    for c in range(QUAD):
        w_ref.wait(4)
        pre = dot(hf[:, :PART], w_ref.block(UP, c, 0), 1, 0) + dot(
            hf[:, PART:], w_ref.block(UP, c, 1), 1, 0
        )
        act, slope = gelu_parts(pre)
        act_out[:, c * PART : (c + 1) * PART] = act
        slope_out[:, c * PART : (c + 1) * PART] = slope
        total = add_up(total, [dot(act, w_ref.block(DOWN, c, c0), 1, 1) for c0 in range(2)])
    return total


def ffn_kernel(
    x_ref, own_ref, other_ref, gain_ref, w_ref, y_out, hf_out, act_out, slope_out, send_out
):
    put_halves(
        ffn_forward(
            x_ref, own_ref, other_ref, gain_ref, w_ref, y_out, hf_out, act_out, slope_out
        ),
        send_out,
    )


def ffn(x, own, other, gain, w):
    return run(
        ffn_kernel,
        [Far(x), Far(own), other, Far(gain), FfnWeight(w)],
        [
            Sent((TOK, D), F32),
            Sent((2, TOK, PART), BF16),
            Sent((TOK, QUAD * PART), BF16),
            Sent((TOK, QUAD * PART), BF16),
            Sent((TOK, D), BF16),
        ],
        name="ffn",
    )


def put_pieces(out_ref, at, row, rows, grad):
    for piece in range(32):
        z, tau, y = piece >> 3, (piece >> 1) & 3, piece & 1
        got = grad[piece * 16 : (piece + 1) * 16]
        if rows == 16:
            out_ref[2 * tau + at, z * 2 + y, row : row + 16] = got
        else:
            out_ref[at, z * 2 + y, row + tau * 16 : row + (tau + 1) * 16] = got


def ffn_backward(back, waits, w_ref, hf_ref, act_ref, slope_ref, send_out, grad_out):
    total = None
    for c in range(QUAD):
        if waits:
            w_ref.wait(4)
        cols = slice(c * PART, (c + 1) * PART)
        d_act = dot(back[0], w_ref.block(DOWN, c, 0), 1, 0) + dot(
            back[1], w_ref.block(DOWN, c, 1), 1, 0
        )
        d_pre = (d_act * slope_ref[:, cols].astype(F32)).astype(BF16)
        total = add_up(total, [dot(d_pre, w_ref.block(UP, c, c0), 1, 1) for c0 in range(2)])
        act = act_ref[:, cols]
        for c0 in range(2):
            put_pieces(grad_out, 2 * c + c0, 0, 64, dot(hf_ref[c0], d_pre, 0, 0).astype(BF16))
            put_pieces(grad_out, 2 * c + c0, 64, 64, dot(back[c0], act, 0, 0).astype(BF16))
        grad_out.flush()
    put_halves(total, send_out)


def turn_kernel(
    x_ref, own_ref, other_ref, gain_ref, g_ref, w_ref,
    y_out, forth_out, send_out, grad_out, hf_ref, act_ref, slope_ref
):
    put_halves(
        ffn_forward(
            x_ref, own_ref, other_ref, gain_ref, w_ref, y_out, hf_ref, act_ref, slope_ref
        ),
        forth_out,
    )
    forth_out.flush()
    back = g_ref[...].astype(BF16)
    back = [back[:, :PART], back[:, PART:]]
    ffn_backward(back, False, w_ref, hf_ref, act_ref, slope_ref, send_out, grad_out)


def turn(x, own, other, gain, g, w):
    return run(
        turn_kernel,
        [Far(x), Far(own), other, Far(gain), Far(g), FfnWeight(w)],
        [
            Sent((TOK, D), F32),
            Sent((TOK, D), BF16),
            Sent((TOK, D), BF16),
            Sent((2 * QUAD, 8, FFN_ROWS, PART), BF16, QUAD),
        ],
        temps=[
            pltpu.VMEM((2, TOK, PART), BF16),
            pltpu.VMEM((TOK, QUAD * PART), BF16),
            pltpu.VMEM((TOK, QUAD * PART), BF16),
        ],
        name="turn",
        vmem=BIG_VMEM_BYTES,
    )


def ffn_back_kernel(
    g_ref, own_ref, other_ref, x_ref, gain_ref, hf_ref, act_ref, slope_ref, w_ref, unused_ref,
    g_out, send_out, grad_out, dgain_out
):
    xhat, rstd = norm_parts(x_ref[...])
    add, dgain = norm_back(
        own_ref[...].astype(F32) + other_ref[...].astype(F32), gain_ref[...], xhat, rstd
    )
    dgain_out[...] = dgain
    g = g_ref[...] + add
    g_out[...] = g
    g_out.flush()
    back = g.astype(BF16)
    back = [back[:, :PART], back[:, PART:]]
    ffn_backward(back, True, w_ref, hf_ref, act_ref, slope_ref, send_out, grad_out)


def ffn_back(g, own, other, x, gain, more, hf, act, slope, w):
    return run(
        ffn_back_kernel,
        [
            Far(g), Far(own), other, Far(x), Far(gain),
            Far(hf), Far(act), Far(slope), FfnWeight(w), Direct(more),
        ],
        [
            Sent((TOK, D), F32),
            Sent((TOK, D), BF16),
            Sent((2 * QUAD, 8, FFN_ROWS + ATTN_ROWS, PART), BF16, QUAD),
            sds((1, D), F32),
        ],
        partial={2: (2 * QUAD, 8, FFN_ROWS, PART)},
        aliases={9: 2},
        name="ffn_back",
        vmem=BIG_VMEM_BYTES,
    )


def merge_back_kernel(count, core_ref, g_ref, own_ref, other_ref, y_ref, gain_ref, *refs):
    w_refs, refs = refs[:count], refs[count:]
    o_ref, share_ref, rank_row_ref, g_out, back_out, send_out, dgain_out = refs
    xhat, rstd = norm_parts(y_ref[...])
    add, dgain = norm_back(own_ref[...].astype(F32) + other_ref[...].astype(F32), gain_ref[...], xhat, rstd)
    dgain_out[...] = dgain
    g = g_ref[...] + add
    g_out[...] = g
    back_out[0] = g[:, :PART].astype(BF16)
    back_out[1] = g[:, PART:].astype(BF16)
    dout = into(core_ref[0], g, w_refs)
    share = share_ref[...]
    o0 = o_ref[0].astype(F32)
    o1 = o_ref[1].astype(F32)
    lanes = iota((TOK, TOK), 1)
    parts = [[], []]
    logs = [[], []]
    for h in range(HN):
        cols = slice(h * DH, (h + 1) * DH)
        s0 = share[:, h : h + 1]
        s1 = share[:, HN + h : HN + h + 1]
        dh = dout[:, cols]
        t0 = jnp.sum(dh * o0[:, cols], axis=-1, keepdims=True)
        t1 = jnp.sum(dh * o1[:, cols], axis=-1, keepdims=True)
        mean = s0 * t0 + s1 * t1
        parts[0].append(s0 * dh)
        parts[1].append(s1 * dh)
        logs[0].append(spread(s0 * (t0 - mean), lanes))
        logs[1].append(spread(s1 * (t1 - mean), lanes))
    lanes = iota((NW, TOK), 1)
    for r in range(ROUNDS):
        moved = dot(
            send_hots(rank_row_ref[r : r + 1, :], 2),
            jnp.concatenate(parts[r] + logs[r], 1).astype(BF16),
            1,
            0,
        )
        even, odd = moved[:NW], moved[NW:]
        for h in range(HN):
            rows = slice((r * HN + h) * NW, (r * HN + h + 1) * NW)
            cols = slice(h * DH, (h + 1) * DH)
            aux = slice(PART + h * DH, PART + (h + 1) * DH)
            send_out[rows, :DH] = even[:, cols].astype(BF16)
            send_out[rows, DH : 2 * DH] = odd[:, cols].astype(BF16)
            send_out[rows, 2 * DH :] = either(lanes, even[:, aux], odd[:, aux]).astype(BF16)


def merge_back(core, g, own, other, y, gain, wo, o, share, rank_row):
    args, specs = unpacked([core, g, own, other, y, gain, wo, o, share, rank_row], 1)
    return call(
        functools.partial(merge_back_kernel, len(wo.parts())),
        args,
        [
            kept((TOK, D), F32),
            kept((2, TOK, PART), BF16),
            kept((ROWS, O_LANES), BF16),
            sds((1, D), F32),
        ],
        specs=specs,
        in_place=(0, 1, 3, *specs, *range(len(args) - 4, len(args) - 1)),
        prefetch=1,
        name="merge_back",
    )


def attend_back_kernel(moved_ref, sorted_ref, place_row_ref, gain_ref, send_out):
    lanes = iota((ROWS, TOK), 1)
    aux = moved_ref[:, 2 * DH :].astype(F32)
    got = jnp.zeros((1024, 2 * DH), F32)
    for j in range(2):
        here = jnp.where(lanes >> 3 == j, aux, 0.0).astype(BF16)
        pair = jnp.concatenate([moved_ref[:, j * DH : (j + 1) * DH], here], 1)
        got = got + arrive(place_row_ref, j, pair)
    d_out = got[:, :DH].astype(BF16)
    d_log = jnp.sum(got[:, DH:], axis=-1, keepdims=True)
    rows = sorted_ref[...]
    keys, inv, unit, own, _, exact = scores_of(rows)
    probs = exact.astype(BF16)
    g_probs = jnp.concatenate(
        [
            dot(d_out[c * SPAN : (c + 1) * SPAN], rows[c * SPAN : (c + 2) * SPAN, DH:], 1, 1)
            for c in range(16)
        ],
        0,
    )
    inner_sum = jnp.sum(g_probs * exact, axis=-1, keepdims=True)
    g_scores = exact * (g_probs - inner_sum + d_log)
    g_scores = jnp.where(own, 0.0, g_scores).astype(BF16)
    d_query, d_unit, d_value = [], [], []
    for c in range(16):
        here = slice(c * SPAN, (c + 1) * SPAN)
        both = slice(c * SPAN, (c + 2) * SPAN)
        after = slice((c + 1) * SPAN, (c + 2) * SPAN)
        d_query.append(dot(g_scores[here], unit[both], 1, 0))
        d_unit.append(dot(g_scores[here], rows[after, :DH], 0, 0))
        d_value.append(dot(probs[here], d_out[here], 0, 0))

    def overlap(parts):
        out = [parts[0][:SPAN]]
        for c in range(15):
            out.append(parts[c][SPAN:] + parts[c + 1][:SPAN])
        out.append(parts[15][SPAN:])
        return jnp.concatenate(out, 0)

    g_unit = overlap(d_unit)
    along = jnp.sum(g_unit * keys, axis=-1, keepdims=True)
    g_keys = inv * g_unit - keys * (inv * inv * inv) * along
    g_query = jnp.concatenate([jnp.zeros((SPAN, DH), F32)] + d_query, 0) + g_keys
    grads = jnp.concatenate([g_query, overlap(d_value)], 1).astype(BF16)
    for j in range(2):
        cols = slice(j * 2 * DH, (j + 1) * 2 * DH)
        send_out[:, cols] = leave(place_row_ref, j, grads[SPAN:]).astype(BF16)
    lent = leave(place_row_ref, 2, grads[:SPAN, :DH]) + leave(place_row_ref, 3, grads[:SPAN, DH:])
    b = iota((ROWS, 1), 0) & 7
    for q in range(4):
        lent = jnp.where(b == 4 + q, gain_ref[:, q * DH : (q + 1) * DH], lent)
    send_out[:, 4 * DH :] = lent.astype(BF16)


def attend_back(moved, rows, place_row, gain):
    return call(
        attend_back_kernel,
        (moved, rows, place_row, gain),
        [kept((ROWS, QV_LANES), BF16)],
        in_place=(1, 2),
        name="attend_back",
    )[0]


def project_back_kernel(count, core_ref, moved_ref, rank_col_ref, *refs):
    q_refs, v_refs = refs[:count], refs[count : 2 * count]
    send_out, dq_out, dv_out, gain_out = refs[2 * count :]
    gain_out[...] = dot(
        hot(iota((8, 1), 0) == (iota((1, ROWS), 1) & 7)), moved_ref[:, 4 * DH :], 1, 0
    )
    total = jnp.zeros((TOK, HN * 2 * DH), F32)
    lent_q = jnp.zeros((TOK, PART), F32)
    lent_v = jnp.zeros((TOK, PART), F32)
    for r in range(ROUNDS):
        hots = return_hots(rank_col_ref[:, r : r + 1])
        total = total + dot(hots[:, :NW], by_head(moved_ref, r, slice(0, 2 * DH)), 1, 0)
        total = total + dot(hots[:, NW : 2 * NW], by_head(moved_ref, r, slice(2 * DH, 4 * DH)), 1, 0)
        lent = by_head(moved_ref, r, slice(4 * DH, 5 * DH))
        lent_q = lent_q + dot(hots[:, 2 * NW : 3 * NW], lent, 1, 0)
        lent_v = lent_v + dot(hots[:, 3 * NW :], lent, 1, 0)
    d_q = jnp.concatenate([total[:, h * 2 * DH : h * 2 * DH + DH] for h in range(HN)], 1)
    d_v = jnp.concatenate([total[:, h * 2 * DH + DH : (h + 1) * 2 * DH] for h in range(HN)], 1)
    d_q = (d_q + lent_q).astype(BF16)
    d_v = (d_v + lent_v).astype(BF16)
    dq_out[...] = d_q
    dv_out[...] = d_v
    core = core_ref[0]
    from_q = out_of(core, d_q, q_refs)
    from_v = out_of(core, d_v, v_refs)
    put_halves([a + b for a, b in zip(from_q, from_v)], send_out)


def project_back(core, moved, rank_col, wq, wv):
    args, specs = unpacked([core, moved, rank_col, wq, wv], 1)
    return call(
        functools.partial(project_back_kernel, len(wq.parts())),
        args,
        [kept((TOK, D), BF16), kept((TOK, PART), BF16), kept((TOK, PART), BF16), sds((8, DH), F32)],
        specs=specs,
        in_place=range(1, len(args) - 1),
        prefetch=1,
        name="project_back",
    )


def attn_part_kernel(back_ref, merged_ref, hn_ref, dq_ref, dv_ref, grad_out, buffer, sems):
    for c0 in range(2):
        for i, (left, right) in enumerate(
            ((back_ref, merged_ref), (hn_ref, dq_ref), (hn_ref, dv_ref))
        ):
            put_pieces(buffer, c0, i * 16, 16, dot(left[c0], right[...], 0, 0).astype(BF16))
    copy = pltpu.make_async_copy(
        buffer, grad_out.at[:, :, pl.ds(FFN_ROWS, ATTN_ROWS), :], sems.at[0]
    )
    copy.start()
    copy.wait()


def attn_part_of(back, merged, hn, dq, dv):
    return call(
        attn_part_kernel,
        (back, merged, hn, dq, dv),
        [kept((2 * QUAD, 8, FFN_ROWS + ATTN_ROWS, PART), BF16)],
        out_specs={0: pl.BlockSpec(memory_space=pl.ANY)},
        scratch=[pltpu.VMEM((2 * QUAD, 8, ATTN_ROWS, PART), BF16), pltpu.SemaphoreType.DMA((1,))],
        in_place=range(5),
        name="attn_part",
    )[0]


def last_kernel(g_ref, own_ref, other_ref, x_ref, gain_ref, g_out, dgain_out):
    xhat, rstd = norm_parts(x_ref[...])
    add, dgain = norm_back(own_ref[...].astype(F32) + other_ref[...].astype(F32), gain_ref[...], xhat, rstd)
    g_out[...] = g_ref[...] + add
    dgain_out[...] = dgain


def last(g, own, other, x, gain):
    return call(
        last_kernel,
        (g, own, other, x, gain),
        [kept((TOK, D), F32), sds((1, D), F32)],
        in_place=(0, 1, 3),
        name="last",
    )


def pair_dot(left_a, left_b, right_a, right_b):
    left = jnp.concatenate([left_a, left_b], 0)
    right = jnp.concatenate([right_a, right_b], 0)
    return dot(left, right, 0, 0).astype(BF16)


def attn_grad_kernel(count, core_ref, *refs):
    out_ref = refs[-1]
    for i in range(count):
        la, lb, ra, rb = refs[4 * i : 4 * i + 4]
        got = pair_dot(la[0], lb[0], ra[...], rb[...])
        out_ref[:, i * 16 : (i + 1) * 16] = got.reshape(32, 16, PART)


def attn_grad(core, pairs):
    half = pl.BlockSpec((1, TOK, PART), lambda i, core: (core[0], 0, 0))
    args = [a for left, right in pairs for a in (*left, *right)]
    specs = {4 * i + j: half for i in range(len(pairs)) for j in range(2)}
    return call(
        functools.partial(attn_grad_kernel, len(pairs)),
        (core, *args),
        [kept((32, 16 * len(pairs), PART), BF16)],
        specs=specs,
        prefetch=1,
        in_place=range(0, len(args), 2),
        name="attn_grad",
    )[0]


def swap_narrow(values):
    return lax.ppermute(values, "narrow", [(0, 1), (1, 0)])


def with_core(values):
    other = lax.ppermute(values, "wide", [(i, i ^ 1) for i in range(NW)])
    return values, other


def to_all(values):
    return lax.all_to_all(values, "wide", split_axis=0, concat_axis=0, tiled=True)


SAME_CORE = [
    [y * 32 + z * 8 + x * 2 + c for z in range(4) for x in range(4) for y in range(2)]
    for c in range(2)
]
LAYER_OF_Y = [[y * 32 + i for i in range(NW // 2)] for y in range(2)]


def summed(values):
    return jnp.sum(to_same_core(values).astype(F32), axis=0).astype(BF16)


ALONG_X_AND_CORE = [[hi * 8 + i for i in range(8)] for hi in range(8)]
ALONG_Z_AND_Y = [
    [y * 32 + z * 8 + i for z in range(4) for y in range(2)] for i in range(8)
]
ALONG_Z = [
    [y * 32 + z * 8 + x * 2 + c for z in range(4)] for y in range(2) for x in range(4) for c in range(2)
]


def summed_along_x(values):
    return lax.psum_scatter(
        values, "wide", scatter_dimension=0, tiled=True, axis_index_groups=ALONG_X_AND_CORE
    ).reshape(values.shape[1:])


def summed_across_x(values):
    moved = lax.all_to_all(
        values, "wide", split_axis=0, concat_axis=0, tiled=True, axis_index_groups=ALONG_Z_AND_Y
    )
    return jnp.sum(moved.astype(F32), axis=0).astype(BF16)


def summed_along_z(values):
    return lax.psum_scatter(
        values, "wide", scatter_dimension=0, tiled=True, axis_index_groups=ALONG_Z
    )


def summed_along_y(values):
    y = lax.axis_index("wide") >> 5
    mine = lax.dynamic_index_in_dim(values, y, keepdims=False)
    theirs = lax.dynamic_index_in_dim(values, 1 - y, keepdims=False)
    got = lax.ppermute(theirs, "wide", [(i, i ^ 32) for i in range(NW)])
    return (mine.astype(F32) + got.astype(F32)).astype(BF16)


def to_same_core(values):
    return lax.all_to_all(
        values, "wide", split_axis=0, concat_axis=0, tiled=True, axis_index_groups=SAME_CORE
    )


def after(values, *others):
    return lax.optimization_barrier((values, others))[0]


def gathered(rows):
    got = lax.all_gather(rows, "wide", axis=0, tiled=True, axis_index_groups=LAYER_OF_Y)
    return got.reshape(QUAD, QUAD, 2, rows.shape[0], PART)


def moved_rows(rows):
    return to_all(rows.reshape(NW, rows.shape[0] // NW, -1)).reshape(rows.shape)


def on_device(
    x_first,
    x_second,
    grad_first,
    grad_second,
    sort_target,
    owner,
    master,
    moment_first,
    moment_second,
    gains,
    gain_first,
    gain_second,
):
    me = lax.axis_index("wide").astype(I32)
    half = lax.axis_index("narrow").astype(I32).reshape(1)
    core = (me & 1).reshape(1)
    owner_row = owner.reshape(1, TILES)

    routed = route_out(me.reshape(1), owner_row, master)
    sort_target, held = after((sort_target, owner), routed)
    moved = moved_rows(routed)
    chunks = []
    for l in range(LAYERS):
        of = held[l * 88 : (l + 1) * 88]
        chunks += [of[at : at + 32].reshape(8, 4).T.reshape(4, 8) for at in (24, 56)]
        chunks += [of[16:24].reshape(1, 8), of[:16].reshape(2, 8)]
    holder = jnp.repeat(jnp.concatenate(chunks), 2, axis=1)
    e = np.arange(16, dtype=np.int32)[None] & 1
    code_row = ((holder // CAP) * PACK + (holder % CAP) * 2 + e).reshape(1, -1)
    there = (holder // CAP) * WIDE_PACK + (holder % CAP) * 4 + e
    both = jnp.stack([there, there + 2], 1)
    mine_only = there + 2 * (me >> 5)
    code_col = jnp.concatenate(
        [
            both[:9].reshape(-1),
            both[19:].reshape(-1),
            both[11:19].reshape(-1),
            mine_only[9:11].reshape(-1),
        ]
    ).reshape(-1, 1)
    mine = lax.dynamic_slice_in_dim(sort_target, me * TOK, TOK, axis=2).reshape(-1, TOK)
    by_source = lax.dynamic_index_in_dim(sort_target, me >> 5, 1, keepdims=False)
    plans = plan((me & 7).reshape(1), mine, by_source.reshape(LAYERS, NW, TOK))
    rank_rows, rank_cols, place_rows = [plans[i::3] for i in range(3)]
    flat_gains = gains.reshape(LAYERS * 2, PART)
    moved = after(moved, code_col, code_row, plans)
    first_rows, early_rows, late_rows = pick(code_col, moved)
    streams = (x_second, flat_gains, x_first, grad_first, grad_second)
    pairs = [(a, swap_narrow(a)) for a in after(streams, moved)]
    x_two, gain_rows = inner(half, pairs[:2], "inner_a")
    pairs = pairs[2:]
    first_w = with_core(after(to_same_core(first_rows), x_two, gain_rows, pairs))
    early = gathered(early_rows)
    late = gathered(late_rows)
    x_one, g_one, g_two = inner(half, pairs, "inner_b")
    w_ffn = [early, late]
    w_attn = [
        [Weight(8, early), Weight(0, *first_w), Weight(1, *first_w)],
        [Weight(9, early), Weight(10, early), Weight(11, early)],
    ]
    gain = [[Gain(gain_rows, 2 * l + i) for i in range(2)] for l in range(LAYERS)]

    saved = []
    pending = None
    for l in range(LAYERS):
        w_out, w_qk, w_value = w_attn[l]
        x_two, hn, send = project(core, x_two, pending, gain[l][0], w_qk, w_value, rank_rows[l])
        moved = moved_rows(send)
        if l == 0:
            moved = after(moved, x_one, g_one, g_two)
        rows, send = attend(moved, place_rows[l])
        moved = moved_rows(send)
        send, o, share, merged = merge(core, moved, rank_cols[l], w_out)
        stream = (x_one, send, swap_narrow(send), gain[l][1])
        if l < LAYERS - 1:
            x_one, *for_ffn, send_f = ffn(*stream, w_ffn[l])
        else:
            x_one, send_f, send, ffn_part = turn(*stream, g_two, w_ffn[l])
        pending = (send_f, swap_narrow(send_f))
        saved.append((x_two, x_one, hn, rows, o, share, merged))
    y_two = x_two + (pending[0].astype(F32) + pending[1].astype(F32))
    y_first, y_second = outer(half, (x_one, y_two), "outer_y")

    pending = None
    dgains = [[None, None], [None, None]]
    gain_sums = []
    for l in reversed(range(LAYERS)):
        x_in, y_mid, hn, rows, o, share, merged = saved[l]
        w_out, w_qk, w_value = w_attn[l]
        if l < LAYERS - 1:
            g_two, send, ffn_part, dgains[l + 1][0] = ffn_back(
                g_two, *pending, *for_ffn, w_ffn[l]
            )
        other = swap_narrow(send)
        ffn_part = summed_along_x(ffn_part)
        if l == 0:
            other = after(other, ffn_rows)
            ffn_rows = summed_along_y(ffn_rows)
        g_one, back, send, dgains[l][1] = merge_back(
            core, g_one, send, other, y_mid, gain[l][1], w_out, o, share, rank_rows[l]
        )
        moved = moved_rows(send)
        if l > 0:
            moved = after(moved, y_first, y_second)
            half_gain = dgains[1][1][:, :PART]
        else:
            dx_first = outer(half, (g_one,), "outer_dx_first")[0]
            moved = after(moved, dx_first, ffn_rows)
            half_gain = dgains[1][1][:, PART:]
        send = attend_back(moved, rows, place_rows[l], half_gain)
        moved = moved_rows(send)
        if l > 0:
            moved = after(moved, ffn_part)
        send, dq, dv, gain_sum = project_back(core, moved, rank_cols[l], w_qk, w_value)
        other = swap_narrow(send)
        if l > 0:
            attn_part = attn_part_of(back, merged, hn, dq, dv)
            other = after(other, attn_part)
            ffn_rows = summed_along_z(after(ffn_part, moved))
        else:
            hn2 = with_core(hn)
            pairs = [(with_core(back), with_core(merged)), (hn2, with_core(dq)), (hn2, with_core(dv))]
            attn_part = attn_grad(core, pairs)
            attn_rows = summed(attn_part)
            ffn_part = after(ffn_part, attn_part)
            last_rows = summed_along_y(summed_along_z(ffn_part[:, SPLIT:]))
            both_rows = summed_across_x(after(ffn_part[:, :SPLIT], other))
        gain_sums.append(gain_sum[4:].reshape(1, PART))
        pending = (send, other, x_in, gain[l][0], attn_part)
    g_two, dgains[0][0] = last(g_two, *pending[:4])
    dx_second = outer(half, (g_two,), "outer_dx_second")[0]
    parts = (both_rows, last_rows, attn_rows, ffn_rows)
    back_rows = moved_rows(
        route_back(code_row, parts, (dgains[1][0], dgains[0][1], dgains[0][0]))
    )
    back_rows = after(back_rows, dx_second)
    slot_grad, slot_first, slot_second, slot_new, *gain_news = slots_update(
        half,
        me.reshape(1),
        owner_row,
        back_rows,
        jnp.concatenate(gain_sums, 1),
        master,
        moment_first,
        moment_second,
        gains,
        gain_first,
        gain_second,
    )
    gain_grad, gain_first_new, gain_second_new, gain_new = gain_news
    return (
        y_first,
        y_second,
        dx_first,
        dx_second,
        slot_grad,
        slot_first,
        slot_second,
        slot_new,
        gain_grad,
        gain_first_new,
        gain_second_new,
        gain_new,
    )


def solution(mesh):
    rows = P("wide", "narrow")
    tiles = P("wide", None, "narrow")
    gains = P(None, None, "narrow")
    return jax.shard_map(
        on_device,
        mesh=mesh,
        in_specs=(rows,) * 4 + (P(), P()) + (tiles,) * 3 + (gains,) * 3,
        out_specs=(rows,) * 4 + (tiles,) * 4 + (gains,) * 4,
        check_vma=False,
    )
```

```python
import functools

import jax
import jax.numpy as jnp
import numpy as np
from jax import lax
from jax.experimental import pallas as pl
from jax.experimental.pallas import tpu as pltpu
from jax.sharding import PartitionSpec as P

D = 1024
PART = 512
DH = 128
HN = 4
SPAN = 64
TR = 128
CAP = 5
TILES = 176
TOK = 128
NW = 64
LAYERS = 2
ROUNDS = 2
STEP = 5
GROUPS = 8
QV_LANES = 5 * DH
O_LANES = 3 * DH
ROWS = NW * 8
PACK = 16
WIDE_PACK = 24
PAIR_ROWS = WIDE_PACK * (NW // 2)
QUAD = 4
UP, DOWN = 0, 1
LAYER_ROWS = 176
ATTN_ROWS = 48
FFN_ROWS = 128
SPLIT = 80
EARLY_ROWS = 384

MASK_FILL = -1000000000.0
NORM_EPS = 1e-05
BETA_ONE = 0.5
BETA_TWO = 0.5
RATE_WEIGHT = 0.05
RATE_GAIN = 0.2
DECAY = 0.01
EPSILON = 1e-08

F32 = jnp.float32
BF16 = jnp.bfloat16
I32 = jnp.int32
VMEM_BYTES = 20 * 1024 * 1024
BIG_VMEM_BYTES = 32 * 1024 * 1024


def feature_of(p):
    c0 = p >> 9
    z = (p >> 7) & 3
    tau = (p >> 5) & 3
    y = (p >> 4) & 1
    t = (p >> 1) & 7
    e = p & 1
    return t * 128 + tau * 32 + c0 * 16 + (y * 4 + z) * 2 + e


def iota(shape, dim):
    return lax.broadcasted_iota(I32, shape, dim)


def hot(mask):
    return jnp.where(mask, 1.0, 0.0).astype(BF16)


def dot(a, b, ca, cb):
    return lax.dot_general(a, b, (((ca,), (cb,)), ((), ())), preferred_element_type=F32)


def in_hbm(array):
    return pltpu.with_memory_space_constraint(array, pltpu.MemorySpace.HBM)


def call(
    kernel, args, outs, grid=(1,), specs=None, out_specs=None, scratch=(), prefetch=0, in_place=(), name=None,
    aliases=None
):
    specs = specs or {}
    out_specs = out_specs or {}
    gains = {i: a.index for i, a in enumerate(args) if isinstance(a, Gain)}
    args = [a.rows if isinstance(a, Gain) else a for a in args]
    if gains:
        inner_kernel_body = kernel

        def kernel(*refs):
            inner_kernel_body(
                *[GainRow(r, gains[i]) if i in gains else r for i, r in enumerate(refs)]
            )

    def whole(shape):
        zeros = (0,) * len(shape)
        return pl.BlockSpec(shape, lambda *_: zeros)
    in_list = [specs.get(i, whole(a.shape)) for i, a in enumerate(args[prefetch:])]
    args = [in_hbm(a) if i - prefetch in in_place else a for i, a in enumerate(args)]
    out_list = [out_specs.get(i, whole(o.shape)) for i, o in enumerate(outs)]
    return pl.pallas_call(
        kernel,
        out_shape=outs,
        grid_spec=pltpu.PrefetchScalarGridSpec(
            num_scalar_prefetch=prefetch,
            grid=grid,
            in_specs=in_list,
            out_specs=out_list,
            scratch_shapes=list(scratch),
        ),
        compiler_params=pltpu.CompilerParams(vmem_limit_bytes=VMEM_BYTES),
        input_output_aliases=aliases or {},
        name=name,
    )(*args)


def sds(shape, dtype):
    return jax.ShapeDtypeStruct(shape, dtype)


def kept(shape, dtype):
    return pltpu.MemorySpace.HBM(shape, dtype)


def norm_parts(values):
    mean = jnp.mean(values, axis=-1, keepdims=True)
    var = jnp.mean(values * values, axis=-1, keepdims=True) - mean * mean
    rstd = lax.rsqrt(var + NORM_EPS)
    return (values - mean) * rstd, rstd


def norm_back(upstream, gain, xhat, rstd):
    gh = upstream * gain
    m1 = jnp.mean(gh, axis=-1, keepdims=True)
    m2 = jnp.mean(gh * xhat, axis=-1, keepdims=True)
    return rstd * (gh - m1 - xhat * m2), jnp.sum(upstream * xhat, axis=0, keepdims=True)


def flat(ref):
    return ref[...].reshape(PART, PART)


def halves(core, first, second):
    mine = core == 0
    return jnp.where(mine, first, second), jnp.where(mine, second, first)


class Gain:
    def __init__(self, rows, index):
        self.rows, self.index = rows, index


class GainRow:
    def __init__(self, ref, index):
        self.ref, self.index = ref, index

    def __getitem__(self, index):
        return self.ref[self.index : self.index + 1, :]


class Far:
    def __init__(self, array):
        self.row = None
        if isinstance(array, Gain):
            array, self.row = array.rows, array.index
        self.operands = [in_hbm(array)]
        self.scratch = [pltpu.VMEM(array.shape, array.dtype), pltpu.SemaphoreType.DMA((1,))]

    def fetch(self, refs, buffer, sems):
        return [pltpu.make_async_copy(refs[0], buffer, sems.at[0])]


class FfnWeight(Far):
    def __init__(self, array):
        self.operands = [in_hbm(array)]
        self.scratch = [
            pltpu.VMEM((2, QUAD, 2, QUAD, FFN_ROWS, PART), BF16),
            pltpu.SemaphoreType.DMA((16,)),
        ]

    def fetch(self, refs, buffer, sems):
        copies = []
        for c in range(QUAD):
            for part in range(2):
                for c0 in range(2):
                    source = refs[0].at[:, c, c0, pl.ds(part * FFN_ROWS, FFN_ROWS), :]
                    copies.append(
                        pltpu.make_async_copy(source, buffer.at[part, c, c0], sems.at[len(copies)])
                    )
        return copies


class Direct(Far):
    def __init__(self, array):
        self.operands = [in_hbm(array)]
        self.scratch = []


class FarSlots(Far):
    def __init__(self, array):
        self.operands = [in_hbm(array)]
        self.scratch = [pltpu.VMEM(array.shape, array.dtype), pltpu.SemaphoreType.DMA((CAP,))]

    def fetch(self, refs, buffer, sems):
        return [
            pltpu.make_async_copy(refs[0].at[s], buffer.at[s], sems.at[s]) for s in range(CAP)
        ]


class Fetched:
    def __init__(self, copies, buffer):
        self.copies = list(copies)
        self.buffer = buffer
        for copy in self.copies:
            copy.start()

    def wait(self, count=None):
        count = len(self.copies) if count is None else count
        for copy in self.copies[:count]:
            copy.wait()
        self.copies = self.copies[count:]

    def __getitem__(self, index):
        self.wait()
        return self.buffer[index]

    def halves(self):
        self.wait()
        return [self.buffer[i].reshape(PART, PART) for i in range(2)]

    def block(self, part, c, c0):
        return self.buffer[part, c, c0].reshape(PART, PART)


class Sent:
    def __init__(self, shape, dtype, pieces=1):
        self.shape, self.dtype, self.pieces = shape, dtype, pieces


class Sending:
    def __init__(self, target, buffer, sems, pieces):
        self.target, self.buffer, self.sems, self.pieces = target, buffer, sems, pieces
        self.copies = []

    def __setitem__(self, index, value):
        self.buffer[index] = value

    def flush(self):
        k = len(self.copies)
        size = self.target.shape[0] // self.pieces
        rows = pl.ds(k * size, size)
        source, target = self.buffer.at[rows], self.target.at[rows]
        if source.shape != target.shape:
            target = target.at[:, :, pl.ds(0, self.buffer.shape[2]), :]
        copy = pltpu.make_async_copy(source, target, self.sems.at[k])
        copy.start()
        self.copies.append(copy)

    def flush_all(self):
        while len(self.copies) < self.pieces:
            self.flush()

    def wait(self):
        for copy in self.copies:
            copy.wait()


def run(kernel, args, outs, prefetch=0, name=None, vmem=None, partial=None, temps=(), aliases=None):
    operands, in_specs, scratch = [], [], []
    for i, a in enumerate(args):
        if isinstance(a, Far):
            operands += a.operands
            in_specs += [pl.BlockSpec(memory_space=pl.ANY)] * len(a.operands)
            scratch += a.scratch
        else:
            operands.append(a)
            if i >= prefetch:
                zeros = (0,) * a.ndim
                in_specs.append(pl.BlockSpec(a.shape, lambda *_, zeros=zeros: zeros))
    out_shapes, out_specs = [], []
    for i, o in enumerate(outs):
        if isinstance(o, Sent):
            out_shapes.append(kept(o.shape, o.dtype))
            out_specs.append(pl.BlockSpec(memory_space=pl.ANY))
            shape = (partial or {}).get(i, o.shape)
            scratch += [pltpu.VMEM(shape, o.dtype), pltpu.SemaphoreType.DMA((o.pieces,))]
        else:
            zeros = (0,) * len(o.shape)
            out_shapes.append(o)
            out_specs.append(pl.BlockSpec(o.shape, lambda *_, zeros=zeros: zeros))

    def body(*refs):
        ins, rest = list(refs[: len(operands)]), list(refs[len(operands) :])
        out_refs, temps = rest[: len(outs)], rest[len(outs) :]
        seen = []
        for a in args:
            if isinstance(a, Far):
                mine = [ins.pop(0) for _ in a.operands]
                if a.scratch:
                    buffer, sems = temps.pop(0), temps.pop(0)
                    got = Fetched(a.fetch(mine, buffer, sems), buffer)
                    row = getattr(a, "row", None)
                    seen.append(got if row is None else GainRow(got, row))
                else:
                    seen.append(mine[0])
            else:
                seen.append(ins.pop(0))
        sending = []
        for o, ref in zip(outs, out_refs):
            if isinstance(o, Sent):
                ref = Sending(ref, temps.pop(0), temps.pop(0), o.pieces)
                sending.append(ref)
            seen.append(ref)
        kernel(*seen, *temps)
        for ref in sending:
            ref.flush_all()
        for ref in sending:
            ref.wait()

    return pl.pallas_call(
        body,
        out_shape=out_shapes,
        grid_spec=pltpu.PrefetchScalarGridSpec(
            num_scalar_prefetch=prefetch,
            grid=(1,),
            in_specs=in_specs,
            out_specs=out_specs,
            scratch_shapes=[*scratch, *temps],
        ),
        compiler_params=pltpu.CompilerParams(vmem_limit_bytes=vmem or VMEM_BYTES),
        input_output_aliases=aliases or {},
        name=name,
    )(*operands)


class Weight:
    def __init__(self, index, *arrays):
        self.index = index
        self.arrays = arrays

    def parts(self):
        index = self.index
        if len(self.arrays) == 2:
            return [
                (a, pl.BlockSpec((8, 16, PART), lambda *_, z=z: (z, index, 0)))
                for a in self.arrays
                for z in range(4)
            ]
        return [
            (self.arrays[0], pl.BlockSpec((1, QUAD, 2, 32, PART), lambda *_, z=z: (z, 0, 0, index, 0)))
            for z in range(4)
        ]


def rows_of(refs):
    return jnp.concatenate([r[...].reshape(-1, PART) for r in refs], 0)


def weight_halves(core, refs):
    if len(refs) == 4:
        return [
            jnp.concatenate([r[0, :, c0].reshape(-1, PART) for r in refs], 0) for c0 in range(2)
        ]
    return rows_of(refs[:4]), rows_of(refs[4:])


def into(core, full, refs):
    first, second = full[:, :PART], full[:, PART:]
    if len(refs) == 8:
        first, second = halves(core, first, second)
    w = weight_halves(core, refs)
    return dot(first.astype(BF16), w[0], 1, 0) + dot(second.astype(BF16), w[1], 1, 0)


def out_of(core, part, refs):
    w = weight_halves(core, refs)
    pair = dot(part, w[0], 1, 1), dot(part, w[1], 1, 1)
    return pair if len(refs) == 4 else halves(core, *pair)


def unpacked(args, prefetch):
    out, specs = [], {}
    for a in args:
        if isinstance(a, Weight):
            for array, spec in a.parts():
                specs[len(out) - prefetch] = spec
                out.append(array)
        else:
            out.append(a)
    return out, specs


def wanted(shape, dim):
    m = iota(shape, dim)
    g16 = (m >> 3) * 16
    b = m & 7
    before = (g16 - 2) & 127
    lent = before + (b >> 1)
    return (
        g16 + 2 * b,
        g16 + 2 * b + 1,
        jnp.where((b == 0) | (b == 2), lent, -1),
        jnp.where((b == 1) | (b == 3), lent, -1),
    )


def send_hots(rank_row, count=4):
    return hot(jnp.concatenate(wanted((NW, 1), 0)[:count], 0) == rank_row)


def return_hots(rank_col, count=4):
    return hot(rank_col == jnp.concatenate(wanted((1, NW), 1)[:count], 1))


def spread(col, lanes):
    hi, mid, lo = pieces(col)
    k = lanes & 7
    return jnp.where(k == 0, hi, jnp.where(k == 1, mid, jnp.where(k == 2, lo, 0.0)))


def pieces(col):
    hi = col.astype(BF16).astype(F32)
    rest = col - hi
    mid = rest.astype(BF16).astype(F32)
    return hi, mid, rest - mid


def either(lanes, even, odd):
    return jnp.where(lanes < 8, even, jnp.where(lanes < 16, odd, 0.0))


def slot_kinds(owner_ref, me):
    lane = iota((1, TILES), 1)
    ffn = jnp.where(lane >= TILES // LAYERS, lane - TILES // LAYERS, lane) >= 24
    return [
        jnp.max(
            jnp.where((owner_ref[...] == me * CAP + s) & ffn, 1, 0), axis=1, keepdims=True
        )
        for s in range(CAP)
    ]


def row_of_slots(kinds):
    r = iota((1, TR), 1)

    def place(low, x):
        j3 = (low >> 1) & 7
        device = (j3 & 3) * 8 + x * 2 + (low >> 4)
        return device * WIDE_PACK + (j3 >> 2) * 2 + (low & 1)

    attn = place(r & 31, r >> 5)
    ffn = place(r >> 2, r & 3)
    return jnp.concatenate([jnp.where(k == 1, ffn, attn) + 4 * s for s, k in enumerate(kinds)], 1)


def slot_of_row(kinds):
    r = iota((1, NW * PACK), 1)
    d, m = r >> 4, r & (PACK - 1)
    s, e = m >> 1, m & 1
    tau = (d >> 1) & 3
    low = (d & 1) * 16 + (d >> 3) * 2 + e
    out = jnp.full((1, NW * PACK), -1, I32)
    for i, k in enumerate(kinds):
        out = jnp.where(s == i, i * TR + jnp.where(k == 1, low * 4 + tau, tau * 32 + low), out)
    return out


def route_out_kernel(me_ref, owner_ref, master_ref, out_ref):
    tiles = master_ref[...].reshape(CAP * TR, PART).astype(BF16)
    place = row_of_slots(slot_kinds(owner_ref, me_ref[0]))
    rows = dot(hot(iota((PAIR_ROWS, 1), 0) == place), tiles, 1, 0).astype(BF16)
    out_ref[:PAIR_ROWS] = rows
    out_ref[PAIR_ROWS:] = rows


def route_out(me, owner_row, master):
    return call(
        route_out_kernel,
        (me, owner_row, master),
        [kept((2 * PAIR_ROWS, PART), BF16)],
        prefetch=1,
        in_place=(1,),
        name="route_out",
    )[0]


def pick_kernel(code_ref, moved_ref, first_ref, early_ref, late_ref):
    picked = hot(code_ref[...] == iota((1, 2 * PAIR_ROWS), 1))
    rows = dot(picked, moved_ref[...], 1, 0).astype(BF16)
    early_ref[...] = rows[:EARLY_ROWS]
    late_ref[...] = rows[EARLY_ROWS : EARLY_ROWS + 2 * FFN_ROWS]
    first = rows[EARLY_ROWS + 2 * FFN_ROWS :]
    first_ref[...] = jnp.broadcast_to(first[None], first_ref.shape)


def pick(code_col, moved):
    return call(
        pick_kernel,
        (code_col, moved),
        [
            kept((32, 32, PART), BF16),
            kept((EARLY_ROWS, PART), BF16),
            kept((2 * FFN_ROWS, PART), BF16),
        ],
        name="pick",
    )


def route_back_kernel(code_ref, *refs):
    first, last_rows, attn, ffn, gain_a, gain_b, gain_c, out_ref = refs
    at = FFN_ROWS - SPLIT
    rows = jnp.concatenate([first[...], last_rows[:at], attn[...], ffn[...], last_rows[at:]], 0)
    place = iota((NW * PACK, 1), 0)
    out = dot(hot(place == code_ref[...]), rows, 1, 0)
    gains = jnp.concatenate(
        [
            half
            for g in (gain_a, gain_b, gain_c)
            for half in (g[:, :PART], g[:, PART:])
        ]
        + [jnp.zeros((2, PART), F32)],
        0,
    ).astype(BF16)
    spare = hot((place & (PACK - 1)) - 2 * CAP == iota((1, 8), 1))
    out_ref[...] = (out + dot(spare, gains, 1, 0)).astype(BF16)


def route_back(code_row, parts, gains):
    return call(
        route_back_kernel,
        (code_row, *parts, *gains),
        [kept((NW * PACK, PART), BF16)],
        name="route_back",
    )[0]


def adam(grad, first, second, weights, rate):
    first_new = BETA_ONE * first + (1.0 - BETA_ONE) * grad
    second_new = BETA_TWO * second + (1.0 - BETA_TWO) * grad * grad
    step = (
        first_new
        / (1.0 - BETA_ONE**STEP)
        / (jnp.sqrt(second_new / (1.0 - BETA_TWO**STEP)) + EPSILON)
    )
    return first_new, second_new, weights - rate * (step + DECAY * weights)


def slots_kernel(
    half_ref, me_ref, owner_ref, moved_ref, ready_ref, m_ref, a_ref, b_ref, gains_ref, ga_ref, gb_ref,
    grad_out, first_out, second_out, new_out, gg_out, gf_out, gs_out, gn_out
):
    rows = moved_ref[...]
    placed = hot(iota((CAP * TR, 1), 0) == slot_of_row(slot_kinds(owner_ref, me_ref[0])))
    grads = dot(placed, rows, 1, 0)
    for s in range(CAP):
        for ref in (m_ref, a_ref, b_ref):
            ref.wait(1)
        grad = grads[s * TR : (s + 1) * TR]
        grad_out[s] = grad
        first_out[s], second_out[s], new_out[s] = adam(
            grad, a_ref.buffer[s], b_ref.buffer[s], m_ref.buffer[s], RATE_WEIGHT
        )
        for out in (grad_out, first_out, second_out, new_out):
            out.flush()
    spare = hot((iota((1, NW * PACK), 1) & (PACK - 1)) - 2 * CAP == iota((8, 1), 0))
    sums = dot(spare, rows, 1, 0)
    gains = [jnp.concatenate([sums[q : q + 1], sums[q + 1 : q + 2]], 1) for q in (4, 2, 0)]
    inner_sum = jnp.concatenate(gains + [ready_ref[...]], 0)
    back = hot(feature_of(iota((1, D), 1)) == iota((PART, 1), 0) + half_ref[0] * PART)
    parts = dot(jnp.concatenate(pieces(inner_sum), 0).astype(BF16), back, 1, 1)
    n = 2 * LAYERS
    total = parts[:n] + parts[n : 2 * n] + parts[2 * n :]
    for l in range(LAYERS):
        gain_grad = total[2 * l : 2 * l + 2]
        gg_out[l] = gain_grad
        gf_out[l], gs_out[l], gn_out[l] = adam(
            gain_grad, ga_ref[l], gb_ref[l], gains_ref[l], RATE_GAIN
        )


def slots_update(half, me, owner_row, moved, ready, master, first, second, gains, gain_first, gain_second):
    return run(
        slots_kernel,
        [
            half, me, owner_row, moved, ready,
            FarSlots(master), FarSlots(first), FarSlots(second),
            gains, gain_first, gain_second,
        ],
        [Sent((CAP, TR, PART), F32, CAP)] * 4 + [sds((LAYERS, 2, PART), F32)] * 4,
        prefetch=2,
        name="slots_update",
    )


def turned(col):
    same = iota((TOK, TOK), 0) == iota((TOK, TOK), 1)
    return jnp.sum(jnp.where(same, col, 0), axis=0, keepdims=True)


def plan_kernel(group_ref, mine_ref, source_ref, *outs):
    same = iota((TOK, TOK), 0) == iota((TOK, TOK), 1)
    b = iota((ROWS, 1), 0) & 7
    block = group_ref[0] * 8 + b
    before = (group_ref[0] * 8 - 1) & 63
    lanes = iota((TOK, TOK), 1)
    for l in range(LAYERS):
        rank_row, rank_col, place_row = outs[3 * l : 3 * l + 3]
        cols = jnp.zeros((TOK, TOK), I32)
        for r in range(ROUNDS):
            row = mine_ref[l * ROUNDS + r : l * ROUNDS + r + 1, :]
            col = jnp.sum(jnp.where(same, row, 0), axis=1, keepdims=True)
            rank_row[r : r + 1, :] = jnp.sum(jnp.where(col < row, 1, 0), axis=0, keepdims=True)
            rank = jnp.sum(jnp.where(row < col, 1, 0), axis=1, keepdims=True)
            cols = jnp.where(lanes == r, rank, cols)
        rank_col[...] = cols
        source = source_ref[l]
        target = jnp.broadcast_to(source[:, None, :], (NW, 8, TOK)).reshape(ROWS, TOK)
        place = target & (TOK - 1)
        got = []
        for want in (block, before):
            inside = (target >> 7) == want
            got.append(jnp.min(jnp.where(inside, place, TOK), axis=1, keepdims=True))
            got.append(jnp.max(jnp.where(inside, place, -1), axis=1, keepdims=True))
        low, high, low_lent, high_lent = got
        columns = (
            low + TOK * b,
            high + TOK * b,
            jnp.where(b == 0, low_lent - SPAN, jnp.where(b == 2, high_lent - SPAN, -1)),
            jnp.where(b == 1, low_lent - SPAN, jnp.where(b == 3, high_lent - SPAN, -1)),
        )
        for j, column in enumerate(columns):
            for q in range(4):
                at = slice(q * TOK, (q + 1) * TOK)
                place_row[j : j + 1, at] = turned(column[at])


def plan(group, mine, source):
    layer = [kept((ROUNDS, TOK), I32), kept((TOK, TOK), I32), kept((4, ROWS), I32)]
    return call(plan_kernel, (group, mine, source), layer * LAYERS, prefetch=1, name="plan")


def inner_kernel(half_ref, *refs):
    count = len(refs) // 3
    n = half_ref[0]
    feature = feature_of(iota((1, D), 1))
    mine = hot(feature == iota((PART, 1), 0) + n * PART)
    theirs = hot(feature == iota((PART, 1), 0) + (1 - n) * PART)
    for i in range(count):
        own, other, out = refs[2 * i], refs[2 * i + 1], refs[2 * count + i]
        if own.dtype == BF16:
            out[...] = dot(own[...], mine, 1, 0) + dot(other[...], theirs, 1, 0)
        else:
            total = jnp.zeros(out.shape, F32)
            for a, b in zip(pieces(own[...]), pieces(other[...])):
                total = total + (dot(a.astype(BF16), mine, 1, 0) + dot(b.astype(BF16), theirs, 1, 0))
            out[...] = total


def inner(half, pairs, name):
    flat = [a for pair in pairs for a in pair]
    outs = [sds((own.shape[0], D), F32) for own, _ in pairs]
    return call(inner_kernel, (half, *flat), outs, prefetch=1, name=name)


def outer_kernel(count, half_ref, *refs):
    n = half_ref[0]
    feature = feature_of(iota((1, D), 1))
    back = hot(feature == iota((PART, 1), 0) + n * PART)
    for i in range(count):
        total = jnp.zeros(refs[count + i].shape, F32)
        for part in pieces(refs[i][...]):
            total = total + dot(part.astype(BF16), back, 1, 1)
        refs[count + i][...] = total


def outer(half, arrays, name):
    outs = [sds((a.shape[0], PART), F32) for a in arrays]
    return call(
        functools.partial(outer_kernel, len(arrays)), (half, *arrays), outs, prefetch=1, name=name
    )


def project_kernel(pending, count, core_ref, *refs):
    if pending:
        x_ref, own_ref, other_ref, *rest = refs
        x = x_ref[...] + (own_ref[...].astype(F32) + other_ref[...].astype(F32))
    else:
        x_ref, *rest = refs
        x = x_ref[...]
    gain_ref, *rest = rest
    q_refs, v_refs = rest[:count], rest[count : 2 * count]
    rank_ref, x_out, hn_out, send_out = rest[2 * count :]
    core = core_ref[0]
    x_out[...] = x
    xhat, _ = norm_parts(x)
    hn = xhat * gain_ref[...]
    hn_out[0] = hn[:, :PART].astype(BF16)
    hn_out[1] = hn[:, PART:].astype(BF16)
    q = into(core, hn, q_refs).astype(BF16)
    v = into(core, hn, v_refs).astype(BF16)
    qv = jnp.concatenate([m[:, h * DH : (h + 1) * DH] for h in range(HN) for m in (q, v)], 1)
    for r in range(ROUNDS):
        moved = dot(send_hots(rank_ref[r : r + 1, :]), qv, 1, 0)
        even, odd = moved[:NW].astype(BF16), moved[NW : 2 * NW].astype(BF16)
        lent_q, lent_v = moved[2 * NW : 3 * NW], moved[3 * NW :]
        for h in range(HN):
            rows = slice((r * HN + h) * NW, (r * HN + h + 1) * NW)
            at = h * 2 * DH
            send_out[rows, : 2 * DH] = even[:, at : at + 2 * DH]
            send_out[rows, 2 * DH : 4 * DH] = odd[:, at : at + 2 * DH]
            send_out[rows, 4 * DH :] = (
                lent_q[:, at : at + DH] + lent_v[:, at + DH : at + 2 * DH]
            ).astype(BF16)


def project(core, x, pending, gain, wq, wv, rank_row):
    args, specs = unpacked([core, x, *(pending or ()), gain, wq, wv, rank_row], 1)
    return call(
        functools.partial(project_kernel, pending is not None, len(wq.parts())),
        args,
        [kept((TOK, D), F32), kept((2, TOK, PART), BF16), kept((ROWS, QV_LANES), BF16)],
        specs=specs,
        in_place=(0, *((1,) if pending else ()), *(tuple(specs) if len(wq.parts()) == 4 else ())),
        prefetch=1,
        name="project",
    )


def scores_of(rows):
    keys = rows[:, :DH].astype(F32)
    inv = lax.rsqrt(jnp.sum(keys * keys, axis=-1, keepdims=True) + 1e-06)
    unit = (keys * inv).astype(BF16)
    scores = jnp.concatenate(
        [
            dot(
                rows[(c + 1) * SPAN : (c + 2) * SPAN, :DH],
                unit[c * SPAN : (c + 2) * SPAN],
                1,
                1,
            )
            for c in range(16)
        ],
        0,
    )
    own = iota((1024, TOK), 1) == (iota((1024, TOK), 0) & (SPAN - 1)) + SPAN
    scores = jnp.where(own, MASK_FILL, scores)
    peak = jnp.max(scores, axis=-1, keepdims=True)
    total = peak + jnp.log(jnp.sum(jnp.exp(scores - peak), axis=-1, keepdims=True))
    exact = jnp.exp(scores - total)
    return keys, inv, unit, own, total, exact


def arrive(place_row_ref, j, rows):
    count = 1024 if j < 2 else SPAN
    return dot(hot(iota((count, 1), 0) == place_row_ref[j : j + 1, :]), rows, 1, 0)


def leave(place_row_ref, j, rows):
    at = hot(iota((rows.shape[0], 1), 0) == place_row_ref[j : j + 1, :])
    return dot(at, rows, 0, 0)


def attend_kernel(moved_ref, place_row_ref, sorted_out, send_out):
    q_lent = arrive(place_row_ref, 2, moved_ref[:, 4 * DH :])
    v_lent = arrive(place_row_ref, 3, moved_ref[:, 4 * DH :])
    main = arrive(place_row_ref, 0, moved_ref[:, : 2 * DH]) + arrive(
        place_row_ref, 1, moved_ref[:, 2 * DH : 4 * DH]
    )
    rows = jnp.concatenate([jnp.concatenate([q_lent, v_lent], 1), main], 0).astype(BF16)
    sorted_out[...] = rows
    _, _, _, _, total, exact = scores_of(rows)
    probs = exact.astype(BF16)
    outs = jnp.concatenate(
        [
            dot(probs[c * SPAN : (c + 1) * SPAN], rows[c * SPAN : (c + 2) * SPAN, DH:], 1, 0)
            for c in range(16)
        ],
        0,
    )
    aux = spread(total, iota((1024, TOK), 1))
    both = jnp.concatenate([outs, aux], 1).astype(BF16)
    even = leave(place_row_ref, 0, both)
    odd = leave(place_row_ref, 1, both)
    send_out[:, :DH] = even[:, :DH].astype(BF16)
    send_out[:, DH : 2 * DH] = odd[:, :DH].astype(BF16)
    lanes = iota((ROWS, TOK), 1)
    send_out[:, 2 * DH :] = either(lanes, even[:, DH:], odd[:, DH:]).astype(BF16)


def attend(moved, place_row):
    return call(
        attend_kernel,
        (moved, place_row),
        [kept((1088, 2 * DH), BF16), kept((ROWS, O_LANES), BF16)],
        in_place=(1,),
        name="attend",
    )


def by_head(ref, r, cols):
    return jnp.concatenate(
        [ref[(r * HN + h) * NW : (r * HN + h + 1) * NW, cols] for h in range(HN)], 1
    )


def merge_kernel(count, core_ref, moved_ref, rank_col_ref, *refs):
    w_refs, refs = refs[:count], refs[count:]
    send_out, o_out, share_out, merged_out = refs
    lanes = iota((TOK, TOK), 1)
    outs, logs = [], []
    for r in range(ROUNDS):
        hots = return_hots(rank_col_ref[:, r : r + 1], 2)
        aux = by_head(moved_ref, r, slice(2 * DH, 3 * DH))
        even = dot(
            hots[:, :NW], jnp.concatenate([by_head(moved_ref, r, slice(0, DH)), aux], 1), 1, 0
        )
        odd = dot(
            hots[:, NW:], jnp.concatenate([by_head(moved_ref, r, slice(DH, 2 * DH)), aux], 1), 1, 0
        )
        outs.append(even[:, :PART] + odd[:, :PART])
        o_out[r] = outs[r].astype(BF16)
        logs.append(
            [
                jnp.sum(
                    either(
                        lanes,
                        even[:, PART + h * DH : PART + (h + 1) * DH],
                        odd[:, PART + h * DH : PART + (h + 1) * DH],
                    ),
                    axis=-1,
                    keepdims=True,
                )
                for h in range(HN)
            ]
        )
    merged = []
    share_all = jnp.zeros((TOK, TOK), F32)
    for h in range(HN):
        top = jnp.maximum(logs[0][h], logs[1][h])
        e0 = jnp.exp(logs[0][h] - top)
        e1 = jnp.exp(logs[1][h] - top)
        total = e0 + e1
        cols = slice(h * DH, (h + 1) * DH)
        s0, s1 = e0 / total, e1 / total
        merged.append(s0 * outs[0][:, cols] + s1 * outs[1][:, cols])
        share_all = jnp.where(lanes == h, s0, jnp.where(lanes == HN + h, s1, share_all))
    share_out[...] = share_all
    merged = jnp.concatenate(merged, 1).astype(BF16)
    merged_out[...] = merged
    put_halves(out_of(core_ref[0], merged, w_refs), send_out)


def put_halves(pair, send_out):
    for i in range(2):
        send_out[:, i * PART : (i + 1) * PART] = pair[i].astype(BF16)


def merge(core, moved, rank_col, wo):
    args, specs = unpacked([core, moved, rank_col, wo], 1)
    return call(
        functools.partial(merge_kernel, len(wo.parts())),
        args,
        [
            kept((TOK, D), BF16),
            kept((ROUNDS, TOK, PART), BF16),
            kept((TOK, TOK), F32),
            kept((TOK, PART), BF16),
        ],
        specs=specs,
        in_place=(1, *specs),
        prefetch=1,
        name="merge",
    )


def gelu_parts(pre):
    half = 0.5 * (1.0 + lax.erf(pre * (0.5**0.5)))
    slope = half + pre * (jnp.exp(-0.5 * pre * pre) * np.float32(1.0 / np.sqrt(2.0 * np.pi)))
    return (pre * half).astype(BF16), slope.astype(BF16)


def add_up(total, more):
    return more if total is None else [a + b for a, b in zip(total, more)]


def ffn_forward(x_ref, own_ref, other_ref, gain_ref, w_ref, y_out, hf_out, act_out, slope_out):
    y = x_ref[...] + (own_ref[...].astype(F32) + other_ref[...].astype(F32))
    y_out[...] = y
    y_out.flush()
    xhat, _ = norm_parts(y)
    hf = (xhat * gain_ref[...]).astype(BF16)
    hf_out[0], hf_out[1] = hf[:, :PART], hf[:, PART:]
    total = None
    for c in range(QUAD):
        w_ref.wait(4)
        pre = dot(hf[:, :PART], w_ref.block(UP, c, 0), 1, 0) + dot(
            hf[:, PART:], w_ref.block(UP, c, 1), 1, 0
        )
        act, slope = gelu_parts(pre)
        act_out[:, c * PART : (c + 1) * PART] = act
        slope_out[:, c * PART : (c + 1) * PART] = slope
        total = add_up(total, [dot(act, w_ref.block(DOWN, c, c0), 1, 1) for c0 in range(2)])
    return total


def ffn_kernel(
    x_ref, own_ref, other_ref, gain_ref, w_ref, y_out, hf_out, act_out, slope_out, send_out
):
    put_halves(
        ffn_forward(
            x_ref, own_ref, other_ref, gain_ref, w_ref, y_out, hf_out, act_out, slope_out
        ),
        send_out,
    )


def ffn(x, own, other, gain, w):
    return run(
        ffn_kernel,
        [Far(x), Far(own), other, Far(gain), FfnWeight(w)],
        [
            Sent((TOK, D), F32),
            Sent((2, TOK, PART), BF16),
            Sent((TOK, QUAD * PART), BF16),
            Sent((TOK, QUAD * PART), BF16),
            Sent((TOK, D), BF16),
        ],
        name="ffn",
    )


def put_pieces(out_ref, at, row, rows, grad):
    for piece in range(32):
        z, tau, y = piece >> 3, (piece >> 1) & 3, piece & 1
        got = grad[piece * 16 : (piece + 1) * 16]
        if rows == 16:
            out_ref[2 * tau + at, z * 2 + y, row : row + 16] = got
        else:
            out_ref[at, z * 2 + y, row + tau * 16 : row + (tau + 1) * 16] = got


def ffn_backward(back, waits, w_ref, hf_ref, act_ref, slope_ref, send_out, grad_out):
    total = None
    for c in range(QUAD):
        if waits:
            w_ref.wait(4)
        cols = slice(c * PART, (c + 1) * PART)
        d_act = dot(back[0], w_ref.block(DOWN, c, 0), 1, 0) + dot(
            back[1], w_ref.block(DOWN, c, 1), 1, 0
        )
        d_pre = (d_act * slope_ref[:, cols].astype(F32)).astype(BF16)
        total = add_up(total, [dot(d_pre, w_ref.block(UP, c, c0), 1, 1) for c0 in range(2)])
        act = act_ref[:, cols]
        for c0 in range(2):
            put_pieces(grad_out, 2 * c + c0, 0, 64, dot(hf_ref[c0], d_pre, 0, 0).astype(BF16))
            put_pieces(grad_out, 2 * c + c0, 64, 64, dot(back[c0], act, 0, 0).astype(BF16))
        grad_out.flush()
    put_halves(total, send_out)


def turn_kernel(
    x_ref, own_ref, other_ref, gain_ref, g_ref, w_ref,
    y_out, forth_out, send_out, grad_out, hf_ref, act_ref, slope_ref
):
    put_halves(
        ffn_forward(
            x_ref, own_ref, other_ref, gain_ref, w_ref, y_out, hf_ref, act_ref, slope_ref
        ),
        forth_out,
    )
    forth_out.flush()
    back = g_ref[...].astype(BF16)
    back = [back[:, :PART], back[:, PART:]]
    ffn_backward(back, False, w_ref, hf_ref, act_ref, slope_ref, send_out, grad_out)


def turn(x, own, other, gain, g, w):
    return run(
        turn_kernel,
        [Far(x), Far(own), other, Far(gain), Far(g), FfnWeight(w)],
        [
            Sent((TOK, D), F32),
            Sent((TOK, D), BF16),
            Sent((TOK, D), BF16),
            Sent((2 * QUAD, 8, FFN_ROWS, PART), BF16, QUAD),
        ],
        temps=[
            pltpu.VMEM((2, TOK, PART), BF16),
            pltpu.VMEM((TOK, QUAD * PART), BF16),
            pltpu.VMEM((TOK, QUAD * PART), BF16),
        ],
        name="turn",
        vmem=BIG_VMEM_BYTES,
    )


def ffn_back_kernel(
    g_ref, own_ref, other_ref, x_ref, gain_ref, hf_ref, act_ref, slope_ref, w_ref, unused_ref,
    g_out, send_out, grad_out, dgain_out
):
    xhat, rstd = norm_parts(x_ref[...])
    add, dgain = norm_back(
        own_ref[...].astype(F32) + other_ref[...].astype(F32), gain_ref[...], xhat, rstd
    )
    dgain_out[...] = dgain
    g = g_ref[...] + add
    g_out[...] = g
    g_out.flush()
    back = g.astype(BF16)
    back = [back[:, :PART], back[:, PART:]]
    ffn_backward(back, True, w_ref, hf_ref, act_ref, slope_ref, send_out, grad_out)


def ffn_back(g, own, other, x, gain, more, hf, act, slope, w):
    return run(
        ffn_back_kernel,
        [
            Far(g), Far(own), other, Far(x), Far(gain),
            Far(hf), Far(act), Far(slope), FfnWeight(w), Direct(more),
        ],
        [
            Sent((TOK, D), F32),
            Sent((TOK, D), BF16),
            Sent((2 * QUAD, 8, FFN_ROWS + ATTN_ROWS, PART), BF16, QUAD),
            sds((1, D), F32),
        ],
        partial={2: (2 * QUAD, 8, FFN_ROWS, PART)},
        aliases={9: 2},
        name="ffn_back",
        vmem=BIG_VMEM_BYTES,
    )


def merge_back_kernel(count, core_ref, g_ref, own_ref, other_ref, y_ref, gain_ref, *refs):
    w_refs, refs = refs[:count], refs[count:]
    o_ref, share_ref, rank_row_ref, g_out, back_out, send_out, dgain_out = refs
    xhat, rstd = norm_parts(y_ref[...])
    add, dgain = norm_back(own_ref[...].astype(F32) + other_ref[...].astype(F32), gain_ref[...], xhat, rstd)
    dgain_out[...] = dgain
    g = g_ref[...] + add
    g_out[...] = g
    back_out[0] = g[:, :PART].astype(BF16)
    back_out[1] = g[:, PART:].astype(BF16)
    dout = into(core_ref[0], g, w_refs)
    share = share_ref[...]
    o0 = o_ref[0].astype(F32)
    o1 = o_ref[1].astype(F32)
    lanes = iota((TOK, TOK), 1)
    parts = [[], []]
    logs = [[], []]
    for h in range(HN):
        cols = slice(h * DH, (h + 1) * DH)
        s0 = share[:, h : h + 1]
        s1 = share[:, HN + h : HN + h + 1]
        dh = dout[:, cols]
        t0 = jnp.sum(dh * o0[:, cols], axis=-1, keepdims=True)
        t1 = jnp.sum(dh * o1[:, cols], axis=-1, keepdims=True)
        mean = s0 * t0 + s1 * t1
        parts[0].append(s0 * dh)
        parts[1].append(s1 * dh)
        logs[0].append(spread(s0 * (t0 - mean), lanes))
        logs[1].append(spread(s1 * (t1 - mean), lanes))
    lanes = iota((NW, TOK), 1)
    for r in range(ROUNDS):
        moved = dot(
            send_hots(rank_row_ref[r : r + 1, :], 2),
            jnp.concatenate(parts[r] + logs[r], 1).astype(BF16),
            1,
            0,
        )
        even, odd = moved[:NW], moved[NW:]
        for h in range(HN):
            rows = slice((r * HN + h) * NW, (r * HN + h + 1) * NW)
            cols = slice(h * DH, (h + 1) * DH)
            aux = slice(PART + h * DH, PART + (h + 1) * DH)
            send_out[rows, :DH] = even[:, cols].astype(BF16)
            send_out[rows, DH : 2 * DH] = odd[:, cols].astype(BF16)
            send_out[rows, 2 * DH :] = either(lanes, even[:, aux], odd[:, aux]).astype(BF16)


def merge_back(core, g, own, other, y, gain, wo, o, share, rank_row):
    args, specs = unpacked([core, g, own, other, y, gain, wo, o, share, rank_row], 1)
    return call(
        functools.partial(merge_back_kernel, len(wo.parts())),
        args,
        [
            kept((TOK, D), F32),
            kept((2, TOK, PART), BF16),
            kept((ROWS, O_LANES), BF16),
            sds((1, D), F32),
        ],
        specs=specs,
        in_place=(0, 1, 3, *specs, *range(len(args) - 4, len(args) - 1)),
        prefetch=1,
        name="merge_back",
    )


def attend_back_kernel(moved_ref, sorted_ref, place_row_ref, gain_ref, send_out):
    lanes = iota((ROWS, TOK), 1)
    aux = moved_ref[:, 2 * DH :].astype(F32)
    got = jnp.zeros((1024, 2 * DH), F32)
    for j in range(2):
        here = jnp.where(lanes >> 3 == j, aux, 0.0).astype(BF16)
        pair = jnp.concatenate([moved_ref[:, j * DH : (j + 1) * DH], here], 1)
        got = got + arrive(place_row_ref, j, pair)
    d_out = got[:, :DH].astype(BF16)
    d_log = jnp.sum(got[:, DH:], axis=-1, keepdims=True)
    rows = sorted_ref[...]
    keys, inv, unit, own, _, exact = scores_of(rows)
    probs = exact.astype(BF16)
    g_probs = jnp.concatenate(
        [
            dot(d_out[c * SPAN : (c + 1) * SPAN], rows[c * SPAN : (c + 2) * SPAN, DH:], 1, 1)
            for c in range(16)
        ],
        0,
    )
    inner_sum = jnp.sum(g_probs * exact, axis=-1, keepdims=True)
    g_scores = exact * (g_probs - inner_sum + d_log)
    g_scores = jnp.where(own, 0.0, g_scores).astype(BF16)
    d_query, d_unit, d_value = [], [], []
    for c in range(16):
        here = slice(c * SPAN, (c + 1) * SPAN)
        both = slice(c * SPAN, (c + 2) * SPAN)
        after = slice((c + 1) * SPAN, (c + 2) * SPAN)
        d_query.append(dot(g_scores[here], unit[both], 1, 0))
        d_unit.append(dot(g_scores[here], rows[after, :DH], 0, 0))
        d_value.append(dot(probs[here], d_out[here], 0, 0))

    def overlap(parts):
        out = [parts[0][:SPAN]]
        for c in range(15):
            out.append(parts[c][SPAN:] + parts[c + 1][:SPAN])
        out.append(parts[15][SPAN:])
        return jnp.concatenate(out, 0)

    g_unit = overlap(d_unit)
    along = jnp.sum(g_unit * keys, axis=-1, keepdims=True)
    g_keys = inv * g_unit - keys * (inv * inv * inv) * along
    g_query = jnp.concatenate([jnp.zeros((SPAN, DH), F32)] + d_query, 0) + g_keys
    grads = jnp.concatenate([g_query, overlap(d_value)], 1).astype(BF16)
    for j in range(2):
        cols = slice(j * 2 * DH, (j + 1) * 2 * DH)
        send_out[:, cols] = leave(place_row_ref, j, grads[SPAN:]).astype(BF16)
    lent = leave(place_row_ref, 2, grads[:SPAN, :DH]) + leave(place_row_ref, 3, grads[:SPAN, DH:])
    b = iota((ROWS, 1), 0) & 7
    for q in range(4):
        lent = jnp.where(b == 4 + q, gain_ref[:, q * DH : (q + 1) * DH], lent)
    send_out[:, 4 * DH :] = lent.astype(BF16)


def attend_back(moved, rows, place_row, gain):
    return call(
        attend_back_kernel,
        (moved, rows, place_row, gain),
        [kept((ROWS, QV_LANES), BF16)],
        in_place=(1, 2),
        name="attend_back",
    )[0]


def project_back_kernel(count, core_ref, moved_ref, rank_col_ref, *refs):
    q_refs, v_refs = refs[:count], refs[count : 2 * count]
    send_out, grad_out, gain_out = refs[2 * count :]
    gain_out[...] = dot(
        hot(iota((8, 1), 0) == (iota((1, ROWS), 1) & 7)), moved_ref[:, 4 * DH :], 1, 0
    )
    total = jnp.zeros((TOK, HN * 2 * DH), F32)
    lent_q = jnp.zeros((TOK, PART), F32)
    lent_v = jnp.zeros((TOK, PART), F32)
    for r in range(ROUNDS):
        hots = return_hots(rank_col_ref[:, r : r + 1])
        total = total + dot(hots[:, :NW], by_head(moved_ref, r, slice(0, 2 * DH)), 1, 0)
        total = total + dot(hots[:, NW : 2 * NW], by_head(moved_ref, r, slice(2 * DH, 4 * DH)), 1, 0)
        lent = by_head(moved_ref, r, slice(4 * DH, 5 * DH))
        lent_q = lent_q + dot(hots[:, 2 * NW : 3 * NW], lent, 1, 0)
        lent_v = lent_v + dot(hots[:, 3 * NW :], lent, 1, 0)
    d_q = jnp.concatenate([total[:, h * 2 * DH : h * 2 * DH + DH] for h in range(HN)], 1)
    d_v = jnp.concatenate([total[:, h * 2 * DH + DH : (h + 1) * 2 * DH] for h in range(HN)], 1)
    d_q = (d_q + lent_q).astype(BF16)
    d_v = (d_v + lent_v).astype(BF16)
    grad_out[0] = d_q
    grad_out[1] = d_v
    core = core_ref[0]
    from_q = out_of(core, d_q, q_refs)
    from_v = out_of(core, d_v, v_refs)
    put_halves([a + b for a, b in zip(from_q, from_v)], send_out)


def project_back(core, moved, rank_col, wq, wv):
    args, specs = unpacked([core, moved, rank_col, wq, wv], 1)
    return call(
        functools.partial(project_back_kernel, len(wq.parts())),
        args,
        [kept((TOK, D), BF16), kept((2, TOK, PART), BF16), sds((8, DH), F32)],
        specs=specs,
        in_place=range(1, len(args) - 1),
        prefetch=1,
        name="project_back",
    )


def attn_part_kernel(back_ref, merged_ref, hn_ref, dqv_ref, grad_out, buffer, sems):
    for c0 in range(2):
        for i, (left, right) in enumerate(
            ((back_ref, merged_ref[...]), (hn_ref, dqv_ref[0]), (hn_ref, dqv_ref[1]))
        ):
            put_pieces(buffer, c0, i * 16, 16, dot(left[c0], right, 0, 0).astype(BF16))
    copy = pltpu.make_async_copy(
        buffer, grad_out.at[:, :, pl.ds(FFN_ROWS, ATTN_ROWS), :], sems.at[0]
    )
    copy.start()
    copy.wait()


def attn_part_of(back, merged, hn, dqv):
    return call(
        attn_part_kernel,
        (back, merged, hn, dqv),
        [kept((2 * QUAD, 8, FFN_ROWS + ATTN_ROWS, PART), BF16)],
        out_specs={0: pl.BlockSpec(memory_space=pl.ANY)},
        scratch=[pltpu.VMEM((2 * QUAD, 8, ATTN_ROWS, PART), BF16), pltpu.SemaphoreType.DMA((1,))],
        in_place=range(4),
        name="attn_part",
    )[0]


def last_kernel(g_ref, own_ref, other_ref, x_ref, gain_ref, g_out, dgain_out):
    xhat, rstd = norm_parts(x_ref[...])
    add, dgain = norm_back(own_ref[...].astype(F32) + other_ref[...].astype(F32), gain_ref[...], xhat, rstd)
    g_out[...] = g_ref[...] + add
    dgain_out[...] = dgain


def last(g, own, other, x, gain):
    return call(
        last_kernel,
        (g, own, other, x, gain),
        [kept((TOK, D), F32), sds((1, D), F32)],
        in_place=(0, 1, 3),
        name="last",
    )


def pair_dot(left_a, left_b, right_a, right_b):
    left = jnp.concatenate([left_a, left_b], 0)
    right = jnp.concatenate([right_a, right_b], 0)
    return dot(left, right, 0, 0).astype(BF16)


def attn_grad_kernel(row, core_ref, la, lb, ra, rb, *refs):
    out_ref, buffer, sems = refs[-3:]
    for i in range(buffer.shape[1] // 16):
        got = pair_dot(la[0], lb[0], ra[i], rb[i])
        buffer[:, i * 16 : (i + 1) * 16] = got.reshape(32, 16, PART)
    rows = pl.ds(row, buffer.shape[1])
    copy = pltpu.make_async_copy(buffer, out_ref.at[:, rows, :], sems.at[0])
    copy.start()
    copy.wait()


def attn_grad(core, left, right, before=None):
    half = pl.BlockSpec((1, TOK, PART), lambda i, core: (core[0], 0, 0))
    args, specs, row, aliases = [*left, *right], {0: half, 1: half}, 0, {}
    if before is not None:
        args.append(before)
        specs[4] = pl.BlockSpec(memory_space=pl.ANY)
        row, aliases = 16, {5: 0}
    rows = 16 * right[0].shape[0]
    return call(
        functools.partial(attn_grad_kernel, row),
        (core, *args),
        [kept((32, ATTN_ROWS, PART), BF16)],
        specs=specs,
        out_specs={0: pl.BlockSpec(memory_space=pl.ANY)},
        scratch=[pltpu.VMEM((32, rows, PART), BF16), pltpu.SemaphoreType.DMA((1,))],
        prefetch=1,
        in_place=(0, 2, 4),
        name="attn_grad",
        aliases=aliases,
    )[0]


def swap_narrow(values):
    return lax.ppermute(values, "narrow", [(0, 1), (1, 0)])


def with_core(values):
    other = lax.ppermute(values, "wide", [(i, i ^ 1) for i in range(NW)])
    return values, other


def to_all(values):
    return lax.all_to_all(values, "wide", split_axis=0, concat_axis=0, tiled=True)


SAME_CORE = [
    [y * 32 + z * 8 + x * 2 + c for z in range(4) for x in range(4) for y in range(2)]
    for c in range(2)
]
LAYER_OF_Y = [[y * 32 + i for i in range(NW // 2)] for y in range(2)]


def summed(values):
    return jnp.sum(to_same_core(values).astype(F32), axis=0).astype(BF16)


ALONG_X_AND_CORE = [[hi * 8 + i for i in range(8)] for hi in range(8)]
ALONG_Z_AND_Y = [
    [y * 32 + z * 8 + i for z in range(4) for y in range(2)] for i in range(8)
]
ALONG_Z = [
    [y * 32 + z * 8 + x * 2 + c for z in range(4)] for y in range(2) for x in range(4) for c in range(2)
]


def summed_along_x(values):
    return lax.psum_scatter(
        values, "wide", scatter_dimension=0, tiled=True, axis_index_groups=ALONG_X_AND_CORE
    ).reshape(values.shape[1:])


def summed_across_x(values):
    moved = lax.all_to_all(
        values, "wide", split_axis=0, concat_axis=0, tiled=True, axis_index_groups=ALONG_Z_AND_Y
    )
    return jnp.sum(moved.astype(F32), axis=0).astype(BF16)


def summed_along_z(values):
    return lax.psum_scatter(
        values, "wide", scatter_dimension=0, tiled=True, axis_index_groups=ALONG_Z
    )


def summed_along_y(values):
    y = lax.axis_index("wide") >> 5
    mine = lax.dynamic_index_in_dim(values, y, keepdims=False)
    theirs = lax.dynamic_index_in_dim(values, 1 - y, keepdims=False)
    got = lax.ppermute(theirs, "wide", [(i, i ^ 32) for i in range(NW)])
    return (mine.astype(F32) + got.astype(F32)).astype(BF16)


def to_same_core(values):
    return lax.all_to_all(
        values, "wide", split_axis=0, concat_axis=0, tiled=True, axis_index_groups=SAME_CORE
    )


def after(values, *others):
    return lax.optimization_barrier((values, others))[0]


def gathered(rows):
    got = lax.all_gather(rows, "wide", axis=0, tiled=True, axis_index_groups=LAYER_OF_Y)
    return got.reshape(QUAD, QUAD, 2, rows.shape[0], PART)


def moved_rows(rows):
    return to_all(rows.reshape(NW, rows.shape[0] // NW, -1)).reshape(rows.shape)


def on_device(
    x_first,
    x_second,
    grad_first,
    grad_second,
    sort_target,
    owner,
    master,
    moment_first,
    moment_second,
    gains,
    gain_first,
    gain_second,
):
    me = lax.axis_index("wide").astype(I32)
    half = lax.axis_index("narrow").astype(I32).reshape(1)
    core = (me & 1).reshape(1)
    owner_row = owner.reshape(1, TILES)

    routed = route_out(me.reshape(1), owner_row, master)
    sort_target, held = after((sort_target, owner), routed)
    moved = moved_rows(routed)
    chunks = []
    for l in range(LAYERS):
        of = held[l * 88 : (l + 1) * 88]
        chunks += [of[at : at + 32].reshape(8, 4).T.reshape(4, 8) for at in (24, 56)]
        chunks += [of[16:24].reshape(1, 8), of[:16].reshape(2, 8)]
    holder = jnp.repeat(jnp.concatenate(chunks), 2, axis=1)
    e = np.arange(16, dtype=np.int32)[None] & 1
    code_row = ((holder // CAP) * PACK + (holder % CAP) * 2 + e).reshape(1, -1)
    there = (holder // CAP) * WIDE_PACK + (holder % CAP) * 4 + e
    both = jnp.stack([there, there + 2], 1)
    mine_only = there + 2 * (me >> 5)
    code_col = jnp.concatenate(
        [
            both[:9].reshape(-1),
            both[19:].reshape(-1),
            both[11:19].reshape(-1),
            mine_only[9:11].reshape(-1),
        ]
    ).reshape(-1, 1)
    mine = lax.dynamic_slice_in_dim(sort_target, me * TOK, TOK, axis=2).reshape(-1, TOK)
    by_source = lax.dynamic_index_in_dim(sort_target, me >> 5, 1, keepdims=False)
    plans = plan((me & 7).reshape(1), mine, by_source.reshape(LAYERS, NW, TOK))
    rank_rows, rank_cols, place_rows = [plans[i::3] for i in range(3)]
    flat_gains = gains.reshape(LAYERS * 2, PART)
    moved = after(moved, code_col, code_row, plans)
    first_rows, early_rows, late_rows = pick(code_col, moved)
    streams = (x_second, flat_gains, x_first, grad_first, grad_second)
    pairs = [(a, swap_narrow(a)) for a in after(streams, moved)]
    x_two, gain_rows = inner(half, pairs[:2], "inner_a")
    pairs = pairs[2:]
    first_w = with_core(after(to_same_core(first_rows), x_two, gain_rows, pairs))
    early = gathered(early_rows)
    late = gathered(late_rows)
    x_one, g_one, g_two = inner(half, pairs, "inner_b")
    w_ffn = [early, late]
    w_attn = [
        [Weight(8, early), Weight(0, *first_w), Weight(1, *first_w)],
        [Weight(9, early), Weight(10, early), Weight(11, early)],
    ]
    gain = [[Gain(gain_rows, 2 * l + i) for i in range(2)] for l in range(LAYERS)]

    saved = []
    pending = None
    for l in range(LAYERS):
        w_out, w_qk, w_value = w_attn[l]
        x_two, hn, send = project(core, x_two, pending, gain[l][0], w_qk, w_value, rank_rows[l])
        moved = moved_rows(send)
        if l == 0:
            moved = after(moved, x_one, g_one, g_two)
        rows, send = attend(moved, place_rows[l])
        moved = moved_rows(send)
        send, o, share, merged = merge(core, moved, rank_cols[l], w_out)
        stream = (x_one, send, swap_narrow(send), gain[l][1])
        if l < LAYERS - 1:
            x_one, *for_ffn, send_f = ffn(*stream, w_ffn[l])
        else:
            x_one, send_f, send, ffn_part = turn(*stream, g_two, w_ffn[l])
        pending = (send_f, swap_narrow(send_f))
        saved.append((x_two, x_one, hn, rows, o, share, merged))
    y_two = x_two + (pending[0].astype(F32) + pending[1].astype(F32))
    y_first, y_second = outer(half, (x_one, y_two), "outer_y")

    pending = None
    dgains = [[None, None], [None, None]]
    gain_sums = []
    for l in reversed(range(LAYERS)):
        x_in, y_mid, hn, rows, o, share, merged = saved[l]
        w_out, w_qk, w_value = w_attn[l]
        if l < LAYERS - 1:
            g_two, send, ffn_part, dgains[l + 1][0] = ffn_back(
                g_two, *pending, *for_ffn, w_ffn[l]
            )
        other = swap_narrow(send)
        ffn_part = summed_along_x(ffn_part)
        if l == 0:
            other = after(other, ffn_rows)
            ffn_rows = summed_along_y(ffn_rows)
        g_one, back, send, dgains[l][1] = merge_back(
            core, g_one, send, other, y_mid, gain[l][1], w_out, o, share, rank_rows[l]
        )
        moved = moved_rows(send)
        if l > 0:
            moved = after(moved, y_first, y_second)
            half_gain = dgains[1][1][:, :PART]
        else:
            dx_first = outer(half, (g_one,), "outer_dx_first")[0]
            moved = after(moved, dx_first, ffn_rows)
            half_gain = dgains[1][1][:, PART:]
        send = attend_back(moved, rows, place_rows[l], half_gain)
        moved = moved_rows(send)
        if l > 0:
            moved = after(moved, ffn_part)
        if l == 0:
            out_part = attn_grad(core, with_core(back), with_core(merged.reshape(1, TOK, PART)))
            moved = after(moved, out_part)
        send, dqv, gain_sum = project_back(core, moved, rank_cols[l], w_qk, w_value)
        other = swap_narrow(send)
        if l > 0:
            attn_part = attn_part_of(back, merged, hn, dqv)
            other = after(other, attn_part)
            ffn_rows = summed_along_z(after(ffn_part, moved))
        else:
            attn_part = attn_grad(core, with_core(hn), with_core(dqv), out_part)
            attn_rows = summed(attn_part)
            ffn_part = after(ffn_part, attn_part)
            last_rows = summed_along_y(summed_along_z(ffn_part[:, SPLIT:]))
            both_rows = summed_across_x(after(ffn_part[:, :SPLIT], other))
        gain_sums.append(gain_sum[4:].reshape(1, PART))
        pending = (send, other, x_in, gain[l][0], attn_part)
    g_two, dgains[0][0] = last(g_two, *pending[:4])
    dx_second = outer(half, (g_two,), "outer_dx_second")[0]
    parts = (both_rows, last_rows, attn_rows, ffn_rows)
    back_rows = moved_rows(
        route_back(code_row, parts, (dgains[1][0], dgains[0][1], dgains[0][0]))
    )
    back_rows = after(back_rows, dx_second)
    slot_grad, slot_first, slot_second, slot_new, *gain_news = slots_update(
        half,
        me.reshape(1),
        owner_row,
        back_rows,
        jnp.concatenate(gain_sums, 1),
        master,
        moment_first,
        moment_second,
        gains,
        gain_first,
        gain_second,
    )
    gain_grad, gain_first_new, gain_second_new, gain_new = gain_news
    return (
        y_first,
        y_second,
        dx_first,
        dx_second,
        slot_grad,
        slot_first,
        slot_second,
        slot_new,
        gain_grad,
        gain_first_new,
        gain_second_new,
        gain_new,
    )


def solution(mesh):
    rows = P("wide", "narrow")
    tiles = P("wide", None, "narrow")
    gains = P(None, None, "narrow")
    return jax.shard_map(
        on_device,
        mesh=mesh,
        in_specs=(rows,) * 4 + (P(), P()) + (tiles,) * 3 + (gains,) * 3,
        out_specs=(rows,) * 4 + (tiles,) * 4 + (gains,) * 4,
        check_vma=False,
    )
```
